32 devices in a mesh: dp: 8 (over z, x), chan: 4 (over y, core).
Axes of the slice: x: 2, y: 2, z: 4, core: 2. Of those that a mesh axis runs over, the one named last changes fastest.
Arguments:
- features_in: float32 [64, 14, 14, 1024], P('dp', None, None, 'chan')
- image_counts: int32 [8], replicated, may hold values from 4 to 8, as said below
- reduce_weight: float32 [1024, 256], P('chan'), may hold values from -0.1875 to 0.1875
- reduce_gain: float32 [256], P('chan'), may hold values from 0.5 to 1.5
- reduce_shift: float32 [256], P('chan'), may hold values from -3 to 3
- split_weight: float32 [3, 3, 128, 2, 256], P(None, None, None, None, 'chan'), may hold values from -0.1875 to 0.1875
- split_gain: float32 [2, 256], P(None, 'chan'), may hold values from 0.5 to 1.5
- split_shift: float32 [2, 256], P(None, 'chan'), may hold values from -3 to 3
- squeeze_weight: float32 [256, 128], P('chan'), may hold values from -0.375 to 0.375
- squeeze_gain: float32 [128], replicated, may hold values from 0.5 to 1.5
- squeeze_shift: float32 [128], replicated, may hold values from -3 to 3
- attend_weight: float32 [128, 2, 256], P(None, None, 'chan'), may hold values from -0.5 to 0.5
- attend_bias: float32 [2, 256], P(None, 'chan'), may hold values from -3 to 3
- expand_weight: float32 [256, 1024], P(None, 'chan'), may hold values from -0.375 to 0.375
- expand_gain: float32 [1024], P('chan'), may hold values from 0.5 to 1.5
- expand_shift: float32 [1024], P('chan'), may hold values from -3 to 3
- grad_out: float32 [64, 14, 14, 1024], P('dp', None, None, 'chan'), may hold values from -6 to 6
Outputs:
- block_out: float32 [64, 14, 14, 1024], P('dp', None, None, 'chan')
- grad_input: float32 [64, 14, 14, 1024], P('dp', None, None, 'chan')
- grad_reduce_weight: float32 [1024, 256], P('chan')
- grad_reduce_gain: float32 [256], P('chan')
- grad_reduce_shift: float32 [256], P('chan')
- grad_split_weight: float32 [3, 3, 128, 2, 256], P(None, None, None, None, 'chan')
- grad_split_gain: float32 [2, 256], P(None, 'chan')
- grad_split_shift: float32 [2, 256], P(None, 'chan')
- grad_squeeze_weight: float32 [256, 128], P('chan')
- grad_squeeze_gain: float32 [128], replicated
- grad_squeeze_shift: float32 [128], replicated
- grad_attend_weight: float32 [128, 2, 256], P(None, None, 'chan')
- grad_attend_bias: float32 [2, 256], P(None, 'chan')
- grad_expand_weight: float32 [256, 1024], P(None, 'chan')
- grad_expand_gain: float32 [1024], P('chan')
- grad_expand_shift: float32 [1024], P('chan')
The draws below stay inside these ranges and needn't reach their ends.
Inputs may be any that keep to these rules, and one draw needn't show every extreme that they name: image_counts[k] valid images fill the first slots of dp index k; in every draw some index holds 8 valid images and some other exactly 4.
All inputs are finite; a program needn't handle non-finite values.
Results may differ from the reference program's by a relative error of at most 0.012.
Values sent between devices are 32-bit elements; how exact they have to be, the bound alone decides.
No kernel may reach another device: no remote copies, remote signals or barrier semaphores. Data moves between devices by JAX's collectives and lax.ppermute only.
A program may use at most 64 MiB of HBM per device.

```python
import jax
import jax.numpy as jnp
from jax import lax

C_IN = 1024
MID = 256
INNER = 128
SIDE = 14
IMG_DEV = 8
SHARDS = 8
IMAGES = 64


def draw_features_in(key, part):
    shape = (IMAGES, SIDE, SIDE, C_IN)
    position = jnp.arange(IMAGES, dtype=jnp.float32) / max(IMAGES - 1, 1)
    values = jax.random.normal(key, shape, jnp.float32)
    scaling = 0.6 + 1.2 * position
    return values * scaling[:, None, None, None]


def draw_image_counts(key, part):
    draw_key = jax.random.fold_in(key, 11)
    rank_key = jax.random.fold_in(key, 23)
    counts = jax.random.randint(draw_key, (SHARDS,), IMG_DEV // 2, IMG_DEV + 1)
    ranking = jax.random.permutation(rank_key, SHARDS)
    counts = counts.at[ranking[0]].set(IMG_DEV)
    counts = counts.at[ranking[1]].set(IMG_DEV // 2)
    return counts.astype(jnp.int32)


def levels(stream_key, dims, shards, least, top_value):
    gain = 1.0
    for dim, parts in shards:
        draws = jax.random.uniform(jax.random.fold_in(jax.random.fold_in(stream_key, 6), dim), (parts,), jnp.float32, least / len(shards), top_value / len(shards))
        gain = gain * jnp.repeat(jnp.exp(draws), dims[dim] // parts).reshape((-1,) + (1,) * (len(dims) - 1 - dim))
    return gain


def noise(rng, dims, deviation, reach, shards=(), held_as=jnp.bfloat16):
    result = jax.random.normal(rng, dims, jnp.float32) * deviation
    if len(shards) > 0:
        result = levels(rng, dims, shards, -0.22, 0.18) * result
    return jnp.clip(result, min=-reach, max=reach).astype(held_as)


def setup_inputs(seed: int = 0) -> dict:
    key_of = jax.random.split(jax.random.key(seed), 18)
    features_in = draw_features_in(jax.random.fold_in(key_of[17], 71), 0)
    image_counts = draw_image_counts(jax.random.fold_in(key_of[17], 71), 0)
    reduce_weight = noise(key_of[2], (C_IN, MID), C_IN ** -0.5, 0.1875, ((0, 4),), jnp.float32)
    reduce_gain = jnp.clip(1.0 + 0.1 * jax.random.normal(key_of[3], (MID,), jnp.float32), 0.5, 1.5)
    reduce_shift = noise(key_of[4], (MID,), 0.3, 3.0, ((0, 4),), jnp.float32)
    split_weight = noise(key_of[5], (3, 3, MID // 2, 2, MID), (9 * MID // 2) ** -0.5, 0.1875, ((4, 4),), jnp.float32)
    split_gain = jnp.clip(1.0 + 0.1 * jax.random.normal(key_of[6], (2, MID), jnp.float32), 0.5, 1.5)
    split_shift = noise(key_of[7], (2, MID), 0.3, 3.0, ((1, 4),), jnp.float32)
    squeeze_weight = noise(key_of[8], (MID, INNER), MID ** -0.5, 0.375, ((0, 4),), jnp.float32)
    squeeze_gain = jnp.clip(1.0 + 0.1 * jax.random.normal(key_of[9], (INNER,), jnp.float32), 0.5, 1.5)
    squeeze_shift = noise(key_of[10], (INNER,), 0.3, 3.0, (), jnp.float32)
    attend_weight = noise(key_of[11], (INNER, 2, MID), INNER ** -0.5, 0.5, ((2, 4),), jnp.float32)
    attend_bias = noise(key_of[12], (2, MID), 0.5, 3.0, ((1, 4),), jnp.float32)
    expand_weight = noise(key_of[13], (MID, C_IN), MID ** -0.5, 0.375, ((1, 4),), jnp.float32)
    expand_gain = jnp.clip(1.0 + 0.1 * jax.random.normal(key_of[14], (C_IN,), jnp.float32), 0.5, 1.5)
    expand_shift = noise(key_of[15], (C_IN,), 0.3, 3.0, ((0, 4),), jnp.float32)
    grad_out = noise(key_of[16], (IMAGES, SIDE, SIDE, C_IN), 1.0, 6.0, ((0, 8), (3, 4)), jnp.float32)
    return {"features_in": features_in, "image_counts": image_counts, "reduce_weight": reduce_weight, "reduce_gain": reduce_gain, "reduce_shift": reduce_shift, "split_weight": split_weight, "split_gain": split_gain, "split_shift": split_shift, "squeeze_weight": squeeze_weight, "squeeze_gain": squeeze_gain, "squeeze_shift": squeeze_shift, "attend_weight": attend_weight, "attend_bias": attend_bias, "expand_weight": expand_weight, "expand_gain": expand_gain, "expand_shift": expand_shift, "grad_out": grad_out}


EPSILON = 1e-05
HIGHEST = lax.Precision.HIGHEST

def normalize(values, weights, count_all, gains, shifts, leading):
    summed_axes = tuple(range(leading))
    average = lax.optimization_barrier(jnp.sum(values * weights, axis=summed_axes)) / count_all
    squares = lax.optimization_barrier(jnp.sum(weights * values * values, axis=summed_axes)) / count_all
    spread = squares - average * average
    return (values - average) * lax.rsqrt(spread + EPSILON) * gains + shifts

def forward(features_in, reduce_weight, reduce_gain, reduce_shift, split_weight, split_gain, split_shift, squeeze_weight, squeeze_gain, squeeze_shift, attend_weight, attend_bias, expand_weight, expand_gain, expand_shift, pixel_mask, image_mask, pixel_total, image_total):
    slot_count = features_in.shape[0]
    reduced = jnp.einsum('bhwc,cd->bhwd', features_in, reduce_weight, precision=HIGHEST)
    relu_one = jax.nn.relu(normalize(reduced, pixel_mask, pixel_total, reduce_gain, reduce_shift, 3))
    kernel = split_weight.reshape(3, 3, MID // 2, 2 * MID)
    split_out = lax.conv_general_dilated(relu_one, kernel, (1, 1), 'SAME', dimension_numbers=('NHWC', 'HWIO', 'NHWC'), feature_group_count=2, precision=HIGHEST)
    split_out = split_out.reshape(slot_count, SIDE, SIDE, 2, MID)
    relu_two = jax.nn.relu(normalize(split_out, pixel_mask[..., None], pixel_total, split_gain, split_shift, 3))
    pooled = lax.optimization_barrier(jnp.mean(lax.optimization_barrier(jnp.sum(relu_two, axis=3)), axis=(1, 2)))
    squeeze = jnp.dot(pooled, squeeze_weight, precision=HIGHEST)
    hidden = jax.nn.relu(normalize(squeeze, image_mask, image_total, squeeze_gain, squeeze_shift, 1))
    logits = jnp.einsum('bc,crk->brk', hidden, attend_weight, precision=HIGHEST) + attend_bias
    weights = jax.nn.softmax(logits, axis=1)
    attended = lax.optimization_barrier(jnp.sum(weights[:, None, None] * relu_two, axis=3))
    expanded = jnp.einsum('bhwc,cd->bhwd', attended, expand_weight, precision=HIGHEST)
    normed = normalize(expanded, pixel_mask, pixel_total, expand_gain, expand_shift, 3)
    return jax.nn.relu(normed + features_in) * pixel_mask

def reference(features_in, image_counts, reduce_weight, reduce_gain, reduce_shift, split_weight, split_gain, split_shift, squeeze_weight, squeeze_gain, squeeze_shift, attend_weight, attend_bias, expand_weight, expand_gain, expand_shift, grad_out):
    slot_index = jnp.arange(features_in.shape[0], dtype=jnp.int32)
    owned_count = image_counts[slot_index // IMG_DEV]
    image_mask = (slot_index % IMG_DEV < owned_count).astype(jnp.float32)[:, None]
    pixel_mask = image_mask[:, :, None, None]
    image_total = jnp.sum(image_counts).astype(jnp.float32)
    pixel_total = image_total * (SIDE * SIDE)

    def whole_block(inputs, w_reduce, g_reduce, s_reduce, w_split, g_split, s_split, w_squeeze, g_squeeze, s_squeeze, w_attend, b_attend, w_expand, g_expand, s_expand):
        return forward(inputs, w_reduce, g_reduce, s_reduce, w_split, g_split, s_split, w_squeeze, g_squeeze, s_squeeze, w_attend, b_attend, w_expand, g_expand, s_expand, pixel_mask, image_mask, pixel_total, image_total)
    block_out, pullback = jax.vjp(whole_block, features_in, reduce_weight, reduce_gain, reduce_shift, split_weight, split_gain, split_shift, squeeze_weight, squeeze_gain, squeeze_shift, attend_weight, attend_bias, expand_weight, expand_gain, expand_shift)
    grad_input, grad_reduce_weight, grad_reduce_gain, grad_reduce_shift, grad_split_weight, grad_split_gain, grad_split_shift, grad_squeeze_weight, grad_squeeze_gain, grad_squeeze_shift, grad_attend_weight, grad_attend_bias, grad_expand_weight, grad_expand_gain, grad_expand_shift = pullback(grad_out)
    return (block_out, grad_input, grad_reduce_weight, grad_reduce_gain, grad_reduce_shift, grad_split_weight, grad_split_gain, grad_split_shift, grad_squeeze_weight, grad_squeeze_gain, grad_squeeze_shift, grad_attend_weight, grad_attend_bias, grad_expand_weight, grad_expand_gain, grad_expand_shift)
```

```python
import jax
import jax.numpy as jnp
from jax import lax
from jax.sharding import PartitionSpec as P

EPSILON = 1e-05
FINE = lax.Precision.HIGH
COARSE = lax.Precision.HIGH


def dot(a, b, precision=FINE):
    return jnp.dot(a, b, precision=precision, preferred_element_type=jnp.float32)


def bits_of(n):
    out, k = [], 1
    while k < n:
        out.append(k)
        k *= 2
    return out


def split_conv(inputs, kernel):
    return lax.conv_general_dilated(
        inputs,
        kernel,
        (1, 1),
        "SAME",
        dimension_numbers=("NHWC", "HWIO", "NHWC"),
        feature_group_count=2,
        precision=FINE,
    )


def build(mesh):
    nd, nc = mesh.shape["dp"], mesh.shape["chan"]
    both = ("dp", "chan")
    cbits, dbits = bits_of(nc), bits_of(nd)

    def swap(x, axis, k):
        n = {"dp": nd, "chan": nc}.get(axis, nd * nc) if isinstance(axis, str) else nd * nc
        return lax.ppermute(x, axis, [(i, i ^ k) for i in range(n)])

    all_bits = [1] + [k | 1 for k in bits_of(nd * nc)[1:]]

    def sum_all(x):
        for k in all_bits:
            x = x + swap(x, both, k)
        return x

    def gather_all(x):
        for k in all_bits[::-1]:
            x = jnp.concatenate([x, swap(x, both, k)], axis=0)
        return x

    def order_all():
        me = lax.axis_index("dp") * nc + lax.axis_index("chan")
        rel = [0]
        for k in all_bits[::-1]:
            rel = rel + [r ^ k for r in rel]
        return jnp.bitwise_xor(me, jnp.array(rel, jnp.int32))

    def sum_dp(x):
        for k in dbits:
            x = x + swap(x, "dp", k)
        return x

    def pick(x, i):
        return lax.dynamic_index_in_dim(x, i, 0, False)

    def scatter_chan(x):
        me = lax.axis_index("chan")
        for k in cbits:
            b = (me // k) % 2
            h = x.reshape((2, x.shape[0] // 2) + x.shape[1:])
            x = pick(h, b) + swap(pick(h, 1 - b), "chan", k)
        return x[0]

    def gather_rows(x):
        me = lax.axis_index("chan")
        x = x[None]
        for k in cbits[::-1]:
            b = (me // k) % 2
            o = swap(x, "chan", k)
            x = jnp.where(b == 0, jnp.concatenate([x, o]), jnp.concatenate([o, x]))
        return x

    def gather_chan(x):
        me = lax.axis_index("chan")
        x = x[None]
        for k in cbits:
            b = (me // k) % 2
            o = swap(x, "chan", k)
            x = jnp.where(b == 0, jnp.concatenate([x, o]), jnp.concatenate([o, x]))
        return x

    def big_sum_dp(x):
        d = lax.axis_index("dp")
        h = x.reshape((nd, x.shape[0] // nd) + x.shape[1:])
        acc = pick(h, d)
        for k in range(1, nd):
            acc = acc + swap(pick(h, d ^ k), "dp", k)
        o = jnp.zeros_like(h)
        for k in range(nd):
            part = acc if k == 0 else swap(acc, "dp", k)
            o = lax.dynamic_update_index_in_dim(o, part, d ^ k, 0)
        return o.reshape(x.shape)

    def quarter_of(chan):
        q = chan * 0
        for k in cbits:
            q = q * 2 + (chan // k) % 2
        return q

    def per_device(
        features_in,
        image_counts,
        reduce_weight,
        reduce_gain,
        reduce_shift,
        split_weight,
        split_gain,
        split_shift,
        squeeze_weight,
        squeeze_gain,
        squeeze_shift,
        attend_weight,
        attend_bias,
        expand_weight,
        expand_gain,
        expand_shift,
        grad_out,
    ):
        slots, edge = features_in.shape[0], features_in.shape[1]
        area = edge * edge
        rows = slots * area
        win = features_in.shape[3]
        mid = reduce_weight.shape[1]
        lw = split_weight.shape[4]
        inner = squeeze_gain.shape[0]
        own = slots // nc
        orows = own * area
        d, c = lax.axis_index("dp"), lax.axis_index("chan")
        q = quarter_of(c)
        owned = lax.dynamic_index_in_dim(image_counts, d, 0, False)
        row_mask = jnp.repeat((jnp.arange(slots) < owned).astype(jnp.float32), area)[:, None]
        omask_img = ((q * own + jnp.arange(own)) < owned).astype(jnp.float32)[:, None]
        omask = jnp.repeat(omask_img, area, axis=0)
        ids = order_all()
        slot_ids = quarter_of(ids % nc)[:, None] * own + jnp.arange(own)[None]
        amask = (slot_ids < image_counts[ids // nc][:, None]).astype(jnp.float32).reshape(-1, 1)
        images = jnp.sum(image_counts).astype(jnp.float32)
        pixels = images * area

        X = features_in.reshape(rows, win)
        red = scatter_chan(dot(X, reduce_weight).reshape(nc, orows, mid))
        small = gather_chan(
            jnp.concatenate(
                [reduce_gain, reduce_shift, split_gain.reshape(-1), split_shift.reshape(-1), attend_bias.reshape(-1)]
            )
        )
        wid = reduce_gain.shape[0]
        g1 = small[:, :wid].reshape(-1)
        b1 = small[:, wid : 2 * wid].reshape(-1)

        def radixed(z):
            return z.reshape(nc, 2, lw).transpose(1, 0, 2).reshape(2, nc * lw)

        off = 2 * wid
        g2 = radixed(small[:, off : off + 2 * lw]).reshape(-1)
        b2 = radixed(small[:, off + 2 * lw : off + 4 * lw]).reshape(-1)
        ab = radixed(small[:, off + 4 * lw :])
        g3 = gather_chan(expand_gain)
        wsp, red_ = lax.optimization_barrier((split_weight, red))
        wsp = gather_chan(wsp)
        kernel = wsp.transpose(1, 2, 3, 4, 0, 5).reshape(3, 3, split_weight.shape[2], 2 * mid)
        wex = gather_chan(expand_weight)
        wsq = gather_chan(squeeze_weight).reshape(mid, inner)
        wat = gather_chan(attend_weight).transpose(1, 2, 0, 3).reshape(inner, 2 * mid)

        s1 = sum_all(jnp.stack([jnp.sum(red * omask, 0), jnp.sum(red * red * omask, 0)]))
        avg1 = s1[0] / pixels
        inv1 = lax.rsqrt(s1[1] / pixels - avg1 * avg1 + EPSILON)
        act1 = (red - avg1) * inv1 * g1 + b1
        relu1 = jax.nn.relu(act1)
        conv_out, conv_back = jax.vjp(split_conv, relu1.reshape(own, edge, edge, mid), kernel)
        spl = conv_out.reshape(orows, 2 * mid)
        red_all = gather_rows(red)

        s2 = sum_all(jnp.stack([jnp.sum(spl * omask, 0), jnp.sum(spl * spl * omask, 0)]))
        avg2 = s2[0] / pixels
        inv2 = lax.rsqrt(s2[1] / pixels - avg2 * avg2 + EPSILON)
        norm2 = (spl - avg2) * inv2
        act2 = norm2 * g2 + b2
        on2 = (act2 > 0).astype(jnp.float32)
        relu2 = act2 * on2

        def per_image(z):
            return jnp.sum(z.reshape(own, area, -1), axis=1)

        c12 = jnp.concatenate([per_image(on2), per_image(on2 * norm2)], axis=1)
        pooled2 = per_image(relu2)
        pooled = (pooled2[:, :mid] + pooled2[:, mid:]) / area
        sq_all = gather_all(dot(pooled, wsq))
        c12_all = gather_all(c12)
        pooled_all = gather_all(pooled)
        sqs = jnp.sum(sq_all * amask, 0)
        sqq = jnp.sum(sq_all * sq_all * amask, 0)
        avgf = sqs / images
        invf = lax.rsqrt(sqq / images - avgf * avgf + EPSILON)
        normf = (sq_all - avgf) * invf
        actf = normf * squeeze_gain + squeeze_shift
        hidden = jax.nn.relu(actf)
        logits = (dot(hidden[:own], wat)).reshape(own, 2, mid) + ab
        wts = jax.nn.softmax(logits, axis=1)
        wrow = jnp.repeat(wts.reshape(own, 2 * mid), area, axis=0)
        mixed = wrow * relu2
        att = mixed[:, :mid] + mixed[:, mid:]

        att_all = gather_rows(att).reshape(rows, mid)
        ex_own = jnp.stack([dot(att, wex[i]) for i in range(nc)])
        s3 = sum_all(jnp.stack([jnp.sum(ex_own * omask, 1), jnp.sum(ex_own * ex_own * omask, 1)]))
        avg3 = s3[0] / pixels
        inv3 = lax.rsqrt(s3[1] / pixels - avg3 * avg3 + EPSILON)
        norm3_own = (ex_own - avg3[:, None]) * inv3[:, None]
        avg3l, inv3l = pick(avg3, c), pick(inv3, c)
        norm3 = (dot(att_all, expand_weight) - avg3l) * inv3l
        pre = norm3 * expand_gain + expand_shift + X
        block_out = (jax.nn.relu(pre) * row_mask).reshape(features_in.shape)
        grad_pre = grad_out.reshape(rows, win) * row_mask * (pre > 0).astype(jnp.float32)
        scale3 = expand_gain * inv3l
        ga_part = dot(grad_pre * scale3, expand_weight.T, COARSE)
        sg3 = sum_dp(jnp.stack([jnp.sum(grad_pre, 0), jnp.sum(grad_pre * norm3, 0)]))
        sg3_all = gather_chan(sg3)
        ga = scatter_chan(ga_part.reshape(nc, orows, mid))
        scale3_all = g3 * inv3 / pixels
        mean_term = (sg3_all[:, 0][:, None] + norm3_own * sg3_all[:, 1][:, None]) * scale3_all[:, None] * omask
        for i in range(nc):
            ga = ga - dot(mean_term[i], wex[i].T, COARSE)
        grad_expanded = scale3 * (grad_pre - row_mask * (sg3[0] + norm3 * sg3[1]) / pixels)
        grad_expand_weight = big_sum_dp(dot(att_all.T, grad_expanded, COARSE))

        ga2 = jnp.concatenate([ga, ga], axis=1) * on2
        a1, a2 = per_image(ga2), per_image(ga2 * norm2)
        grad_wts = (g2 * a2 + b2 * a1).reshape(own, 2, mid)
        grad_logits = wts * (grad_wts - jnp.sum(wts * grad_wts, axis=1, keepdims=True))
        wflat = wts.reshape(own, 2 * mid)
        part = jnp.stack([jnp.sum(wflat * a1, 0), jnp.sum(wflat * a2, 0)])
        part = sum_all(part)
        gl_all = gather_all(grad_logits.reshape(own, 2 * mid))
        grad_hidden = dot(gl_all, wat.T, COARSE)
        dzf = grad_hidden * (actf > 0).astype(jnp.float32) * amask
        grad_squeeze_shift = jnp.sum(dzf, 0)
        grad_squeeze_gain = jnp.sum(dzf * normf, 0)
        grad_squeeze = (
            squeeze_gain
            * invf
            * (dzf - amask * (grad_squeeze_shift + normf * grad_squeeze_gain) / images)
        )
        gp_all = dot(grad_squeeze, wsq.T, COARSE) / area
        gp2 = jnp.concatenate([gp_all, gp_all], axis=1)
        shift2 = part[0] + jnp.sum(gp2 * c12_all[:, : 2 * mid], 0)
        gain2 = part[1] + jnp.sum(gp2 * c12_all[:, 2 * mid :], 0)
        grad_squeeze_weight = dot(
            lax.dynamic_slice_in_dim(pooled_all, c * lw, lw, 1).T, grad_squeeze, COARSE
        )
        glc = lax.dynamic_slice_in_dim(gl_all.reshape(-1, 2, mid), c * lw, lw, 2)
        grad_attend_bias = jnp.sum(glc, 0)
        grad_attend_weight = dot((hidden * amask).T, glc.reshape(-1, 2 * lw), COARSE).reshape(inner, 2, lw)

        gprow = jnp.repeat(gp2[:own], area, axis=0)
        dz2 = wrow * ga2 + gprow * on2
        grad_split = g2 * inv2 * (dz2 - omask * (shift2 + norm2 * gain2) / pixels)
        grad_grid, _ = conv_back(grad_split.reshape(own, edge, edge, 2 * mid))
        dz1 = grad_grid.reshape(orows, mid) * (act1 > 0).astype(jnp.float32)
        norm1_own = (red - avg1) * inv1
        sg1 = sum_all(jnp.stack([jnp.sum(dz1 * omask, 0), jnp.sum(dz1 * norm1_own * omask, 0)]))
        dz1_all = gather_rows(dz1).reshape(rows, mid)
        norm1 = (red_all.reshape(rows, mid) - avg1) * inv1
        grad_reduced = g1 * inv1 * (dz1_all - row_mask * (sg1[0] + norm1 * sg1[1]) / pixels)
        grad_reduce_weight = big_sum_dp(dot(X.T, grad_reduced, COARSE))
        grad_input = (grad_pre + dot(grad_reduced, reduce_weight.T, COARSE)).reshape(features_in.shape)

        gs = grad_split.reshape(orows, 2, nc, lw)
        mine, red_rel = [], []
        for k in range(nc):
            blk = lax.dynamic_index_in_dim(gs, c ^ k, 2, False).reshape(orows, 2 * lw)
            mine.append(blk if k == 0 else swap(blk, "chan", k))
            red_rel.append(pick(red_all, quarter_of(c ^ k)))
        gs_all = jnp.concatenate(mine).reshape(slots, edge, edge, 2 * lw)
        relu1_all = jax.nn.relu((jnp.concatenate(red_rel) - avg1) * inv1 * g1 + b1)
        relu1_all = relu1_all.reshape(slots, edge, edge, mid)
        kern0 = jnp.zeros((3, 3, split_weight.shape[2], 2 * lw), jnp.float32)
        _, kback = jax.vjp(lambda k: split_conv(relu1_all, k), kern0)
        (dws,) = kback(gs_all)
        dws = big_sum_dp(dws.reshape(-1, 2 * lw)).reshape(split_weight.shape)

        def own_part(z):
            return lax.dynamic_slice_in_dim(z, c * wid, wid)

        def own_radix(z):
            return lax.dynamic_slice_in_dim(z.reshape(2, mid), c * lw, lw, 1)

        return (
            block_out,
            grad_input,
            grad_reduce_weight,
            own_part(sg1[1]),
            own_part(sg1[0]),
            dws,
            own_radix(gain2),
            own_radix(shift2),
            grad_squeeze_weight,
            grad_squeeze_gain,
            grad_squeeze_shift,
            grad_attend_weight,
            grad_attend_bias,
            grad_expand_weight,
            sg3[1],
            sg3[0],
        )

    return per_device


def solution(mesh):
    in_specs = (
        P("dp", None, None, "chan"),
        P(),
        P("chan", None),
        P("chan"),
        P("chan"),
        P(None, None, None, None, "chan"),
        P(None, "chan"),
        P(None, "chan"),
        P("chan", None),
        P(),
        P(),
        P(None, None, "chan"),
        P(None, "chan"),
        P(None, "chan"),
        P("chan"),
        P("chan"),
        P("dp", None, None, "chan"),
    )
    out_specs = (
        P("dp", None, None, "chan"),
        P("dp", None, None, "chan"),
        P("chan", None),
        P("chan"),
        P("chan"),
        P(None, None, None, None, "chan"),
        P(None, "chan"),
        P(None, "chan"),
        P("chan", None),
        P(),
        P(),
        P(None, None, "chan"),
        P(None, "chan"),
        P(None, "chan"),
        P("chan"),
        P("chan"),
    )
    return jax.shard_map(
        build(mesh), mesh=mesh, in_specs=in_specs, out_specs=out_specs, check_vma=False
    )
```

```python
import functools

import jax
import jax.numpy as jnp
from jax import lax
from jax.experimental import pallas as pl
from jax.experimental.pallas import tpu as pltpu
from jax.sharding import PartitionSpec as P

EPSILON = 1e-05
F32, BF16 = jnp.float32, jnp.bfloat16
PAD = 16
VMEM_LIMIT = 44 * 1024 * 1024


def bits_of(n):
    out, k = [], 1
    while k < n:
        out.append(k)
        k *= 2
    return out


def split2(x):
    hi = x.astype(BF16)
    return hi, (x - hi.astype(F32)).astype(BF16)


def mm(a, b, dims=((1,), (0,))):
    return lax.dot_general(a, b, (dims, ((), ())), preferred_element_type=F32)


def mm3(ah, al, bh, bl):
    return mm(ah, bh) + (mm(ah, bl) + mm(al, bh))


def exact(a, b, dims=((1,), (0,))):
    return lax.dot_general(
        a, b, (dims, ((), ())), precision=lax.Precision.HIGHEST, preferred_element_type=F32
    )


def call(body, ins, outs, scratch=(), scalars=None, specs=None, flops=0):
    out_shape = [jax.ShapeDtypeStruct(s, d) for s, d in outs]
    whole = lambda n: lambda *_: (0,) * n
    in_specs = []
    for k, a in enumerate(ins):
        s = None if specs is None else specs.get(k)
        in_specs.append(s or pl.BlockSpec(a.shape, whole(a.ndim)))
    moved = sum(a.size * a.dtype.itemsize for a in ins) + sum(
        int(jnp.dtype(d).itemsize) * functools.reduce(lambda x, y: x * y, s, 1) for s, d in outs
    )
    return pl.pallas_call(
        body,
        out_shape=out_shape,
        grid_spec=pltpu.PrefetchScalarGridSpec(
            num_scalar_prefetch=1,
            grid=(1,),
            in_specs=in_specs,
            out_specs=[pl.BlockSpec(s, whole(len(s))) for s, _ in outs],
            scratch_shapes=list(scratch),
        ),
        compiler_params=pltpu.CompilerParams(vmem_limit_bytes=VMEM_LIMIT),
        cost_estimate=pl.CostEstimate(flops=flops, bytes_accessed=moved, transcendentals=0),
    )(scalars, *ins)


def mask_of(nv, rows, cols, edge):
    r = lax.broadcasted_iota(jnp.int32, (rows, cols), 0)
    return ((r & (PAD - 1)) < edge) & (r < nv * (edge * PAD))


def padded(ref, scr, mask):
    n, e, _, w = ref.shape
    scr[:, :e, :] = ref[...].reshape(n * e, e, w)
    return jnp.where(mask, scr[...].reshape(n * e * PAD, w), 0.0)


def colsum(x):
    return jnp.sum(x, axis=0, keepdims=True)


def build(mesh):
    nd, nc = mesh.shape["dp"], mesh.shape["chan"]
    both = ("dp", "chan")
    cbits, dbits = bits_of(nc), bits_of(nd)
    all_bits = [1] + [k | 1 for k in bits_of(nd * nc)[1:]]
    sum_order = [all_bits[0]] + all_bits[:0:-1]

    def swap(x, axis, k):
        n = {"dp": nd, "chan": nc}[axis] if isinstance(axis, str) else nd * nc
        return lax.ppermute(x, axis, [(i, i ^ k) for i in range(n)])

    def sum_all(x):
        for k in sum_order:
            x = x + swap(x, both, k)
        return x

    def gather_all(x):
        for k in all_bits[::-1]:
            x = jnp.concatenate([x, swap(x, both, k)], axis=0)
        return x

    def order_all():
        me = lax.axis_index("dp") * nc + lax.axis_index("chan")
        rel = [0]
        for k in all_bits[::-1]:
            rel = rel + [r ^ k for r in rel]
        return jnp.bitwise_xor(me, jnp.array(rel, jnp.int32))

    def pick(x, i):
        return lax.dynamic_index_in_dim(x, i, 0, False)

    def big_sum_dp(x):
        d = lax.axis_index("dp")
        h = x.reshape((nd, x.shape[0] // nd) + x.shape[1:])
        if nd <= 8:
            acc = pick(h, d)
            for k in range(1, nd):
                acc = acc + swap(pick(h, d ^ k), "dp", k)
            parts = [acc] + [swap(acc, "dp", k) for k in range(1, nd)]
            o = jnp.zeros_like(h)
            for k in range(nd):
                o = lax.dynamic_update_index_in_dim(o, parts[k], d ^ k, 0)
            return o.reshape(x.shape)
        cur = h
        for k in dbits:
            b = (d // k) % 2
            g = cur.reshape((2, cur.shape[0] // 2) + cur.shape[1:])
            cur = pick(g, b) + swap(pick(g, 1 - b), "dp", k)
        for k in dbits[::-1]:
            b = (d // k) % 2
            o = swap(cur, "dp", k)
            cur = jnp.where(b == 0, jnp.concatenate([cur, o]), jnp.concatenate([o, cur]))
        return cur.reshape(x.shape)

    def quarter_of(chan):
        q = chan * 0
        for k in cbits:
            q = q * 2 + (chan // k) % 2
        return q

    def per_device(
        features_in,
        image_counts,
        reduce_weight,
        reduce_gain,
        reduce_shift,
        split_weight,
        split_gain,
        split_shift,
        squeeze_weight,
        squeeze_gain,
        squeeze_shift,
        attend_weight,
        attend_bias,
        expand_weight,
        expand_gain,
        expand_shift,
        grad_out,
    ):
        slots, edge = features_in.shape[0], features_in.shape[1]
        area = edge * edge
        win = features_in.shape[3]
        mid = reduce_weight.shape[1]
        half = mid // 2
        lw = split_weight.shape[4]
        inner = squeeze_gain.shape[0]
        own = slots // nc
        span = edge * PAD
        R = own * span
        ni = nd * slots
        d, c = lax.axis_index("dp"), lax.axis_index("chan")
        q = quarter_of(c)
        owned = lax.dynamic_index_in_dim(image_counts, d, 0, False)
        nv = [jnp.clip(owned - (q ^ r) * own, 0, own) for r in range(nc)]
        isc = jnp.stack([c, q] + nv + [d * slots + q * own]).astype(jnp.int32)
        NV, G0 = 2, 2 + nc
        images = jnp.sum(image_counts).astype(F32)
        fsc = jnp.stack([1.0 / (images * area), 1.0 / images, images * area, images])
        fsc = jnp.broadcast_to(fsc[:, None], (4, 128))

        TAPS = [(u, v) for u in range(3) for v in range(3)]

        def stats(sum_ref, fs, gains=None):
            avg = sum_ref[0:1] * fs[0:1, 0:1]
            inv = lax.rsqrt(sum_ref[1:2] * fs[0:1, 0:1] - avg * avg + EPSILON)
            return avg, inv

        def quarter_spec(r):
            return pl.BlockSpec((own, edge, edge, win), lambda i, s: (s[1] ^ r, 0, 0, 0))

        pa = jnp.concatenate(
            [
                split_weight.reshape(-1, 2 * lw),
                attend_weight.reshape(-1, 2 * lw),
                jnp.stack(
                    [
                        split_gain.reshape(-1),
                        split_shift.reshape(-1),
                        attend_bias.reshape(-1),
                        jnp.concatenate([reduce_gain, reduce_shift]),
                    ]
                ),
                jnp.zeros((4, 2 * lw), F32),
                squeeze_weight,
            ]
        )
        pb = jnp.concatenate([expand_weight, expand_gain[None], jnp.zeros((7, win), F32)])
        nw = 9 * half

        def reduce_body(rels, s, *refs):
            n = len(rels)
            w_ref, outs, scr = refs[n], refs[n + 1 : n + 1 + n], refs[-1]
            wh, wl = split2(w_ref[...])
            for k, r in enumerate(rels):
                x = padded(refs[k], scr, mask_of(s[NV + r], R, win, edge))
                xh, xl = split2(x)
                outs[k][...] = mm3(xh, xl, wh, wl)

        def reduce_call(rels):
            return call(
                functools.partial(reduce_body, rels),
                [features_in] * len(rels) + [reduce_weight],
                [((R, mid), F32)] * len(rels),
                [pltpu.VMEM((own * edge, PAD, win), F32)],
                isc,
                {k: quarter_spec(r) for k, r in enumerate(rels)},
                flops=6 * R * win * mid * len(rels),
            )

        p3, p1 = reduce_call((3, 1))
        p2, p0 = reduce_call((2, 0))
        y1 = p1 + swap(p3, "chan", 1)
        ys = swap(y1, "chan", 2)
        rc = swap(p2, "chan", 1)

        def red_body(s, a, b, y, red, sums):
            v = a[...] + b[...] + y[...]
            red[...] = v
            sums[0:1] = colsum(v)
            sums[1:2] = colsum(v * v)

        red, s1 = call(red_body, [p0, rc, ys], [((R, mid), F32), ((2, mid), F32)], scalars=isc)
        s1 = sum_all(s1)

        def gather3(x):
            y = swap(x, "chan", 2)
            return [x, y, swap(x, "chan", 1), swap(y, "chan", 1)]

        pa, _ = lax.optimization_barrier((pa, y1))
        pa_all = gather3(pa)

        def pa_body(s, p0, p1, p2, p3, wh, wl, wat, vec, wsq, scr):
            c = s[0]
            scr[c] = p0[...]
            scr[c ^ 2] = p1[...]
            scr[c ^ 1] = p2[...]
            scr[c ^ 3] = p3[...]

            def wide(lo, n):
                lane = lax.broadcasted_iota(jnp.int32, (n, 2 * lw), 1)
                out = [[], []]
                for pair in range(nc // 2):
                    a, b = scr[2 * pair, lo : lo + n, :], scr[2 * pair + 1, lo : lo + n, :]
                    out[0].append(jnp.where(lane < lw, a, pltpu.roll(b, lw, 1)))
                    out[1].append(jnp.where(lane < lw, pltpu.roll(a, lw, 1), b))
                return [jnp.concatenate(o, axis=1) for o in out]

            for t in range(9):
                for r, z in enumerate(wide(t * half, half)):
                    h, low = split2(z)
                    wh[r, t * half : (t + 1) * half, :] = h
                    wl[r, t * half : (t + 1) * half, :] = low
            for r, z in enumerate(wide(nw, inner)):
                wat[r] = z
            for r, z in enumerate(wide(nw + inner, 8)):
                vec[r] = z
            for k in range(nc):
                wsq[k * lw : (k + 1) * lw, :] = scr[k, nw + inner + 8 :, :]

        wh, wl, wat, vec, wsq = call(
            pa_body,
            pa_all,
            [
                ((2, nw, mid), BF16),
                ((2, nw, mid), BF16),
                ((2, inner, mid), F32),
                ((2, 8, mid), F32),
                ((mid, inner), F32),
            ],
            [pltpu.VMEM((nc,) + pa.shape, F32)],
            isc,
        )

        def taps_in(z, scrs, n):
            w = z.shape[1]
            rows = n * span
            for v in range(3):
                zz = z if v == 1 else pltpu.roll(z, 1 if v == 0 else rows - 1, 0)
                parts = split2(zz) if len(scrs) == 2 else [zz.astype(BF16)]
                for scr, part in zip(scrs, parts):
                    scr[v, :, 0] = jnp.zeros((n, PAD, w), BF16)
                    scr[v, :, edge + 1] = jnp.zeros((n, PAD, w), BF16)
                    scr[v, :, 1 : edge + 1] = part.reshape(n, edge, PAD, w)

        def conv_body(s, red, sums, fs, vec, wh, wl, out, sums2, zh, zl):
            avg, inv = stats(sums, fs)
            mask = mask_of(s[NV], R, mid, edge)
            z = jnp.maximum((red[...] - avg) * inv * vec[0, 3:4] + vec[1, 3:4], 0.0)
            z = jnp.where(mask, z, 0.0)
            taps_in(z, (zh, zl), own)
            for r in range(2):
                cols = slice(r * half, (r + 1) * half)
                hi = jnp.concatenate([zh[v, :, u : u + edge, :, cols].reshape(R, half) for u, v in TAPS], axis=1)
                lo = jnp.concatenate([zl[v, :, u : u + edge, :, cols].reshape(R, half) for u, v in TAPS], axis=1)
                y = mm3(hi, lo, wh[r], wl[r])
                out[:, r * mid : (r + 1) * mid] = y
                y = jnp.where(mask, y, 0.0)
                sums2[0:1, r * mid : (r + 1) * mid] = colsum(y)
                sums2[1:2, r * mid : (r + 1) * mid] = colsum(y * y)

        spl, s2 = call(
            conv_body,
            [red, s1, fsc, vec, wh, wl],
            [((R, 2 * mid), F32), ((2, 2 * mid), F32)],
            [pltpu.VMEM((3, own, PAD, PAD, mid), BF16)] * 2,
            isc,
            flops=12 * R * nw * mid,
        )
        red_r = gather3(lax.optimization_barrier((red, spl))[0])
        s2 = sum_all(s2)

        def second(spl, sums, fs, vec, r, mask):
            cols = slice(r * mid, (r + 1) * mid)
            avg = sums[0:1, cols] * fs[0:1, 0:1]
            inv = lax.rsqrt(sums[1:2, cols] * fs[0:1, 0:1] - avg * avg + EPSILON)
            norm = (spl[:, cols] - avg) * inv
            act = norm * vec[r, 0:1] + vec[r, 1:2]
            return norm, act, (act > 0) & mask, inv

        def per_image(z):
            return [colsum(z[b * span : (b + 1) * span]) for b in range(own)]

        def pool_body(s, spl, sums, fs, vec, wsq, c12, sq, sfc):
            mask = mask_of(s[NV], R, mid, edge)
            pooled = [0.0] * own
            nb = mid // 128
            for r in range(2):
                norm, act, on, _ = second(spl, sums, fs, vec, r, mask)
                c1 = per_image(jnp.where(on, 1.0, 0.0))
                c2 = per_image(jnp.where(on, norm, 0.0))
                for b in range(own):
                    for i in range(nb):
                        sl = slice(i * 128, (i + 1) * 128)
                        c12[b, r * nb + i : r * nb + i + 1, :] = c1[b][:, sl]
                        c12[b, (2 + r) * nb + i : (2 + r) * nb + i + 1, :] = c2[b][:, sl]
                    pooled[b] = pooled[b] + vec[r, 0:1] * c2[b] + vec[r, 1:2] * c1[b]
            p = jnp.concatenate(pooled + [jnp.zeros((8 - own, mid), F32)], axis=0) * (1.0 / area)
            v = exact(p, wsq[...])
            sq[...] = v
            live = lax.broadcasted_iota(jnp.int32, (8, inner), 0) < s[NV]
            v = jnp.where(live, v, 0.0)
            sfc[0:1] = colsum(v)
            sfc[1:2] = colsum(v * v)

        c12, sq, sfc = call(
            pool_body,
            [spl, s2, fsc, vec, wsq],
            [((own, 4 * mid // 128, 128), F32), ((8, inner), F32), ((2, inner), F32)],
            scalars=isc,
        )
        sfc = sum_all(sfc)
        ids = order_all()
        first_row = (ids // nc) * slots + quarter_of(ids % nc) * own
        c12_rel = gather_all(lax.optimization_barrier((c12, sfc))[0])
        sgb = jnp.stack([squeeze_gain, squeeze_shift])

        pb_all = gather3(lax.optimization_barrier((pb, s2))[0])

        def pb_body(s, p0, p1, p2, p3, wh, wl, g3):
            c = s[0]
            row = lax.broadcasted_iota(jnp.int32, (8, win), 0)
            g = jnp.zeros((8, win), F32)
            for k, p in ((0, p0), (2, p1), (1, p2), (3, p3)):
                h, low = split2(p[0:mid])
                wh[c ^ k] = h
                wl[c ^ k] = low
                g = jnp.where(row == (c ^ k), p[mid : mid + 1], g)
            g3[...] = g

        weh, wel, g3 = call(
            pb_body,
            pb_all,
            [((nc, mid, win), BF16), ((nc, mid, win), BF16), ((8, win), F32)],
            scalars=isc,
        )

        def squeeze_norm(sq, sums, fs, sgb):
            avg = sums[0:1] * fs[1:2, 0:1]
            inv = lax.rsqrt(sums[1:2] * fs[1:2, 0:1] - avg * avg + EPSILON)
            norm = (sq - avg) * inv
            return norm, norm * sgb[0:1] + sgb[1:2], inv

        def attend_body(s, spl, sums, fs, vec, sfc, sq, sgb, wat, att, wts):
            mask = mask_of(s[NV], R, mid, edge)
            _, actf, _ = squeeze_norm(sq[...], sfc, fs, sgb)
            hidden = jnp.maximum(actf, 0.0)
            lg = [exact(hidden, wat[r]) + vec[r, 2:3] for r in range(2)]
            top = jnp.maximum(lg[0], lg[1])
            e = [jnp.exp(z - top) for z in lg]
            total = e[0] + e[1]
            acc = 0.0
            imgs = lax.broadcasted_iota(jnp.int32, (R, mid), 0)
            for r in range(2):
                w = e[r] / total
                wts[r] = w
                _, act, on, _ = second(spl, sums, fs, vec, r, mask)
                wrow = w[0:1]
                for b in range(1, own):
                    wrow = jnp.where(imgs >= b * span, w[b : b + 1], wrow)
                acc = acc + jnp.where(on, act * wrow, 0.0)
            att[...] = acc

        att, wts = call(
            attend_body,
            [spl, s2, fsc, vec, sfc, sq, sgb, wat],
            [((R, mid), F32), ((2, 8, mid), F32)],
            scalars=isc,
        )
        att_r = gather3(att)

        def own_expand_body(s, att, wh, wl, sums):
            ah, al = split2(att[...])
            for k in range(nc):
                y = mm3(ah, al, wh[k], wl[k])
                sums[2 * k : 2 * k + 1] = colsum(y)
                sums[2 * k + 1 : 2 * k + 2] = colsum(y * y)

        (s3,) = call(
            own_expand_body, [att, weh, wel], [((2 * nc, win), F32)], scalars=isc, flops=6 * R * mid * win * nc
        )
        s3 = sum_all(s3)
        s3l = lax.dynamic_slice_in_dim(s3, 2 * c, 2, 0)
        eg = jnp.stack([expand_gain, expand_shift])

        def expand_body(rels, s, *refs):
            n = len(rels)
            atts, xs, gs = refs[:n], refs[n : 2 * n], refs[2 * n : 3 * n]
            w_ref, sums, fs, eg = refs[3 * n : 3 * n + 4]
            bos, gas = refs[3 * n + 4 : 4 * n + 4], refs[4 * n + 4 : 5 * n + 4]
            sg, t1, t2, u1 = refs[5 * n + 4 : 5 * n + 8]
            scr = refs[-1]
            avg, inv = stats(sums, fs)
            wh, wl = split2(w_ref[...])
            sg_acc, t1_acc, t2_acc, u_acc = [0.0, 0.0], 0.0, 0.0, 0.0
            for k, r in enumerate(rels):
                mask = mask_of(s[NV + r], R, win, edge)
                a = atts[k][...]
                ah, al = split2(a)
                norm = (mm3(ah, al, wh, wl) - avg) * inv
                x = padded(xs[k], scr, mask)
                pre = norm * eg[0:1] + eg[1:2] + x
                on = (pre > 0) & mask
                out = jnp.where(on, pre, 0.0)
                scr[...] = out.reshape(own * edge, PAD, win)
                bos[k][...] = scr[:, :edge, :].reshape(own, edge, edge, win)
                g = padded(gs[k], scr, on)
                sg_acc[0] += colsum(g)
                sg_acc[1] += colsum(g * norm)
                gb = g.astype(BF16)
                nb = jnp.where(mask, norm, 0.0).astype(BF16)
                gas[k][...] = mm((g * (eg[0:1] * inv)).astype(BF16), wh, ((1,), (1,)))
                t1_acc += mm(ah, gb, ((0,), (0,)))
                t2_acc += mm(ah, nb, ((0,), (0,)))
                u_acc += colsum(a)
            row = lax.broadcasted_iota(jnp.int32, (2 * nc, win), 0)
            z = jnp.where(row == 2 * s[0], sg_acc[0], 0.0)
            sg[...] = jnp.where(row == 2 * s[0] + 1, sg_acc[1], z)
            t1[...] = t1_acc
            t2[...] = t2_acc
            u1[...] = u_acc

        def expand_call(rels):
            n = len(rels)
            specs = {n + k: quarter_spec(r) for k, r in enumerate(rels)}
            specs.update({2 * n + k: quarter_spec(r) for k, r in enumerate(rels)})
            return call(
                functools.partial(expand_body, rels),
                [att_r[r] for r in rels] + [features_in] * n + [grad_out] * n + [expand_weight, s3l, fsc, eg],
                [((own, edge, edge, win), F32)] * n
                + [((R, mid), F32)] * n
                + [((2 * nc, win), F32), ((mid, win), F32), ((mid, win), F32), ((1, mid), F32)],
                [pltpu.VMEM((own * edge, PAD, win), F32)],
                isc,
                specs,
                flops=12 * R * mid * win * n,
            )

        bo3, bo1, ga3, ga1, sga, t1a, t2a, ua = expand_call((3, 1))
        bo2, bo0, ga2, ga0, sgb3, t1b, t2b, ub = expand_call((2, 0))
        gy1 = ga1 + swap(ga3, "chan", 1)
        gys = swap(gy1, "chan", 2)
        grc = swap(ga2, "chan", 1)
        sg3 = sum_all(sga + sgb3)
        bos = [bo0, bo1, bo2, bo3]
        sg3l = lax.dynamic_slice_in_dim(sg3, 2 * c, 2, 0)

        def dwe_body(s, t1a, t1b, t2a, t2b, ua, ub, sums, sg, fs, eg, out):
            avg, inv = stats(sums, fs)
            u = ua[...] + ub[...]
            outer = exact(u, sg[0:1], ((0,), (0,)))
            out[...] = (eg[0:1] * inv) * (
                t1a[...] + t1b[...] - (outer + (t2a[...] + t2b[...]) * sg[1:2]) * fs[0:1, 0:1]
            )

        def gatt_body(s, p, rc, ys, att, weh, g3, sums, sg, spl, sums2, fs, vec, wts, sfc, sq, sgb, wat, ga, gl, merged):
            m_acc, v_acc = 0.0, 0.0
            for k in range(nc):
                avg = sums[2 * k : 2 * k + 1] * fs[0:1, 0:1]
                inv = lax.rsqrt(sums[2 * k + 1 : 2 * k + 2] * fs[0:1, 0:1] - avg * avg + EPSILON)
                sc = g3[k : k + 1] * inv * fs[0:1, 0:1]
                kap = sg[2 * k + 1 : 2 * k + 2] * inv * sc
                w = weh[k]
                m_acc += mm((w.astype(F32) * kap).astype(BF16), w, ((1,), (1,)))
                vv = sg[2 * k : 2 * k + 1] * sc - avg * kap
                v_acc += exact(vv, w.astype(F32), ((1,), (1,)))
            mask = mask_of(s[NV], R, mid, edge)
            g = p[...] + rc[...] + ys[...] - mm(att[...].astype(BF16), m_acc.astype(BF16)) - v_acc
            g = jnp.where(mask, g, 0.0)
            ga[...] = g
            gw, a12 = [], []
            for r in range(2):
                norm, act, on, _ = second(spl, sums2, fs, vec, r, mask)
                gon = jnp.where(on, g, 0.0)
                a1, a2 = per_image(gon), per_image(gon * norm)
                zero = [jnp.zeros((8 - own, mid), F32)]
                a1, a2 = jnp.concatenate(a1 + zero, axis=0), jnp.concatenate(a2 + zero, axis=0)
                a12.append((a1, a2))
                gw.append(vec[r, 0:1] * a2 + vec[r, 1:2] * a1)
            mean = wts[0] * gw[0] + wts[1] * gw[1]
            gh = 0.0
            nb = mid // 128
            parts = []
            for r in range(2):
                z = wts[r] * (gw[r] - mean)
                for b in range(own):
                    for i in range(nb):
                        k = (b * 2 + r) * nb + i
                        gl[k : k + 1, :] = z[b : b + 1, i * 128 : (i + 1) * 128]
                gh = gh + exact(z, wat[r], ((1,), (1,)))
                for j in range(2):
                    parts.append(colsum(wts[r] * a12[r][j]))
            _, actf, _ = squeeze_norm(sq[...], sfc, fs, sgb)
            dzf = jnp.where(actf > 0, gh, 0.0)
            row = lax.broadcasted_iota(jnp.int32, (ni, inner), 0)
            z = jnp.zeros((ni, inner), F32)
            for b in range(own):
                z = jnp.where(row == s[G0] + b, dzf[b : b + 1], z)
            merged[0:ni] = z
            for k, pz in enumerate(parts):
                for i in range(nb):
                    merged[ni + k * nb + i : ni + k * nb + i + 1] = pz[:, i * 128 : (i + 1) * 128]

        nb = mid // 128
        ga, gl, merged = call(
            gatt_body,
            [ga0, grc, gys, att, weh, g3, s3, sg3, spl, s2, fsc, vec, wts, sfc, sq, sgb, wat],
            [((R, mid), F32), ((own * 2 * nb, 128), F32), ((ni + 4 * nb, inner), F32)],
            scalars=isc,
            flops=2 * R * mid * mid + 2 * nc * mid * mid * win,
        )
        merged = sum_all(merged)
        gl_rel = gather_all(lax.optimization_barrier((gl, merged))[0])

        osc = jnp.concatenate([isc, first_row.astype(jnp.int32)])
        ID0 = isc.shape[0]

        def all_body(s, c12r, vec, wsq, sfc, fs, sgb, c1_ref, c2_ref, pool_ref, norm_ref, hid_ref, scr):
            def place(j, _):
                for b in range(own):
                    scr[s[ID0 + j] + b] = c12r[j * own + b]
                return 0

            lax.fori_loop(0, nd * nc, place, 0)
            v = scr[...]
            pooled = 0.0
            for r in range(2):
                c1 = jnp.concatenate([v[:, r * nb + i, :] for i in range(nb)], axis=1)
                c2 = jnp.concatenate([v[:, (2 + r) * nb + i, :] for i in range(nb)], axis=1)
                c1_ref[r] = c1
                c2_ref[r] = c2
                pooled = pooled + vec[r, 0:1] * c2 + vec[r, 1:2] * c1
            pooled = pooled * (1.0 / area)
            pool_ref[...] = pooled
            norm, actf, _ = squeeze_norm(exact(pooled, wsq[...]), sfc, fs, sgb)
            norm_ref[...] = norm
            hid_ref[...] = jnp.maximum(actf, 0.0)

        c1_all, c2_all, pool_all, normf_all, hid_all = call(
            all_body,
            [c12_rel, vec, wsq, sfc, fsc, sgb],
            [
                ((2, ni, mid), F32),
                ((2, ni, mid), F32),
                ((ni, mid), F32),
                ((ni, inner), F32),
                ((ni, inner), F32),
            ],
            [pltpu.VMEM((ni, 4 * nb, 128), F32)],
            osc,
        )
        slot = jnp.arange(slots)
        amask = (slot[None] < image_counts[:, None]).astype(F32).reshape(ni, 1)
        amask = jnp.broadcast_to(amask, (ni, inner))

        def back_body(
            s, merged, c1a, c2a, normf, amask, sfc, fs, sgb, wsq, ga, spl, sums2, vec, wts, red, sums1, wh,
            dz1, sg1, b0, b1, b2, b3, gq_ref, sg2, gfc, zh, blk,
        ):
            dzf = merged[0:ni]
            norm_all = normf[...]
            s_f = colsum(dzf)
            g_f = colsum(dzf * norm_all)
            gfc[0:1] = g_f
            gfc[1:2] = s_f
            avg = sfc[0:1] * fs[1:2, 0:1]
            inv = lax.rsqrt(sfc[1:2] * fs[1:2, 0:1] - avg * avg + EPSILON)
            gq = sgb[0:1] * inv * (dzf - amask[...] * (s_f + norm_all * g_f) * fs[1:2, 0:1])
            gq_ref[...] = gq
            gp = exact(gq, wsq[...], ((1,), (1,))) * (1.0 / area)
            mask = mask_of(s[NV], R, mid, edge)
            imgs = lax.broadcasted_iota(jnp.int32, (R, mid), 0)
            grow = lax.broadcasted_iota(jnp.int32, (ni, mid), 0)
            gpo = [colsum(jnp.where(grow == s[G0] + b, gp, 0.0)) for b in range(own)]
            gprow = gpo[0]
            for b in range(1, own):
                gprow = jnp.where(imgs >= b * span, gpo[b], gprow)
            lane = lax.broadcasted_iota(jnp.int32, (R, 2 * lw), 1)
            gss = []
            acts = []
            for r in range(2):
                def piece(j):
                    k = (r * 2 + j) * nb
                    return jnp.concatenate([merged[ni + k + i : ni + k + i + 1] for i in range(nb)], axis=1)

                s2v = piece(0) + colsum(gp * c1a[r])
                g2v = piece(1) + colsum(gp * c2a[r])
                sg2[0, r : r + 1] = s2v
                sg2[1, r : r + 1] = g2v
                norm, act, on, inv2 = second(spl, sums2, fs, vec, r, mask)
                w = wts[r]
                wrow = w[0:1]
                for b in range(1, own):
                    wrow = jnp.where(imgs >= b * span, w[b : b + 1], wrow)
                dz = jnp.where(on, wrow * ga[...] + gprow, 0.0)
                gs = vec[r, 0:1] * inv2 * (dz - (s2v + norm * g2v) * fs[0:1, 0:1])
                gs = jnp.where(mask, gs, 0.0)
                gss.append(gs)
            for pair in range(nc // 2):
                cols = slice(pair * 2 * lw, (pair + 1) * 2 * lw)
                a, b = gss[0][:, cols], gss[1][:, cols]
                blk[2 * pair] = jnp.where(lane < lw, a, pltpu.roll(b, lw, 1))
                blk[2 * pair + 1] = jnp.where(lane < lw, pltpu.roll(a, lw, 1), b)
            for k, o in enumerate((b0, b1, b2, b3)):
                o[...] = blk[s[0] ^ k]
            avg1, inv1 = stats(sums1, fs)
            norm1 = (red[...] - avg1) * inv1
            on1 = (norm1 * vec[0, 3:4] + vec[1, 3:4] > 0) & mask
            for r in range(2):
                taps_in(gss[r], (zh,), own)
                acc = 0.0
                for t, (u, v) in enumerate(TAPS):
                    z = zh[2 - v, :, 2 - u : 2 - u + edge].reshape(R, mid)
                    acc += mm(z, wh[r, t * half : (t + 1) * half, :], ((1,), (1,)))
                cols = slice(r * half, (r + 1) * half)
                acc = jnp.where(on1[:, cols], acc, 0.0)
                dz1[:, cols] = acc
                sg1[0:1, cols] = colsum(acc)
                sg1[1:2, cols] = colsum(acc * norm1[:, cols])

        dz1, sg1, blk0, blk1, blk2, blk3, gq, sg2, gfc = call(
            back_body,
            [merged, c1_all, c2_all, normf_all, amask, sfc, fsc, sgb, wsq, ga, spl, s2, vec, wts, red, s1, wh],
            [((R, mid), F32), ((2, mid), F32)]
            + [((R, 2 * lw), F32)] * 4
            + [((ni, inner), F32), ((2, 2, mid), F32), ((2, inner), F32)],
            [pltpu.VMEM((3, own, PAD, PAD, mid), BF16), pltpu.VMEM((nc, R, 2 * lw), F32)],
            isc,
            flops=4 * R * nw * mid,
        )
        dz1_r = gather3(dz1)
        sg1 = sum_all(sg1)

        def final_grad(dz, red, sums, sg, fs, vec, mask):
            avg, inv = stats(sums, fs)
            norm = (red - avg) * inv
            g = vec[0, 3:4] * inv * (dz - (sg[0:1] + norm * sg[1:2]) * fs[0:1, 0:1])
            return jnp.where(mask, g, 0.0).astype(BF16)

        def dwr_body(s, d0, d1, d2, d3, r0, r1, r2, r3, x0, x1, x2, x3, sums, sg, fs, vec, out, go0, go1, go2, go3, scr):
            acc = 0.0
            for r, (dz, rd, x, go) in enumerate(
                ((d0, r0, x0, go0), (d1, r1, x1, go1), (d2, r2, x2, go2), (d3, r3, x3, go3))
            ):
                mask = mask_of(s[NV + r], R, win, edge)
                g = final_grad(dz[...], rd[...], sums, sg, fs, vec, mask)
                go[...] = g
                x = padded(x, scr, mask).astype(BF16)
                acc += mm(x, g, ((0,), (0,)))
            out[...] = acc

        dwr, gr0, gr1, gr2, gr3 = call(
            dwr_body,
            dz1_r + red_r + [features_in] * 4 + [s1, sg1, fsc, vec],
            [((win, mid), F32)] + [((R, mid), BF16)] * 4,
            [pltpu.VMEM((own * edge, PAD, win), F32)],
            isc,
            {8 + r: quarter_spec(r) for r in range(4)},
            flops=8 * R * win * mid,
        )
        grad_reduce_weight = big_sum_dp(dwr)

        def gin_body(s, g0, g1, g2, g3, bo0, bo1, bo2, bo3, go, w_ref, out_bo, out_gi, scr):
            w = w_ref[...].astype(BF16)
            for r, (g, bo) in enumerate(((g0, bo0), (g1, bo1), (g2, bo2), (g3, bo3))):
                z = mm(g[...], w, ((1,), (1,)))
                scr[...] = z.reshape(own * edge, PAD, win)
                z = scr[:, :edge, :].reshape(own, edge, edge, win)
                at = pl.ds((s[1] ^ r) * own, own)
                out_bo[at] = bo[...]
                out_gi[at] = z + jnp.where(bo[...] > 0, go[at], 0.0)

        block_out, grad_input = call(
            gin_body,
            [gr0, gr1, gr2, gr3] + bos + [grad_out, reduce_weight],
            [(features_in.shape, F32)] * 2,
            [pltpu.VMEM((own * edge, PAD, win), F32)],
            isc,
            flops=8 * R * win * mid,
        )

        blks = [blk0, swap(blk1, "chan", 1), swap(blk2, "chan", 2), swap(blk3, "chan", 3)]

        def dws_body(s, k0, k1, k2, k3, r0, r1, r2, r3, sums, fs, vec, out, zg, relu):
            avg, inv = stats(sums, fs)
            for k, (bk, rd, r) in enumerate(((k0, r0, 0), (k1, r2, 2), (k2, r1, 1), (k3, r3, 3))):
                mask = mask_of(s[NV + r], R, mid, edge)
                z = jnp.maximum((rd[...] - avg) * inv * vec[0, 3:4] + vec[1, 3:4], 0.0)
                relu[k * R : (k + 1) * R, :] = jnp.where(mask, z, 0.0).astype(BF16)
                taps_in(bk[...], (zg.at[:, k * own : (k + 1) * own],), own)
            rl = relu[...]
            lane = lax.broadcasted_iota(jnp.int32, (half, 2 * lw), 1)
            for t, (u, v) in enumerate(TAPS):
                z = zg[2 - v, :, 2 - u : 2 - u + edge].reshape(nc * R, 2 * lw)
                y = mm(rl, z, ((0,), (0,)))
                out[t * half : (t + 1) * half, :] = jnp.where(lane < lw, y[:half], y[half:])

        (dws,) = call(
            dws_body,
            blks + red_r + [s1, fsc, vec],
            [((nw, 2 * lw), F32)],
            [pltpu.VMEM((3, slots, PAD, PAD, 2 * lw), BF16), pltpu.VMEM((nc * R, mid), BF16)],
            isc,
            flops=2 * nc * R * mid * 9 * 2 * lw,
        )
        grad_split_weight = big_sum_dp(dws).reshape(split_weight.shape)

        (dwe,) = call(
            dwe_body,
            [t1a, t1b, t2a, t2b, ua, ub, s3l, sg3l, fsc, eg],
            [((mid, win), F32)],
            scalars=isc,
        )
        grad_expand_weight = big_sum_dp(dwe)

        def fc_body(s, glr, hid, pool, gq, waw, wab, wsw, scr):
            n = 2 * nb

            def place(j, _):
                for b in range(own):
                    scr[s[ID0 + j] + b] = glr[j * own + b]
                return 0

            lax.fori_loop(0, nd * nc, place, 0)
            v = scr[...]
            for r in range(2):
                z = jnp.concatenate([v[:, r * nb + i, :] for i in range(nb)], axis=1)
                wab[r : r + 1] = colsum(z)
                waw[r] = exact(hid[...], z, ((0,), (0,)))
            wsw[...] = exact(pool[...], gq[...], ((0,), (0,)))

        waw, wab, wsw = call(
            fc_body,
            [gl_rel.reshape(ni, 2 * nb, 128), hid_all, pool_all, gq],
            [((2, inner, mid), F32), ((2, mid), F32), ((mid, inner), F32)],
            [pltpu.VMEM((ni, 2 * nb, 128), F32)],
            osc,
        )

        def own_lanes(z, axis):
            return lax.dynamic_slice_in_dim(z, c * lw, lw, axis)

        return (
            block_out,
            grad_input,
            grad_reduce_weight,
            own_lanes(sg1[1], 0),
            own_lanes(sg1[0], 0),
            grad_split_weight,
            own_lanes(sg2[1], 1),
            own_lanes(sg2[0], 1),
            own_lanes(wsw, 0),
            gfc[0],
            gfc[1],
            own_lanes(waw, 2).transpose(1, 0, 2),
            own_lanes(wab, 1),
            grad_expand_weight,
            sg3l[1],
            sg3l[0],
        )

    return per_device


def solution(mesh):
    in_specs = (
        P("dp", None, None, "chan"),
        P(),
        P("chan", None),
        P("chan"),
        P("chan"),
        P(None, None, None, None, "chan"),
        P(None, "chan"),
        P(None, "chan"),
        P("chan", None),
        P(),
        P(),
        P(None, None, "chan"),
        P(None, "chan"),
        P(None, "chan"),
        P("chan"),
        P("chan"),
        P("dp", None, None, "chan"),
    )
    out_specs = (
        P("dp", None, None, "chan"),
        P("dp", None, None, "chan"),
        P("chan", None),
        P("chan"),
        P("chan"),
        P(None, None, None, None, "chan"),
        P(None, "chan"),
        P(None, "chan"),
        P("chan", None),
        P(),
        P(),
        P(None, None, "chan"),
        P(None, "chan"),
        P(None, "chan"),
        P("chan"),
        P("chan"),
    )
    return jax.shard_map(
        build(mesh), mesh=mesh, in_specs=in_specs, out_specs=out_specs, check_vma=False
    )
```

```python
import functools

import jax
import jax.numpy as jnp
from jax import lax
from jax.experimental import pallas as pl
from jax.experimental.pallas import tpu as pltpu
from jax.sharding import PartitionSpec as P

EPSILON = 1e-05
F32, BF16 = jnp.float32, jnp.bfloat16
PAD = 16
VMEM_LIMIT = 32 * 1024 * 1024


def bits_of(n):
    out, k = [], 1
    while k < n:
        out.append(k)
        k *= 2
    return out


def split2(x):
    hi = x.astype(BF16)
    return hi, (x - hi.astype(F32)).astype(BF16)


def mm(a, b, dims=((1,), (0,))):
    return lax.dot_general(a, b, (dims, ((), ())), preferred_element_type=F32)


def split3(x):
    hi = x.astype(BF16)
    x = x - hi.astype(F32)
    mid = x.astype(BF16)
    return hi, mid, (x - mid.astype(F32)).astype(BF16)


def mm3(a, b, dims=((1,), (0,))):
    return mm(a[0], b[0], dims) + (mm(a[0], b[1], dims) + mm(a[1], b[0], dims))


def mm6(a, b, dims=((1,), (0,))):
    small = mm(a[0], b[2], dims) + mm(a[2], b[0], dims) + mm(a[1], b[1], dims)
    return mm(a[0], b[0], dims) + (mm(a[0], b[1], dims) + mm(a[1], b[0], dims) + small)


def exact(a, b, dims=((1,), (0,))):
    return lax.dot_general(
        a, b, (dims, ((), ())), precision=lax.Precision.HIGHEST, preferred_element_type=F32
    )


def call(body, counts, ins, outs, scratch=(), flops=0, far=(), far_out=()):
    far, far_out = sorted(far), sorted(far_out)
    moved = sum(a.size * a.dtype.itemsize for a in ins) + sum(
        int(jnp.dtype(d).itemsize) * functools.reduce(lambda x, y: x * y, s, 1) for s, d in outs
    )
    vmem, hbm = pl.BlockSpec(memory_space=pltpu.VMEM), pl.BlockSpec(memory_space=pltpu.HBM)
    own_scratch = len(scratch)
    held = [pltpu.VMEM(ins[k].shape, ins[k].dtype) for k in far] + [pltpu.VMEM(*outs[k]) for k in far_out]
    sems = [pltpu.SemaphoreType.DMA] * len(held)

    def kernel(s, *refs):
        n, m = len(ins), len(outs)
        refs_in, refs_out = list(refs[:n]), list(refs[n : n + m])
        rest = refs[n + m :]
        scr, bufs, sem = rest[:own_scratch], rest[own_scratch : own_scratch + len(held)], rest[own_scratch + len(held) :]
        copies = []
        for i, k in enumerate(far):
            copies.append(pltpu.make_async_copy(refs_in[k], bufs[i], sem[i]))
            copies[-1].start()
            refs_in[k] = bufs[i]
        homes = []
        for i, k in enumerate(far_out):
            i += len(far)
            homes.append(pltpu.make_async_copy(bufs[i], refs_out[k], sem[i]))
            refs_out[k] = bufs[i]
        for copy in copies:
            copy.wait()
        body(s, *refs_in, *refs_out, *scr)
        for copy in homes:
            copy.start()
        for copy in homes:
            copy.wait()

    ins = [pltpu.with_memory_space_constraint(a, pltpu.HBM) if k in far else a for k, a in enumerate(ins)]
    return pl.pallas_call(
        kernel,
        out_shape=[pltpu.HBM(s, d) if k in far_out else jax.ShapeDtypeStruct(s, d) for k, (s, d) in enumerate(outs)],
        in_specs=[pl.BlockSpec(memory_space=pltpu.SMEM)] + [hbm if k in far else vmem for k in range(len(ins))],
        out_specs=[hbm if k in far_out else vmem for k in range(len(outs))],
        scratch_shapes=list(scratch) + held + sems,
        compiler_params=pltpu.CompilerParams(vmem_limit_bytes=VMEM_LIMIT),
        cost_estimate=pl.CostEstimate(flops=flops, bytes_accessed=moved, transcendentals=0),
    )(counts, *ins)


def mask_of(nv, rows, cols, edge):
    r = lax.broadcasted_iota(jnp.int32, (rows, cols), 0)
    return ((r & (PAD - 1)) < edge) & (r < nv * (edge * PAD))


def colsum(x):
    return jnp.sum(x, axis=0, keepdims=True)


def build(mesh):
    nd, nc = mesh.shape["dp"], mesh.shape["chan"]
    both = ("dp", "chan")
    cbits, dbits = bits_of(nc), bits_of(nd)
    flat_bits = bits_of(nd * nc)
    pairs = [flat_bits[i : i + 2] for i in range(1, len(flat_bits), 2)]
    sum_groups = [[1]] + [[k | 1 for k in ([p[0], p[1], p[0] ^ p[1]] if len(p) == 2 else p)] for p in pairs[::-1]]

    def swap(x, axis, k):
        n = {"dp": nd, "chan": nc}[axis] if isinstance(axis, str) else nd * nc
        return lax.ppermute(x, axis, [(i, i ^ k) for i in range(n)])

    def sum_steps(x):
        out = [x]
        for g in sum_groups:
            x = out[-1]
            got = [swap(x, both, k) for k in g]
            x = x + got[0]
            out.append(x + (got[1] + got[2]) if len(g) == 3 else x)
        return out

    def sum_all(x):
        return sum_steps(x)[-1]

    def after(x, *deps):
        return lax.optimization_barrier((x,) + deps)[0]

    def pick(x, i):
        return lax.dynamic_index_in_dim(x, i, 0, False)

    groups = [dbits[:1]] + [dbits[i : i + 2] for i in range(1, len(dbits), 2)]

    def masks(g):
        out = [0]
        for k in g:
            out = out + [m ^ k for m in out]
        return out

    def place_in(g):
        n = 2 ** len(g)
        return (lax.axis_index("dp") // g[0]) % n, n

    def cut_chunks(scr, g, outs):
        at, n = place_in(g)
        rows = scr.shape[0] // n
        for m, o in enumerate(outs):
            o[...] = scr[pl.ds(pl.multiple_of((at ^ m) * rows, 8), rows), :]

    def chunk_outs(rows, g):
        n = 2 ** len(g)
        return [((rows // n, 128), F32)] * n

    def padded_rows(rows):
        return -(-rows // (8 * nd)) * 8 * nd

    def big_sum_dp(counts, chunks):
        for i, g in enumerate(groups):
            got = [chunks[0]] + [swap(z, "dp", m) for z, m in zip(chunks[1:], masks(g)[1:])]
            rows = got[0].shape[0]
            last = i == len(groups) - 1

            def add_body(s, *refs, n=len(got), last=last, i=i):
                v = refs[0][...]
                for z in refs[1:n]:
                    v = v + z[...]
                if last:
                    refs[n][...] = v
                else:
                    refs[-1][...] = v
                    cut_chunks(refs[-1], groups[i + 1], refs[n:-1])

            chunks = call(
                add_body,
                counts,
                got,
                [((rows, 128), F32)] if last else chunk_outs(rows, groups[i + 1]),
                [] if last else [pltpu.VMEM((rows, 128), F32)],
            )
        (x,) = chunks
        for g in groups[::-1]:
            got = [x] + [swap(x, "dp", m) for m in masks(g)[1:]]
            rows = x.shape[0]

            def join_body(s, *refs, g=g, rows=rows):
                at, _ = place_in(g)
                for m, z in enumerate(refs[:-1]):
                    refs[-1][pl.ds(pl.multiple_of((at ^ m) * rows, 8), rows), :] = z[...]

            (x,) = call(join_body, counts, got, [((rows * len(got), 128), F32)])
        return x

    def quarter_of(chan):
        q = chan * 0
        for k in cbits:
            q = q * 2 + (chan // k) % 2
        return q

    def per_device(
        features_in,
        image_counts,
        reduce_weight,
        reduce_gain,
        reduce_shift,
        split_weight,
        split_gain,
        split_shift,
        squeeze_weight,
        squeeze_gain,
        squeeze_shift,
        attend_weight,
        attend_bias,
        expand_weight,
        expand_gain,
        expand_shift,
        grad_out,
    ):
        slots, edge = features_in.shape[0], features_in.shape[1]
        area = edge * edge
        win = features_in.shape[3]
        mid = reduce_weight.shape[1]
        half = mid // 2
        lw = split_weight.shape[4]
        inner = squeeze_gain.shape[0]
        own = slots // nc
        span = edge * PAD
        R = own * span
        ni = nd * slots
        c = lax.axis_index("chan")

        def me():
            c = lax.axis_index("chan")
            return c, quarter_of(c)

        def valid(s, r):
            return jnp.clip(s[lax.axis_index("dp")] - (me()[1] ^ r) * own, 0, own)

        def recip(s, each):
            total = s[0]
            for i in range(1, nd):
                total = total + s[i]
            return (1.0 / (jnp.full((1, 128), total, jnp.int32).astype(F32) * each))[:, 0:1]

        TAPS = [(u, v) for u in range(3) for v in range(3)]

        def stats(sum_ref, s):
            n = recip(s, area)
            avg = sum_ref[0:1] * n
            inv = lax.rsqrt(sum_ref[1:2] * n - avg * avg + EPSILON)
            return avg, inv, n

        lb = win // 128

        def native(x):
            x = x.transpose(1, 2, 0, 3).reshape(area, slots, lb, 128)
            return x.transpose(0, 2, 1, 3).reshape(area * lb * slots, 128)

        def from_native(z):
            z = z.reshape(area, lb, slots, 128).transpose(0, 2, 1, 3)
            return z.reshape(edge, edge, slots, win).transpose(2, 0, 1, 3)

        def place_of(h, i, b, r):
            at = (h * edge * lb + i) * slots + (me()[1] ^ r) * own + b
            return pl.ds(at, edge, stride=lb * slots)

        def load_quarter(ref, scr, r, mask):
            for b in range(own):
                for h in range(edge):
                    for i in range(lb):
                        scr[b * edge + h, :edge, i * 128 : (i + 1) * 128] = ref[place_of(h, i, b, r), :]
            return jnp.where(mask, scr[...].reshape(R, win), 0.0)

        def store_quarter(ref, scr, r, z):
            scr[...] = z.reshape(own * edge, PAD, win)
            for b in range(own):
                for h in range(edge):
                    for i in range(lb):
                        ref[place_of(h, i, b, r), :] = scr[b * edge + h, :edge, i * 128 : (i + 1) * 128]

        feats, gouts = native(features_in), native(grad_out)
        quarter_scratch = pltpu.VMEM((own * edge, PAD, win), F32)

        wt = split_weight.transpose(0, 1, 3, 4, 2).reshape(-1, half)

        wt_c, wt_y = swap(wt, "chan", 1), swap(wt, "chan", 2)

        def pack(att_w, sq_w, rg, rs, sg, ss, ab, eg):
            return jnp.concatenate(
                [
                    att_w.transpose(1, 2, 0).reshape(2 * lw, inner),
                    sq_w,
                    sg.reshape(1, -1),
                    ss.reshape(1, -1),
                    ab.reshape(1, -1),
                    jnp.concatenate([rg, rs])[None],
                    eg.reshape(-1, 2 * lw),
                    jnp.zeros((8 - 4 - win // (2 * lw), 2 * lw), F32),
                ]
            )

        nw = 9 * half

        def reduce_body(rels, s, x_ref, w_ref, *refs):
            outs, scr = refs[:-1], refs[-1]
            w = split3(w_ref[...])
            for o, r in zip(outs, rels):
                x = load_quarter(x_ref, scr, r, mask_of(valid(s, r), R, win, edge))
                o[...] = mm6(split3(x), w)

        def reduce_call(rels):
            return call(
                functools.partial(reduce_body, rels),
                image_counts,
                [feats, reduce_weight],
                [((R, mid), F32)] * len(rels),
                [quarter_scratch],
                flops=12 * R * win * mid * len(rels),
                far=(0, 1),
            )

        p3, p1 = reduce_call((3, 1))
        p2, p0 = reduce_call((2, 0))
        y1 = p1 + swap(p3, "chan", 1)
        ys = swap(y1, "chan", 2)
        rc = swap(p2, "chan", 1)

        def gather3(x, gate=None):
            y = swap(x, "chan", 2)
            return [x, y, swap(x, "chan", 1), swap(y if gate is None else after(y, gate), "chan", 1)]

        small = lax.optimization_barrier(
            (
                y1,
                attend_weight,
                squeeze_weight,
                reduce_gain,
                reduce_shift,
                split_gain,
                split_shift,
                attend_bias,
                expand_gain,
            )
        )
        ps = pack(*small[1:])
        wt_r = [wt, wt_y, wt_c, swap(after(wt_y, y1), "chan", 1)]
        ps_all = gather3(ps)

        def pa_body(s, p0, p1, p2, p3, wat, vec, wsq, g3, scr):
            c, _ = me()
            scr[c] = p0[...]
            scr[c ^ 2] = p1[...]
            scr[c ^ 1] = p2[...]
            scr[c ^ 3] = p3[...]
            lo = 2 * lw + lw
            lane = lax.broadcasted_iota(jnp.int32, (8, 2 * lw), 1)
            for pair in range(nc // 2):
                a, b = scr[2 * pair, lo : lo + 8, :], scr[2 * pair + 1, lo : lo + 8, :]
                cols = slice(pair * 2 * lw, (pair + 1) * 2 * lw)
                vec[0, :, cols] = jnp.where(lane < lw, a, pltpu.roll(b, lw, 1))
                vec[1, :, cols] = jnp.where(lane < lw, pltpu.roll(a, lw, 1), b)
            g3[...] = jnp.zeros((8, win), F32)
            for k in range(nc):
                rows = slice(k * lw, (k + 1) * lw)
                for r in range(2):
                    wat[r, rows, :] = scr[k, r * lw : (r + 1) * lw, :]
                wsq[rows, :] = scr[k, 2 * lw : lo, :]
                for i in range(win // (2 * lw)):
                    g3[k : k + 1, i * 2 * lw : (i + 1) * 2 * lw] = scr[k, lo + 4 + i : lo + 5 + i, :]

        wat, vec, wsq, g3 = call(
            pa_body,
            image_counts,
            ps_all,
            [((2, mid, inner), F32), ((2, 8, mid), F32), ((mid, inner), F32), ((8, win), F32)],
            [pltpu.VMEM((nc,) + ps.shape, F32)],
        )

        CHAN_REL = (0, 2, 1, 3)

        def wt_body(s, v0, v1, v2, v3, w1, w2, w3, w1_home):
            for rel, ref in enumerate((v0, v1, v2, v3)):
                rows = pl.ds(pl.multiple_of((me()[0] ^ CHAN_REL[rel]) * lw, lw), lw)
                for t in range(9):
                    for r in range(2):
                        at = t * 2 * lw + r * lw
                        for o, z in zip((w1, w2, w3), split3(ref[at : at + lw, :])):
                            o[r, rows, t * half : (t + 1) * half] = z
            w1_home[...] = w1[...]

        w1, w2, w3, w1_home = call(
            wt_body, image_counts, wt_r, [((2, mid, nw), BF16)] * 4, far=(0,), far_out=(3,)
        )

        def red_body(s, a, b, y, red, sums):
            v = a[...] + b[...] + y[...]
            red[...] = v
            sums[0:1] = colsum(v)
            sums[1:2] = colsum(v * v)

        red, s1 = call(red_body, image_counts, [p0, rc, after(ys, vec, w1)], [((R, mid), F32), ((2, mid), F32)])
        s1_steps = sum_steps(s1)
        s1 = s1_steps[-1]

        def taps_in(z, scrs, n):
            w = z.shape[1]
            rows = n * span
            for v in range(3):
                zz = z if v == 1 else pltpu.roll(z, 1 if v == 0 else rows - 1, 0)
                parts = split3(zz) if len(scrs) == 3 else [zz.astype(BF16)]
                for scr, part in zip(scrs, parts):
                    scr[v, :, 0] = jnp.zeros((n, PAD, w), BF16)
                    scr[v, :, edge + 1] = jnp.zeros((n, PAD, w), BF16)
                    scr[v, :, 1 : edge + 1] = part.reshape(n, edge, PAD, w)

        def conv_body(s, red, sums, vec, w1, w2, w3, out, sums2, za, zb, zc):
            avg, inv, _ = stats(sums, s)
            mask = mask_of(valid(s, 0), R, mid, edge)
            z = jnp.maximum((red[...] - avg) * inv * vec[0, 3:4] + vec[1, 3:4], 0.0)
            z = jnp.where(mask, z, 0.0)
            taps_in(z, (za, zb, zc), own)
            for r in range(2):
                cols = slice(r * half, (r + 1) * half)
                lhs = [
                    jnp.concatenate([z[v, :, u : u + edge, :, cols].reshape(R, half) for u, v in TAPS], axis=1)
                    for z in (za, zb, zc)
                ]
                y = mm6(lhs, (w1[r], w2[r], w3[r]), ((1,), (1,)))
                out[:, r * mid : (r + 1) * mid] = y
                y = jnp.where(mask, y, 0.0)
                sums2[0:1, r * mid : (r + 1) * mid] = colsum(y)
                sums2[1:2, r * mid : (r + 1) * mid] = colsum(y * y)

        spl, s2 = call(
            conv_body,
            image_counts,
            [red, s1, vec, w1, w2, w3],
            [((R, 2 * mid), F32), ((2, 2 * mid), F32)],
            [pltpu.VMEM((3, own, PAD, PAD, mid), BF16)] * 3,
            flops=24 * R * nw * mid,
        )
        we_all = lax.all_gather(after(expand_weight, s1), "chan")
        s2_steps = sum_steps(s2)
        s2 = s2_steps[-1]

        def second(spl, sums, n, vec, r, mask):
            cols = slice(r * mid, (r + 1) * mid)
            avg = sums[0:1, cols] * n
            inv = lax.rsqrt(sums[1:2, cols] * n - avg * avg + EPSILON)
            norm = (spl[:, cols] - avg) * inv
            act = norm * vec[r, 0:1] + vec[r, 1:2]
            return norm, act, (act > 0) & mask, inv

        def per_image(z):
            return [colsum(z[b * span : (b + 1) * span]) for b in range(own)]

        nb = mid // 128
        BLOCK = max(64, 4 * nb * own)
        ND = nd * nc

        def pool_body(s, spl, sums, vec, wsq, c12, sq, sfc):
            mask = mask_of(valid(s, 0), R, mid, edge)
            n = recip(s, area)
            pooled = [0.0] * own
            c12[...] = jnp.zeros((BLOCK, 128), F32)
            for r in range(2):
                norm, act, on, _ = second(spl, sums, n, vec, r, mask)
                c1 = per_image(jnp.where(on, 1.0, 0.0))
                c2 = per_image(jnp.where(on, norm, 0.0))
                for b in range(own):
                    for i in range(nb):
                        sl = slice(i * 128, (i + 1) * 128)
                        for k, z in ((r * nb + i, c1), ((2 + r) * nb + i, c2)):
                            c12[k * own + b : k * own + b + 1, :] = z[b][:, sl]
                    pooled[b] = pooled[b] + vec[r, 0:1] * c2[b] + vec[r, 1:2] * c1[b]
            p = jnp.concatenate(pooled + [jnp.zeros((8 - own, mid), F32)], axis=0) * (1.0 / area)
            v = exact(p, wsq[...])
            sq[...] = v
            live = lax.broadcasted_iota(jnp.int32, (8, inner), 0) < valid(s, 0)
            v = jnp.where(live, v, 0.0)
            sfc[0:1] = colsum(v)
            sfc[1:2] = colsum(v * v)

        c12, sq, sfc = call(
            pool_body,
            image_counts,
            [spl, s2, vec, wsq],
            [((BLOCK, 128), F32), ((8, inner), F32), ((2, inner), F32)],
        )
        c12_g = lax.all_gather(c12, both, axis=0, tiled=True)
        sfc = sum_all(sfc)
        red_g = lax.all_gather(after(red, sfc), "chan")
        sgb = jnp.stack([squeeze_gain, squeeze_shift])

        def squeeze_norm(sq, sums, s, sgb):
            n = recip(s, 1)
            avg = sums[0:1] * n
            inv = lax.rsqrt(sums[1:2] * n - avg * avg + EPSILON)
            norm = (sq - avg) * inv
            return norm, norm * sgb[0:1] + sgb[1:2], inv

        def attend_body(s, spl, sums, vec, sfc, sq, sgb, wat, att, wts):
            mask = mask_of(valid(s, 0), R, mid, edge)
            n = recip(s, area)
            _, actf, _ = squeeze_norm(sq[...], sfc, s, sgb)
            hidden = jnp.maximum(actf, 0.0)
            lg = [exact(hidden, wat[r], ((1,), (1,))) + vec[r, 2:3] for r in range(2)]
            top = jnp.maximum(lg[0], lg[1])
            e = [jnp.exp(z - top) for z in lg]
            total = e[0] + e[1]
            acc = 0.0
            imgs = lax.broadcasted_iota(jnp.int32, (R, mid), 0)
            for r in range(2):
                w = e[r] / total
                wts[r] = w
                _, act, on, _ = second(spl, sums, n, vec, r, mask)
                wrow = w[0:1]
                for b in range(1, own):
                    wrow = jnp.where(imgs >= b * span, w[b : b + 1], wrow)
                acc = acc + jnp.where(on, act * wrow, 0.0)
            att[...] = acc

        att, wts = call(
            attend_body,
            image_counts,
            [spl, s2, vec, sfc, sq, sgb, wat],
            [((R, mid), F32), ((2, 8, mid), F32)],
        )

        def own_expand_body(s, att, w, sums):
            a = split2(att[...])
            for k in range(nc):
                y = mm3(a, split2(w[k]))
                sums[2 * k : 2 * k + 1] = colsum(y)
                sums[2 * k + 1 : 2 * k + 2] = colsum(y * y)

        (s3,) = call(
            own_expand_body, image_counts, [att, we_all], [((2 * nc, win), F32)], flops=6 * R * mid * win * nc, far=(1,)
        )
        s3_steps = sum_steps(s3)
        s3 = s3_steps[-1]
        att_r = gather3(att, s3_steps[-2])
        s3l = lax.dynamic_slice_in_dim(s3, 2 * c, 2, 0)
        eg = jnp.stack([expand_gain, expand_shift])

        def expand_body(rels, extra, s, *refs):
            n = len(rels)
            atts, (x_ref, g_ref, w_ref, sums, eg) = refs[:n], refs[n : n + 5]
            prev, refs = refs[n + 5 : n + 5 + extra], refs[n + 5 + extra :]
            bos, gas = refs[:n], refs[n : 2 * n]
            sg, t1, t2, u1, scr = refs[2 * n :]
            avg, inv, _ = stats(sums, s)
            w = split2(w_ref[...])
            sg_acc, t1_acc, t2_acc, u_acc = [0.0, 0.0], 0.0, 0.0, 0.0
            for k, r in enumerate(rels):
                mask = mask_of(valid(s, r), R, win, edge)
                a = atts[k][...]
                ap = split2(a)
                norm = (mm3(ap, w) - avg) * inv
                x = load_quarter(x_ref, scr, r, mask)
                pre = norm * eg[0:1] + eg[1:2] + x
                on = (pre > 0) & mask
                bos[k][...] = jnp.where(on, pre, 0.0)
                g = load_quarter(g_ref, scr, r, on)
                sg_acc[0] += colsum(g)
                sg_acc[1] += colsum(g * norm)
                gb = g.astype(BF16)
                nb = jnp.where(mask, norm, 0.0).astype(BF16)
                gas[k][...] = mm((g * (eg[0:1] * inv)).astype(BF16), w[0], ((1,), (1,)))
                t = mm(ap[0], jnp.concatenate([gb, nb], axis=1), ((0,), (0,)))
                t1_acc += t[:, :win]
                t2_acc += t[:, win:]
                u_acc += colsum(a)
            row = lax.broadcasted_iota(jnp.int32, (2 * nc, win), 0)
            c, _ = me()
            z = jnp.where(row == 2 * c, sg_acc[0], 0.0)
            sg[...] = jnp.where(row == 2 * c + 1, sg_acc[1], z)
            for o, z, p in zip((t1, t2, u1), (t1_acc, t2_acc, u_acc), prev[1:] or (None,) * 3):
                o[...] = z if p is None else z + p[...]
            if prev:
                sg[...] = sg[...] + prev[0][...]

        def expand_call(rels, prev):
            n = len(rels)
            return call(
                functools.partial(expand_body, rels, len(prev)),
                image_counts,
                [att_r[r] for r in rels] + [feats, gouts, expand_weight, s3l, eg] + prev,
                [((R, win), F32)] * n
                + [((R, mid), F32)] * n
                + [((2 * nc, win), F32), ((mid, win), F32), ((mid, win), F32), ((1, mid), F32)],
                [quarter_scratch],
                flops=12 * R * mid * win * n,
                far=(n, n + 1, n + 2),
                far_out=tuple(range(n)) + ((2 * n + 1, 2 * n + 2) if prev else ()),
            )

        bo3, bo1, ga3, ga1, *prev = expand_call((3, 1), [])
        bo2, bo0, ga2, ga0, sg3, t1, t2, u1 = expand_call((2, 0), list(prev))
        gy1 = ga1 + swap(ga3, "chan", 1)
        gys = swap(gy1, "chan", 2)
        grc = swap(ga2, "chan", 1)
        sg3 = sum_all(sg3)
        bos = [bo0, bo1, bo2, bo3]
        sg3l = lax.dynamic_slice_in_dim(sg3, 2 * c, 2, 0)

        def gatt_body(s, p, rc, ys, att, we, g3, sums, sg, spl, sums2, vec, wts, sfc, sq, sgb, wat, ga, l0, l1, l2, l3, merged, scr):
            m_acc, v_acc = 0.0, 0.0
            n = recip(s, area)
            for k in range(nc):
                avg = sums[2 * k : 2 * k + 1] * n
                inv = lax.rsqrt(sums[2 * k + 1 : 2 * k + 2] * n - avg * avg + EPSILON)
                sc = g3[k : k + 1] * inv * n
                kap = sg[2 * k + 1 : 2 * k + 2] * inv * sc
                w = we[k]
                wb = w.astype(BF16)
                m_acc += mm((w * kap).astype(BF16), wb, ((1,), (1,)))
                vv = sg[2 * k : 2 * k + 1] * sc - avg * kap
                row = lax.broadcasted_iota(jnp.int32, (16, win), 0)
                high = jnp.where(row == 0, vv, 0.0)
                low = jnp.where(row == 1, vv - vv.astype(BF16).astype(F32), 0.0)
                v_acc += colsum(mm((high + low).astype(BF16), wb, ((1,), (1,))))
            mask = mask_of(valid(s, 0), R, mid, edge)
            g = p[...] + rc[...] + ys[...] - mm(att[...].astype(BF16), m_acc.astype(BF16)) - v_acc
            g = jnp.where(mask, g, 0.0)
            ga[...] = g
            gw, a12 = [], []
            for r in range(2):
                norm, act, on, _ = second(spl, sums2, n, vec, r, mask)
                gon = jnp.where(on, g, 0.0)
                a1, a2 = per_image(gon), per_image(gon * norm)
                zero = [jnp.zeros((8 - own, mid), F32)]
                a1, a2 = jnp.concatenate(a1 + zero, axis=0), jnp.concatenate(a2 + zero, axis=0)
                a12.append((a1, a2))
                gw.append(vec[r, 0:1] * a2 + vec[r, 1:2] * a1)
            mean = wts[0] * gw[0] + wts[1] * gw[1]
            gh = 0.0
            parts, zs = [], []
            for r in range(2):
                z = wts[r] * (gw[r] - mean)
                zs.append(z)
                gh = gh + exact(z, wat[r])
                for j in range(2):
                    parts.append(colsum(wts[r] * a12[r][j]))
            parts += [colsum(z) for z in zs]
            _, actf, _ = squeeze_norm(sq[...], sfc, s, sgb)
            dzf = jnp.where(actf > 0, gh, 0.0)
            c, _ = me()
            row = lax.broadcasted_iota(jnp.int32, (ni, inner), 0)
            z = jnp.zeros((ni, inner), F32)
            for b in range(own):
                z = jnp.where(row == lax.axis_index("dp") * nc + c + b * ND, dzf[b : b + 1], z)
            merged[0:ni] = z
            lane = lax.broadcasted_iota(jnp.int32, (8, 2 * lw), 1)
            for pair in range(nc // 2):
                cols = slice(pair * 2 * lw, (pair + 1) * 2 * lw)
                a, b = zs[0][:, cols], zs[1][:, cols]
                scr[2 * pair] = jnp.where(lane < lw, a, pltpu.roll(b, lw, 1))
                scr[2 * pair + 1] = jnp.where(lane < lw, pltpu.roll(a, lw, 1), b)
            for k, o in enumerate((l0, l1, l2, l3)):
                o[...] = scr[c ^ k]
            merged[ni:] = jnp.zeros((6 * nb + 4, inner), F32)
            for k, pz in enumerate(parts):
                for i in range(nb):
                    merged[ni + k * nb + i : ni + k * nb + i + 1] = pz[:, i * 128 : (i + 1) * 128]

        ga, l0, l1, l2, l3, merged = call(
            gatt_body,
            image_counts,
            [ga0, grc, gys, att, we_all, g3, s3, sg3, spl, s2, vec, wts, sfc, sq, sgb, wat],
            [((R, mid), F32)] + [((8, 2 * lw), F32)] * 4 + [((ni + 6 * nb + 4, inner), F32)],
            [pltpu.VMEM((nc, 8, 2 * lw), F32)],
            flops=2 * R * mid * mid + 2 * nc * mid * mid * win,
            far=(4,),
            far_out=(0,),
        )

        def all_body(s, g, vec, wsq, sfc, sgb, c1_ref, c2_ref, pool_ref, norm_ref, hid_ref):
            def rows(k):
                return jnp.concatenate([g[pl.ds(k * own + b, ND, stride=BLOCK), :] for b in range(own)], axis=0)

            pooled = 0.0
            for r in range(2):
                c1 = jnp.concatenate([rows(r * nb + i) for i in range(nb)], axis=1)
                c2 = jnp.concatenate([rows((2 + r) * nb + i) for i in range(nb)], axis=1)
                c1_ref[r] = c1
                c2_ref[r] = c2
                pooled = pooled + vec[r, 0:1] * c2 + vec[r, 1:2] * c1
            pooled = pooled * (1.0 / area)
            pool_ref[...] = pooled
            norm, actf, _ = squeeze_norm(exact(pooled, wsq[...]), sfc, s, sgb)
            norm_ref[...] = norm
            hid_ref[...] = jnp.maximum(actf, 0.0)

        c1_all, c2_all, pool_all, normf_all, hid_all = call(
            all_body,
            image_counts,
            [c12_g, vec, wsq, sfc, sgb],
            [
                ((2, ni, mid), F32),
                ((2, ni, mid), F32),
                ((ni, mid), F32),
                ((ni, inner), F32),
                ((ni, inner), F32),
            ],
            far=(0,),
        )
        for k, g in enumerate(sum_groups):
            got = [swap(merged, both, m) for m in g]
            z = merged + got[0]
            merged = z + (got[1] + got[2]) if len(g) == 3 else z
            if k == 1:
                merged, c1_all = lax.optimization_barrier((merged, c1_all))

        def all_valid(s):
            row = lax.broadcasted_iota(jnp.int32, (ni, inner), 0)
            dev = row & (ND - 1)
            at, chan = dev >> (nc.bit_length() - 1), dev & (nc - 1)
            slot = (row >> (ND.bit_length() - 1)) + own * sum(
                ((chan >> i) & 1) * (nc >> (i + 1)) for i in range(len(cbits))
            )
            live = jnp.zeros((ni, inner), jnp.int32)
            for i in range(nd):
                live = jnp.where(at == i, s[i], live)
            return jnp.where(slot < live, 1.0, 0.0)

        def back_body(
            s, merged, c1a, c2a, normf, sfc, sgb, wsq, ga, spl, sums2, vec, wts, red, sums1, w1,
            dz1, sg1, b0, b1, b2, b3, gq_ref, sg2, gfc, wab, zh, blk,
        ):
            dzf = merged[0:ni]
            norm_all = normf[...]
            s_f = colsum(dzf)
            g_f = colsum(dzf * norm_all)
            gfc[0:1] = g_f
            gfc[1:2] = s_f
            for r in range(2):
                for i in range(nb):
                    k = ni + (4 + r) * nb + i
                    wab[r : r + 1, i * 128 : (i + 1) * 128] = merged[k : k + 1]
            nf, n = recip(s, 1), recip(s, area)
            _, _, inv = squeeze_norm(0.0, sfc, s, sgb)
            gq = sgb[0:1] * inv * (dzf - all_valid(s) * (s_f + norm_all * g_f) * nf)
            gq_ref[...] = gq
            gp = exact(gq, wsq[...], ((1,), (1,))) * (1.0 / area)
            mask = mask_of(valid(s, 0), R, mid, edge)
            imgs = lax.broadcasted_iota(jnp.int32, (R, mid), 0)
            grow = lax.broadcasted_iota(jnp.int32, (ni, mid), 0)
            c, _ = me()
            mine = lax.axis_index("dp") * nc + c
            gpo = [colsum(jnp.where(grow == mine + b * ND, gp, 0.0)) for b in range(own)]
            gprow = gpo[0]
            for b in range(1, own):
                gprow = jnp.where(imgs >= b * span, gpo[b], gprow)
            lane = lax.broadcasted_iota(jnp.int32, (R, 2 * lw), 1)
            gss = []
            acts = []
            for r in range(2):
                def piece(j):
                    k = (r * 2 + j) * nb
                    return jnp.concatenate([merged[ni + k + i : ni + k + i + 1] for i in range(nb)], axis=1)

                s2v = piece(0) + colsum(gp * c1a[r])
                g2v = piece(1) + colsum(gp * c2a[r])
                sg2[0, r : r + 1] = s2v
                sg2[1, r : r + 1] = g2v
                norm, act, on, inv2 = second(spl, sums2, n, vec, r, mask)
                w = wts[r]
                wrow = w[0:1]
                for b in range(1, own):
                    wrow = jnp.where(imgs >= b * span, w[b : b + 1], wrow)
                dz = jnp.where(on, wrow * ga[...] + gprow, 0.0)
                gs = vec[r, 0:1] * inv2 * (dz - (s2v + norm * g2v) * n)
                gs = jnp.where(mask, gs, 0.0)
                gss.append(gs)
            for pair in range(nc // 2):
                cols = slice(pair * 2 * lw, (pair + 1) * 2 * lw)
                a, b = gss[0][:, cols], gss[1][:, cols]
                blk[2 * pair] = jnp.where(lane < lw, a, pltpu.roll(b, lw, 1))
                blk[2 * pair + 1] = jnp.where(lane < lw, pltpu.roll(a, lw, 1), b)
            for k, o in enumerate((b0, b1, b2, b3)):
                o[...] = blk[c ^ k]
            avg1, inv1, _ = stats(sums1, s)
            norm1 = (red[...] - avg1) * inv1
            on1 = (norm1 * vec[0, 3:4] + vec[1, 3:4] > 0) & mask
            for r in range(2):
                taps_in(gss[r], (zh,), own)
                acc = 0.0
                for t, (u, v) in enumerate(TAPS):
                    z = zh[2 - v, :, 2 - u : 2 - u + edge].reshape(R, mid)
                    acc += mm(z, w1[r, :, t * half : (t + 1) * half])
                cols = slice(r * half, (r + 1) * half)
                acc = jnp.where(on1[:, cols], acc, 0.0)
                dz1[:, cols] = acc
                sg1[0:1, cols] = colsum(acc)
                sg1[1:2, cols] = colsum(acc * norm1[:, cols])

        dz1, sg1, blk0, blk1, blk2, blk3, gq, sg2, gfc, wab = call(
            back_body,
            image_counts,
            [merged, c1_all, c2_all, normf_all, sfc, sgb, wsq, ga, spl, s2, vec, wts, red, s1, w1_home],
            [((R, mid), F32), ((2, mid), F32)]
            + [((R, 2 * lw), F32)] * 4
            + [((ni, inner), F32), ((2, 2, mid), F32), ((2, inner), F32), ((2, mid), F32)],
            [pltpu.VMEM((3, own, PAD, PAD, mid), BF16), pltpu.VMEM((nc, R, 2 * lw), F32)],
            flops=4 * R * nw * mid,
            far=(7, 13),
            far_out=(2,),
        )
        blks = [blk0, swap(blk1, "chan", 1), swap(blk2, "chan", 2), swap(blk3, "chan", 3)]
        sg1_steps = sum_steps(sg1)
        sg1 = sg1_steps[-1]
        dz1_r = gather3(after(dz1, sg1_steps[1]), sg1)

        gl_r = [l0, swap(after(l1, sg1_steps[0]), "chan", 1), swap(after(l2, sg1_steps[0]), "chan", 2), swap(after(l3, sg1_steps[0]), "chan", 3)]

        def early_body(s, a0, a1, a2, a3, hid, t1, t2, u1, sums, sg, eg, out):
            acc = 0.0
            base = lax.axis_index("dp") * nc
            for k, a in enumerate((a0, a1, a2, a3)):
                z = a[...]
                row = lax.broadcasted_iota(jnp.int32, (8, inner), 0)
                h = jnp.zeros((8, inner), F32)
                for b in range(own):
                    h = jnp.where(row == b, hid[pl.ds(base + (me()[0] ^ k) + b * ND, 1), :], h)
                acc += exact(z, h, ((0,), (0,)))
            avg, inv, n = stats(sums, s)
            outer = exact(u1[...], sg[0:1], ((0,), (0,)))
            z = (eg[0:1] * inv) * (t1[...] - (outer + t2[...] * sg[1:2]) * n)
            for i in range(lb):
                out[i * mid : (i + 1) * mid] = z[:, i * 128 : (i + 1) * 128]
            at = lb * mid
            out[at : at + 2 * lw] = acc

        (early,) = call(
            early_body,
            image_counts,
            gl_r + [hid_all, t1, t2, u1, s3l, sg3l, eg],
            [((lb * mid + 2 * lw, inner), F32)],
            far=(5, 6),
        )

        n_early, n_total = lb * mid + 2 * lw, padded_rows(lb * mid + 2 * lw + win * mid // 128)
        mb = mid // 128

        def dwr_body(s, d0, d1, d2, d3, red_g, x_ref, sums, sg, vec, early, *refs):
            outs, (go0, go1, go2, go3, scr, sent) = refs[:-6], refs[-6:]
            avg, inv, n = stats(sums, s)
            acc = 0.0
            for r, (dz, go) in enumerate(((d0, go0), (d1, go1), (d2, go2), (d3, go3))):
                mask = mask_of(valid(s, r), R, win, edge)
                norm = (red_g[me()[0] ^ CHAN_REL[r]] - avg) * inv
                g = vec[0, 3:4] * inv * (dz[...] - (sg[0:1] + norm * sg[1:2]) * n)
                g = jnp.where(mask, g, 0.0).astype(BF16)
                go[...] = g
                acc += mm(load_quarter(x_ref, scr, r, mask).astype(BF16), g, ((0,), (0,)))
            sent[0:n_early] = early[...]
            for i in range(mb):
                sent[n_early + i * win : n_early + (i + 1) * win] = acc[:, i * 128 : (i + 1) * 128]
            cut_chunks(sent, groups[0], outs)

        *sent, gr0, gr1, gr2, gr3 = call(
            dwr_body,
            image_counts,
            dz1_r + [red_g, feats, s1, sg1, vec, early],
            chunk_outs(n_total, groups[0]) + [((R, mid), BF16)] * 4,
            [quarter_scratch, pltpu.VMEM((n_total, 128), F32)],
            flops=8 * R * win * mid,
            far=(4, 5),
        )
        summed = big_sum_dp(image_counts, sent)
        grad_expand_weight = summed[: lb * mid].reshape(lb, mid, 128).transpose(1, 0, 2).reshape(mid, win)
        watt = summed[lb * mid : n_early]
        dwr = summed[n_early : n_early + mb * win]
        grad_reduce_weight = dwr.reshape(mb, win, 128).transpose(1, 0, 2).reshape(win, mid)

        def gin_body(s, g0, g1, g2, g3, b0, b1, b2, b3, go, w_ref, out_bo, out_gi, scr):
            w = w_ref[...].astype(BF16)
            for r, (g, b) in enumerate(((g0, b0), (g1, b1), (g2, b2), (g3, b3))):
                bo = b[...]
                z = mm(g[...], w, ((1,), (1,))) + load_quarter(go, scr, r, bo > 0)
                store_quarter(out_gi, scr, r, z)
                store_quarter(out_bo, scr, r, bo)

        block_out, grad_input = call(
            gin_body,
            image_counts,
            [gr0, gr1, gr2, gr3] + bos + [gouts, reduce_weight],
            [(feats.shape, F32)] * 2,
            [quarter_scratch],
            flops=8 * R * win * mid,
            far=(4, 5, 6, 7, 8, 9),
            far_out=(0, 1),
        )
        block_out, grad_input = from_native(block_out), from_native(grad_input)

        n_dws = padded_rows(9 * 2 * lw)

        def dws_body(s, k0, k1, k2, k3, red_g, sums, vec, *refs):
            outs, (zg, relu, out) = refs[:-3], refs[-3:]
            avg, inv, _ = stats(sums, s)
            for k, bk in enumerate((k0, k1, k2, k3)):
                mask = mask_of(valid(s, CHAN_REL[k]), R, mid, edge)
                z = jnp.maximum((red_g[me()[0] ^ k] - avg) * inv * vec[0, 3:4] + vec[1, 3:4], 0.0)
                relu[k * R : (k + 1) * R, :] = jnp.where(mask, z, 0.0).astype(BF16)
                taps_in(bk[...], (zg.at[:, k * own : (k + 1) * own],), own)
            taps = [zg[2 - v, :, 2 - u : 2 - u + edge].reshape(nc * R, 2 * lw) for u, v in TAPS]
            y = mm(relu[...], jnp.concatenate(taps, axis=1), ((0,), (0,)))
            lane = lax.broadcasted_iota(jnp.int32, (half, 2 * lw), 1)
            for t in range(9):
                cols = slice(t * 2 * lw, (t + 1) * 2 * lw)
                out[t * 2 * lw : (t + 1) * 2 * lw, :] = jnp.where(lane < lw, y[:half, cols], y[half:, cols]).T
            cut_chunks(out, groups[0], outs)

        dws = call(
            dws_body,
            image_counts,
            blks + [red_g, s1, vec],
            chunk_outs(n_dws, groups[0]),
            [pltpu.VMEM((3, slots, PAD, PAD, 2 * lw), BF16), pltpu.VMEM((nc * R, mid), BF16), pltpu.VMEM((n_dws, 128), F32)],
            flops=2 * nc * R * mid * 9 * 2 * lw,
            far=(0, 4),
        )
        dws = big_sum_dp(image_counts, dws)[: 9 * 2 * lw]
        grad_split_weight = dws.reshape(3, 3, 2, lw, half).transpose(0, 1, 4, 2, 3)

        def sq_body(s, pool, gq, out):
            out[...] = exact(pool[...], gq[...], ((0,), (0,)))

        (wsw,) = call(sq_body, image_counts, [pool_all, gq], [((mid, inner), F32)])

        def own_lanes(z, axis):
            return lax.dynamic_slice_in_dim(z, c * lw, lw, axis)

        return (
            block_out,
            grad_input,
            grad_reduce_weight,
            own_lanes(sg1[1], 0),
            own_lanes(sg1[0], 0),
            grad_split_weight,
            own_lanes(sg2[1], 1),
            own_lanes(sg2[0], 1),
            own_lanes(wsw, 0),
            gfc[0],
            gfc[1],
            watt.reshape(2, lw, inner).transpose(2, 0, 1),
            own_lanes(wab, 1),
            grad_expand_weight,
            sg3l[1],
            sg3l[0],
        )

    return per_device


def solution(mesh):
    in_specs = (
        P("dp", None, None, "chan"),
        P(),
        P("chan", None),
        P("chan"),
        P("chan"),
        P(None, None, None, None, "chan"),
        P(None, "chan"),
        P(None, "chan"),
        P("chan", None),
        P(),
        P(),
        P(None, None, "chan"),
        P(None, "chan"),
        P(None, "chan"),
        P("chan"),
        P("chan"),
        P("dp", None, None, "chan"),
    )
    out_specs = (
        P("dp", None, None, "chan"),
        P("dp", None, None, "chan"),
        P("chan", None),
        P("chan"),
        P("chan"),
        P(None, None, None, None, "chan"),
        P(None, "chan"),
        P(None, "chan"),
        P("chan", None),
        P(),
        P(),
        P(None, None, "chan"),
        P(None, "chan"),
        P(None, "chan"),
        P("chan"),
        P("chan"),
    )
    return jax.shard_map(
        build(mesh), mesh=mesh, in_specs=in_specs, out_specs=out_specs, check_vma=False
    )
```

```python
import functools

import jax
import jax.numpy as jnp
from jax import lax
from jax.experimental import pallas as pl
from jax.experimental.pallas import tpu as pltpu
from jax.sharding import PartitionSpec as P

EPSILON = 1e-05
F32, BF16 = jnp.float32, jnp.bfloat16
PAD = 16
VMEM_LIMIT = 32 * 1024 * 1024


def bits_of(n):
    out, k = [], 1
    while k < n:
        out.append(k)
        k *= 2
    return out


def split2(x):
    hi = x.astype(BF16)
    return hi, (x - hi.astype(F32)).astype(BF16)


def mm(a, b, dims=((1,), (0,))):
    return lax.dot_general(a, b, (dims, ((), ())), preferred_element_type=F32)


def split3(x):
    hi = x.astype(BF16)
    x = x - hi.astype(F32)
    mid = x.astype(BF16)
    return hi, mid, (x - mid.astype(F32)).astype(BF16)


def mm3(a, b, dims=((1,), (0,))):
    return mm(a[0], b[0], dims) + (mm(a[0], b[1], dims) + mm(a[1], b[0], dims))


def mm6(a, b, dims=((1,), (0,))):
    small = mm(a[0], b[2], dims) + mm(a[2], b[0], dims) + mm(a[1], b[1], dims)
    return mm(a[0], b[0], dims) + (mm(a[0], b[1], dims) + mm(a[1], b[0], dims) + small)


def exact(a, b, dims=((1,), (0,))):
    return lax.dot_general(
        a, b, (dims, ((), ())), precision=lax.Precision.HIGHEST, preferred_element_type=F32
    )


def call(body, counts, ins, outs, scratch=(), flops=0, far=(), far_out=(), lazy=False):
    cuts = far if isinstance(far, dict) else {k: None for k in far}
    far, far_out = sorted(cuts), sorted(far_out)
    moved = sum(a.size * a.dtype.itemsize for a in ins) + sum(
        int(jnp.dtype(d).itemsize) * functools.reduce(lambda x, y: x * y, s, 1) for s, d in outs
    )
    vmem, hbm = pl.BlockSpec(memory_space=pltpu.VMEM), pl.BlockSpec(memory_space=pltpu.HBM)
    own_scratch = len(scratch)
    def shape_of(k):
        shape, part = ins[k].shape, cuts[k]
        return shape if part is None else shape[:1] + (part.stop - part.start,) + shape[2:]

    held = [pltpu.VMEM(shape_of(k), ins[k].dtype) for k in far] + [pltpu.VMEM(*outs[k]) for k in far_out]
    sems = [pltpu.SemaphoreType.DMA] * len(held)

    def kernel(s, *refs):
        n, m = len(ins), len(outs)
        refs_in, refs_out = list(refs[:n]), list(refs[n : n + m])
        rest = refs[n + m :]
        scr, bufs, sem = rest[:own_scratch], rest[own_scratch : own_scratch + len(held)], rest[own_scratch + len(held) :]
        copies = []
        for i, k in enumerate(far):
            part = cuts[k]
            src = refs_in[k] if part is None else refs_in[k].at[:, part.start : part.stop, :]
            copies.append(pltpu.make_async_copy(src, bufs[i], sem[i]))
            copies[-1].start()
            refs_in[k] = bufs[i]
        homes = []
        for i, k in enumerate(far_out):
            i += len(far)
            homes.append(pltpu.make_async_copy(bufs[i], refs_out[k], sem[i]))
            refs_out[k] = bufs[i]
        if lazy:
            body(s, *refs_in, *refs_out, *scr, arrive=lambda k: copies[far.index(k)].wait())
        else:
            for copy in copies:
                copy.wait()
            body(s, *refs_in, *refs_out, *scr)
        for copy in homes:
            copy.start()
        for copy in homes:
            copy.wait()

    ins = [pltpu.with_memory_space_constraint(a, pltpu.HBM) if k in far else a for k, a in enumerate(ins)]
    return pl.pallas_call(
        kernel,
        out_shape=[pltpu.HBM(s, d) if k in far_out else jax.ShapeDtypeStruct(s, d) for k, (s, d) in enumerate(outs)],
        in_specs=[pl.BlockSpec(memory_space=pltpu.SMEM)] + [hbm if k in far else vmem for k in range(len(ins))],
        out_specs=[hbm if k in far_out else vmem for k in range(len(outs))],
        scratch_shapes=list(scratch) + held + sems,
        compiler_params=pltpu.CompilerParams(vmem_limit_bytes=VMEM_LIMIT),
        cost_estimate=pl.CostEstimate(flops=flops, bytes_accessed=moved, transcendentals=0),
    )(counts, *ins)


def mask_of(nv, rows, cols, edge):
    r = lax.broadcasted_iota(jnp.int32, (rows, cols), 0)
    return ((r & (PAD - 1)) < edge) & (r < nv * (edge * PAD))


def colsum(x):
    return jnp.sum(x, axis=0, keepdims=True)


def build(mesh):
    nd, nc = mesh.shape["dp"], mesh.shape["chan"]
    both = ("dp", "chan")
    cbits, dbits = bits_of(nc), bits_of(nd)
    flat_bits = bits_of(nd * nc)
    pairs = [flat_bits[i : i + 2] for i in range(1, len(flat_bits), 2)]
    sum_groups = [[1]] + [[k | 1 for k in ([p[0], p[1], p[0] ^ p[1]] if len(p) == 2 else p)] for p in pairs[::-1]]

    def swap(x, axis, k):
        n = {"dp": nd, "chan": nc}[axis] if isinstance(axis, str) else nd * nc
        return lax.ppermute(x, axis, [(i, i ^ k) for i in range(n)])

    def after(x, *deps):
        return lax.optimization_barrier((x,) + deps)[0]

    def sum_steps(x, before_last=()):
        out = [x]
        for i, g in enumerate(sum_groups):
            x = out[-1]
            if before_last and i == len(sum_groups) - 1:
                x = after(x, *before_last)
            got = [swap(x, both, k) for k in g]
            x = x + got[0]
            out.append(x + (got[1] + got[2]) if len(g) == 3 else x)
        return out

    def sum_all(x):
        return sum_steps(x)[-1]

    def pick(x, i):
        return lax.dynamic_index_in_dim(x, i, 0, False)

    groups = [dbits[:1]] + [dbits[i : i + 2] for i in range(1, len(dbits), 2)]

    def masks(g):
        out = [0]
        for k in g:
            out = out + [m ^ k for m in out]
        return out

    def place_in(g):
        n = 2 ** len(g)
        return (lax.axis_index("dp") // g[0]) % n, n

    def cut_chunks(scr, g, outs):
        at, n = place_in(g)
        rows = scr.shape[0] // n
        for m, o in enumerate(outs):
            o[...] = scr[pl.ds(pl.multiple_of((at ^ m) * rows, 8), rows), :]

    def chunk_outs(rows, g):
        n = 2 ** len(g)
        return [((rows // n, 128), F32)] * n

    def padded_rows(rows):
        return -(-rows // (8 * nd)) * 8 * nd

    def sum_dp(counts, chunks, write, outs, before=()):
        stages = []

        def exchanged(first, rest, g):
            got = [first] + [swap(z, "dp", m) for z, m in zip(rest, masks(g)[1:])]
            k = len(stages)
            if k < len(before) and before[k]:
                got[0] = after(got[0], *before[k])
            return got

        for i, g in enumerate(groups):
            got = exchanged(chunks[0], chunks[1:], g)
            rows = got[0].shape[0]
            last = i == len(groups) - 1

            def add_body(s, *refs, n=len(got), last=last, i=i):
                v = refs[0][...]
                for z in refs[1:n]:
                    v = v + z[...]
                if last:
                    refs[n][...] = v
                else:
                    refs[-1][...] = v
                    cut_chunks(refs[-1], groups[i + 1], refs[n:-1])

            chunks = call(
                add_body,
                counts,
                got,
                [((rows, 128), F32)] if last else chunk_outs(rows, groups[i + 1]),
                [] if last else [pltpu.VMEM((rows, 128), F32)],
            )
            stages.append(chunks[0])
        (x,) = chunks
        for g in groups[::-1]:
            got = exchanged(x, [x] * (2 ** len(g) - 1), g)
            rows = x.shape[0]
            last = g is groups[0]

            def join_body(s, *refs, n=len(got), g=g, rows=rows, last=last):
                at, _ = place_in(g)
                for m, z in enumerate(refs[:n]):
                    refs[-1][pl.ds(pl.multiple_of((at ^ m) * rows, 8), rows), :] = z[...]
                if last:
                    write(refs[-1], *refs[n:-1])

            whole = ((rows * len(got), 128), F32)
            if last:
                return call(join_body, counts, got, outs, [pltpu.VMEM(*whole)])
            (x,) = call(join_body, counts, got, [whole])
            stages.append(x)

    def quarter_of(chan):
        q = chan * 0
        for k in cbits:
            q = q * 2 + (chan // k) % 2
        return q

    def per_device(
        features_in,
        image_counts,
        reduce_weight,
        reduce_gain,
        reduce_shift,
        split_weight,
        split_gain,
        split_shift,
        squeeze_weight,
        squeeze_gain,
        squeeze_shift,
        attend_weight,
        attend_bias,
        expand_weight,
        expand_gain,
        expand_shift,
        grad_out,
    ):
        slots, edge = features_in.shape[0], features_in.shape[1]
        area = edge * edge
        win = features_in.shape[3]
        mid = reduce_weight.shape[1]
        half = mid // 2
        lw = split_weight.shape[4]
        inner = squeeze_gain.shape[0]
        own = slots // nc
        span = edge * PAD
        R = own * span
        ni = nd * slots
        c = lax.axis_index("chan")

        def me():
            c = lax.axis_index("chan")
            return c, quarter_of(c)

        def valid(s, r):
            return jnp.clip(s[lax.axis_index("dp")] - (me()[1] ^ r) * own, 0, own)

        def recip(s, each):
            total = s[0]
            for i in range(1, nd):
                total = total + s[i]
            return (1.0 / (jnp.full((1, 128), total, jnp.int32).astype(F32) * each))[:, 0:1]

        TAPS = [(u, v) for u in range(3) for v in range(3)]

        def stats(sum_ref, s):
            n = recip(s, area)
            avg = sum_ref[0:1] * n
            inv = lax.rsqrt(sum_ref[1:2] * n - avg * avg + EPSILON)
            return avg, inv, n

        lb = win // 128

        def native(x):
            x = x.transpose(1, 2, 0, 3).reshape(area, slots, lb, 128)
            return x.transpose(0, 2, 1, 3).reshape(area * lb * slots, 128)

        def from_native(z):
            z = z.reshape(area, lb, slots, 128).transpose(0, 2, 1, 3)
            return z.reshape(edge, edge, slots, win).transpose(2, 0, 1, 3)

        def place_of(h, i, b, r):
            at = (h * edge * lb + i) * slots + (me()[1] ^ r) * own + b
            return pl.ds(at, edge, stride=lb * slots)

        def load_quarter(ref, scr, r, mask):
            for b in range(own):
                for h in range(edge):
                    for i in range(lb):
                        scr[b * edge + h, :edge, i * 128 : (i + 1) * 128] = ref[place_of(h, i, b, r), :]
            return jnp.where(mask, scr[...].reshape(R, win), 0.0)

        def store_quarter(ref, scr, r, z):
            scr[...] = z.reshape(own * edge, PAD, win)
            for b in range(own):
                for h in range(edge):
                    for i in range(lb):
                        ref[place_of(h, i, b, r), :] = scr[b * edge + h, :edge, i * 128 : (i + 1) * 128]

        def mine_of(ref):
            c, out = me()[0], ref[0:2]
            for k in range(1, nc):
                out = jnp.where(c == k, ref[2 * k : 2 * k + 2], out)
            return out

        feats, gouts = native(features_in), native(grad_out)
        quarter_scratch = pltpu.VMEM((own * edge, PAD, win), F32)

        wt = split_weight.transpose(0, 1, 3, 4, 2).reshape(-1, half)


        def pack(rg, rs, sg, ss, ab, eg):
            return jnp.concatenate(
                [
                    sg.reshape(1, -1),
                    ss.reshape(1, -1),
                    ab.reshape(1, -1),
                    jnp.concatenate([rg, rs])[None],
                    eg.reshape(-1, 2 * lw),
                    jnp.zeros((8 - 4 - win // (2 * lw), 2 * lw), F32),
                ]
            )

        nw = 9 * half

        def reduce_body(rels, s, x_ref, w_ref, *refs):
            n, scr = len(rels), refs[-1]
            w = split3(w_ref[...])
            for k, r in enumerate(rels):
                x = split3(load_quarter(x_ref, scr, r, mask_of(valid(s, r), R, win, edge)))
                refs[n + k][...] = x[0]
                refs[k][...] = mm6(x, w)

        def reduce_call(rels, feats=feats):
            return call(
                functools.partial(reduce_body, rels),
                image_counts,
                [feats, reduce_weight],
                [((R, mid), F32)] * len(rels) + [((R, win), BF16)] * len(rels),
                [quarter_scratch],
                flops=12 * R * win * mid * len(rels),
                far=(0, 1),
                far_out=(len(rels), len(rels) + 1),
            )

        p3, p1, x3, x1 = reduce_call((3, 1))
        p2, p0, x2, x0 = reduce_call((2, 0))
        y1 = p1 + swap(p3, "chan", 1)
        ys = swap(y1, "chan", 2)
        rc = swap(p2, "chan", 1)

        def gather3(x, gate=None):
            y = swap(x, "chan", 2)
            return [x, y, swap(x, "chan", 1), swap(y if gate is None else after(y, gate), "chan", 1)]

        small = lax.optimization_barrier(
            (y1, reduce_gain, reduce_shift, split_gain, split_shift, attend_bias, expand_gain)
        )
        ps = pack(*small[1:])

        wt_y = swap(after(wt, ys), "chan", 2)
        wt_r = [wt, wt_y, swap(wt, "chan", 1), swap(wt_y, "chan", 1)]

        small = lax.optimization_barrier((y1, expand_weight, attend_weight, squeeze_weight))
        pw = jnp.concatenate(
            [small[1][:, i * 128 : (i + 1) * 128] for i in range(lb)]
            + [small[2].transpose(1, 2, 0).reshape(2 * lw, inner), small[3]]
        )
        CHAN_REL = (0, 2, 1, 3)

        nl = mid // 128

        def red_body(s, a, b, y, ps, red, sums):
            v = a[...] + b[...] + y[...]
            red[...] = v
            sums[...] = jnp.zeros((8 + 8 * nc, 128), F32)
            for k, z in enumerate((colsum(v), colsum(v * v))):
                for i in range(nl):
                    sums[k * nl + i : k * nl + i + 1, :] = z[:, i * 128 : (i + 1) * 128]
            sums[pl.ds(pl.multiple_of(8 + 8 * me()[0], 8), 8), :] = ps[...]

        red, s1 = call(red_body, image_counts, [p0, rc, ys, ps], [((R, mid), F32), ((8 + 8 * nc, 128), F32)])
        s1_steps = sum_steps(s1, (wt_y,))

        def vec_body(s, sums, s1, vec, g3):
            for k in range(2):
                for i in range(nl):
                    s1[k : k + 1, i * 128 : (i + 1) * 128] = sums[k * nl + i : k * nl + i + 1, :]
            own_of = [sums[8 + 8 * k : 16 + 8 * k, :] * (1.0 / nd) for k in range(nc)]
            lane = lax.broadcasted_iota(jnp.int32, (8, 2 * lw), 1)
            for pair in range(nc // 2):
                a, b = own_of[2 * pair], own_of[2 * pair + 1]
                cols = slice(pair * 2 * lw, (pair + 1) * 2 * lw)
                vec[0, :, cols] = jnp.where(lane < lw, a, pltpu.roll(b, lw, 1))
                vec[1, :, cols] = jnp.where(lane < lw, pltpu.roll(a, lw, 1), b)
            g3[...] = jnp.zeros((8, win), F32)
            for k in range(nc):
                for i in range(win // (2 * lw)):
                    g3[k : k + 1, i * 2 * lw : (i + 1) * 2 * lw] = own_of[k][4 + i : 5 + i, :]

        s1, vec, g3 = call(
            vec_body, image_counts, [s1_steps[-1]], [((2, mid), F32), ((2, 8, mid), F32), ((8, win), F32)]
        )

        pw_all = lax.all_gather(after(pw, s1_steps[-2], wt_y), "chan")
        WE = slice(0, lb * mid)
        WAT = slice(lb * mid, lb * mid + 2 * lw)
        WSQ = slice(lb * mid + 2 * lw, lb * mid + 3 * lw)

        def we_of(ref, k):
            return jnp.concatenate([ref[k, i * mid : (i + 1) * mid, :] for i in range(lb)], axis=1)

        def wat_of(ref, r):
            return jnp.concatenate([ref[k, r * lw : (r + 1) * lw, :] for k in range(nc)], axis=0)

        def wsq_of(ref):
            return ref[...].reshape(mid, inner)

        def taps_in(z, scrs, n):
            w = z.shape[1]
            rows = n * span
            for v in range(3):
                zz = z if v == 1 else pltpu.roll(z, 1 if v == 0 else rows - 1, 0)
                parts = split2(zz) if len(scrs) == 2 else [zz.astype(BF16)]
                for scr, part in zip(scrs, parts):
                    scr[v, :, 0] = jnp.zeros((n, PAD, w), BF16)
                    scr[v, :, edge + 1] = jnp.zeros((n, PAD, w), BF16)
                    scr[v, :, 1 : edge + 1] = part.reshape(n, edge, PAD, w)

        def conv_body(s, red, sums, vec, v0, v1, v2, v3, out, sums2, w1, za, zb, w2, arrive):
            avg, inv, _ = stats(sums, s)
            mask = mask_of(valid(s, 0), R, mid, edge)
            z = jnp.maximum((red[...] - avg) * inv * vec[0, 3:4] + vec[1, 3:4], 0.0)
            z = jnp.where(mask, z, 0.0)
            taps_in(z, (za, zb), own)
            for rel, ref in enumerate((v0, v1, v2, v3)):
                arrive(3 + rel)
                rows = pl.ds(pl.multiple_of((me()[0] ^ CHAN_REL[rel]) * lw, lw), lw)
                for t in range(9):
                    for r in range(2):
                        at = t * 2 * lw + r * lw
                        for o, z in zip((w1, w2), split2(ref[at : at + lw, :])):
                            o[r, rows, t * half : (t + 1) * half] = z
            for r in range(2):
                cols = slice(r * half, (r + 1) * half)
                lhs = [
                    jnp.concatenate([z[v, :, u : u + edge, :, cols].reshape(R, half) for u, v in TAPS], axis=1)
                    for z in (za, zb)
                ]
                y = mm3(lhs, (w1[r], w2[r]), ((1,), (1,)))
                out[:, r * mid : (r + 1) * mid] = y
                y = jnp.where(mask, y, 0.0)
                sums2[0:1, r * mid : (r + 1) * mid] = colsum(y)
                sums2[1:2, r * mid : (r + 1) * mid] = colsum(y * y)

        spl, s2, w1 = call(
            conv_body,
            image_counts,
            [red, s1, vec] + wt_r,
            [((R, 2 * mid), F32), ((2, 2 * mid), F32), ((2, mid, nw), BF16)],
            [pltpu.VMEM((3, own, PAD, PAD, mid), BF16)] * 2 + [pltpu.VMEM((2, mid, nw), BF16)],
            flops=12 * R * nw * mid,
            far=(3, 4, 5, 6),
            far_out=(2,),
            lazy=True,
        )

        s2_steps = sum_steps(s2)
        s2 = s2_steps[-1]

        def second(spl, sums, n, vec, r, mask):
            cols = slice(r * mid, (r + 1) * mid)
            avg = sums[0:1, cols] * n
            inv = lax.rsqrt(sums[1:2, cols] * n - avg * avg + EPSILON)
            norm = (spl[:, cols] - avg) * inv
            act = norm * vec[r, 0:1] + vec[r, 1:2]
            return norm, act, (act > 0) & mask, inv

        def per_image(z):
            return [colsum(z[b * span : (b + 1) * span]) for b in range(own)]

        nb = mid // 128
        BLOCK = max(64, 4 * nb * own)
        ND = nd * nc

        def pool_body(s, spl, sums, vec, wsq, c12, sq, sfc, arrive):
            mask = mask_of(valid(s, 0), R, mid, edge)
            n = recip(s, area)
            pooled = [0.0] * own
            c12[...] = jnp.zeros((BLOCK, 128), F32)
            for r in range(2):
                norm, act, on, _ = second(spl, sums, n, vec, r, mask)
                c1 = per_image(jnp.where(on, 1.0, 0.0))
                c2 = per_image(jnp.where(on, norm, 0.0))
                for b in range(own):
                    for i in range(nb):
                        sl = slice(i * 128, (i + 1) * 128)
                        for k, z in ((r * nb + i, c1), ((2 + r) * nb + i, c2)):
                            c12[k * own + b : k * own + b + 1, :] = z[b][:, sl]
                    pooled[b] = pooled[b] + vec[r, 0:1] * c2[b] + vec[r, 1:2] * c1[b]
            p = jnp.concatenate(pooled + [jnp.zeros((8 - own, mid), F32)], axis=0) * (1.0 / area)
            arrive(3)
            v = exact(p, wsq_of(wsq))
            sq[...] = v
            live = lax.broadcasted_iota(jnp.int32, (8, inner), 0) < valid(s, 0)
            v = jnp.where(live, v, 0.0)
            sfc[0:1] = colsum(v)
            sfc[1:2] = colsum(v * v)

        c12, sq, sfc = call(
            pool_body,
            image_counts,
            [spl, s2, vec, pw_all],
            [((BLOCK, 128), F32), ((8, inner), F32), ((2, inner), F32)],
            far={3: WSQ},
            lazy=True,
        )
        c12_g = lax.all_gather(c12, both, axis=0, tiled=True)
        sfc = sum_all(sfc)
        red_g = lax.all_gather(after(red, sfc), "chan")
        sgb = jnp.stack([squeeze_gain, squeeze_shift])

        def squeeze_norm(sq, sums, s, sgb):
            n = recip(s, 1)
            avg = sums[0:1] * n
            inv = lax.rsqrt(sums[1:2] * n - avg * avg + EPSILON)
            norm = (sq - avg) * inv
            return norm, norm * sgb[0:1] + sgb[1:2], inv

        def attend_body(s, spl, sums, vec, sfc, sq, sgb, wat, att, wts, arrive):
            mask = mask_of(valid(s, 0), R, mid, edge)
            n = recip(s, area)
            _, actf, _ = squeeze_norm(sq[...], sfc, s, sgb)
            hidden = jnp.maximum(actf, 0.0)
            halves = [second(spl, sums, n, vec, r, mask) for r in range(2)]
            arrive(6)
            lg = [exact(hidden, wat_of(wat, r), ((1,), (1,))) + vec[r, 2:3] for r in range(2)]
            top = jnp.maximum(lg[0], lg[1])
            e = [jnp.exp(z - top) for z in lg]
            total = e[0] + e[1]
            acc = 0.0
            imgs = lax.broadcasted_iota(jnp.int32, (R, mid), 0)
            for r in range(2):
                w = e[r] / total
                wts[r] = w
                _, act, on, _ = halves[r]
                wrow = w[0:1]
                for b in range(1, own):
                    wrow = jnp.where(imgs >= b * span, w[b : b + 1], wrow)
                acc = acc + jnp.where(on, act * wrow, 0.0)
            att[...] = acc

        att, wts = call(
            attend_body,
            image_counts,
            [spl, s2, vec, sfc, sq, sgb, pw_all],
            [((R, mid), F32), ((2, 8, mid), F32)],
            far={6: WAT},
            lazy=True,
        )

        def own_expand_body(s, att, we, sums):
            a = split2(att[...])
            for k in range(nc):
                y = mm3(a, split2(we_of(we, k)))
                sums[2 * k : 2 * k + 1] = colsum(y)
                sums[2 * k + 1 : 2 * k + 2] = colsum(y * y)

        (s3,) = call(
            own_expand_body, image_counts, [att, pw_all], [((2 * nc, win), F32)], flops=6 * R * mid * win * nc, far={1: WE}
        )
        att_y = swap(att, "chan", 2)
        s3_steps = sum_steps(s3, (att_y,))
        s3 = s3_steps[-1]
        att_r = [att, att_y, swap(att, "chan", 1), swap(after(att_y, s3_steps[-2]), "chan", 1)]
        eg = jnp.stack([expand_gain, expand_shift])

        def expand_body(rels, extra, s, *refs, arrive):
            n = len(rels)
            atts, (x_ref, g_ref, w_ref, sums, eg) = refs[:n], refs[n : n + 5]
            prev, refs = refs[n + 5 : n + 5 + extra], refs[n + 5 + extra :]
            bos, gas = refs[:n], refs[n : 2 * n]
            sg, t1, t2, u1, scr = refs[2 * n :]
            avg, inv, _ = stats(mine_of(sums), s)
            arrive(n + 2)
            w = split2(w_ref[...])
            sg_acc, t1_acc, t2_acc, u_acc = [0.0, 0.0], 0.0, 0.0, 0.0
            for k, r in enumerate(rels):
                mask = mask_of(valid(s, r), R, win, edge)
                a = atts[k][...]
                ap = split2(a)
                norm = (mm3(ap, w) - avg) * inv
                if k == 0:
                    arrive(n)
                x = load_quarter(x_ref, scr, r, mask)
                pre = norm * eg[0:1] + eg[1:2] + x
                on = (pre > 0) & mask
                bos[k][...] = jnp.where(on, pre, 0.0)
                if k == 0:
                    arrive(n + 1)
                g = load_quarter(g_ref, scr, r, on)
                sg_acc[0] += colsum(g)
                sg_acc[1] += colsum(g * norm)
                gb = g.astype(BF16)
                nb = jnp.where(mask, norm, 0.0).astype(BF16)
                gas[k][...] = mm((g * (eg[0:1] * inv)).astype(BF16), w[0], ((1,), (1,)))
                t = mm(ap[0], jnp.concatenate([gb, nb], axis=1), ((0,), (0,)))
                t1_acc += t[:, :win]
                t2_acc += t[:, win:]
                u_acc += colsum(a)
            row = lax.broadcasted_iota(jnp.int32, (2 * nc, win), 0)
            c, _ = me()
            z = jnp.where(row == 2 * c, sg_acc[0], 0.0)
            sg[...] = jnp.where(row == 2 * c + 1, sg_acc[1], z)
            for o, z, p in zip((t1, t2, u1), (t1_acc, t2_acc, u_acc), prev[1:] or (None,) * 3):
                o[...] = z if p is None else z + p[...]
            if prev:
                sg[...] = sg[...] + prev[0][...]

        def expand_call(rels, prev):
            n = len(rels)
            return call(
                functools.partial(expand_body, rels, len(prev)),
                image_counts,
                [att_r[r] for r in rels] + [feats, gouts, expand_weight, s3, eg] + prev,
                [((R, win), F32)] * n
                + [((R, mid), F32)] * n
                + [((2 * nc, win), F32), ((mid, win), F32), ((mid, win), F32), ((1, mid), F32)],
                [quarter_scratch],
                flops=12 * R * mid * win * n,
                far=(n, n + 1, n + 2),
                far_out=tuple(range(n)) + ((2 * n + 1, 2 * n + 2) if prev else ()),
                lazy=True,
            )

        bo3, bo1, ga3, ga1, *prev = expand_call((3, 1), [])
        gy1 = ga1 + swap(ga3, "chan", 1)
        bo2, bo0, ga2, ga0, sg3, t1, t2, u1 = expand_call((2, 0), [after(prev[0], gy1)] + list(prev[1:]))
        gys = swap(gy1, "chan", 2)
        grc = swap(ga2, "chan", 1)
        sg3 = sum_steps(sg3, (gys,))[-1]
        bos = [bo0, bo1, bo2, bo3]

        def gatt_body(s, p, rc, ys, att, we, g3, sums, sg, spl, sums2, vec, wts, sfc, sq, sgb, wat, ga, l0, l1, l2, l3, merged, scr):
            m_acc, v_acc = 0.0, 0.0
            n = recip(s, area)
            for k in range(nc):
                avg = sums[2 * k : 2 * k + 1] * n
                inv = lax.rsqrt(sums[2 * k + 1 : 2 * k + 2] * n - avg * avg + EPSILON)
                sc = g3[k : k + 1] * inv * n
                kap = sg[2 * k + 1 : 2 * k + 2] * inv * sc
                w = we_of(we, k)
                wb = w.astype(BF16)
                m_acc += mm((w * kap).astype(BF16), wb, ((1,), (1,)))
                vv = sg[2 * k : 2 * k + 1] * sc - avg * kap
                row = lax.broadcasted_iota(jnp.int32, (16, win), 0)
                high = jnp.where(row == 0, vv, 0.0)
                low = jnp.where(row == 1, vv - vv.astype(BF16).astype(F32), 0.0)
                v_acc += colsum(mm((high + low).astype(BF16), wb, ((1,), (1,))))
            mask = mask_of(valid(s, 0), R, mid, edge)
            g = p[...] + rc[...] + ys[...] - mm(att[...].astype(BF16), m_acc.astype(BF16)) - v_acc
            g = jnp.where(mask, g, 0.0)
            ga[...] = g
            gw, a12 = [], []
            for r in range(2):
                norm, act, on, _ = second(spl, sums2, n, vec, r, mask)
                gon = jnp.where(on, g, 0.0)
                a1, a2 = per_image(gon), per_image(gon * norm)
                zero = [jnp.zeros((8 - own, mid), F32)]
                a1, a2 = jnp.concatenate(a1 + zero, axis=0), jnp.concatenate(a2 + zero, axis=0)
                a12.append((a1, a2))
                gw.append(vec[r, 0:1] * a2 + vec[r, 1:2] * a1)
            mean = wts[0] * gw[0] + wts[1] * gw[1]
            gh = 0.0
            parts, zs = [], []
            for r in range(2):
                z = wts[r] * (gw[r] - mean)
                zs.append(z)
                gh = gh + exact(z, wat_of(wat, r))
                for j in range(2):
                    parts.append(colsum(wts[r] * a12[r][j]))
            parts += [colsum(z) for z in zs]
            _, actf, _ = squeeze_norm(sq[...], sfc, s, sgb)
            dzf = jnp.where(actf > 0, gh, 0.0)
            c, _ = me()
            row = lax.broadcasted_iota(jnp.int32, (ni, inner), 0)
            z = jnp.zeros((ni, inner), F32)
            for b in range(own):
                z = jnp.where(row == lax.axis_index("dp") * nc + c + b * ND, dzf[b : b + 1], z)
            merged[0:ni] = z
            lane = lax.broadcasted_iota(jnp.int32, (8, 2 * lw), 1)
            for pair in range(nc // 2):
                cols = slice(pair * 2 * lw, (pair + 1) * 2 * lw)
                a, b = zs[0][:, cols], zs[1][:, cols]
                scr[2 * pair] = jnp.where(lane < lw, a, pltpu.roll(b, lw, 1))
                scr[2 * pair + 1] = jnp.where(lane < lw, pltpu.roll(a, lw, 1), b)
            for k, o in enumerate((l0, l1, l2, l3)):
                o[...] = scr[c ^ k]
            merged[ni:] = jnp.zeros((6 * nb + 4, inner), F32)
            for k, pz in enumerate(parts):
                for i in range(nb):
                    merged[ni + k * nb + i : ni + k * nb + i + 1] = pz[:, i * 128 : (i + 1) * 128]

        ga, l0, l1, l2, l3, merged = call(
            gatt_body,
            image_counts,
            [ga0, grc, gys, att, pw_all, g3, s3, sg3, spl, s2, vec, wts, sfc, sq, sgb, pw_all],
            [((R, mid), F32)] + [((8, 2 * lw), F32)] * 4 + [((ni + 6 * nb + 4, inner), F32)],
            [pltpu.VMEM((nc, 8, 2 * lw), F32)],
            flops=2 * R * mid * mid + 2 * nc * mid * mid * win,
            far={4: WE, 15: WAT},
            far_out=(0,),
        )

        used = 4 * nb * own

        def all_body(s, g, vec, wsq, sfc, sgb, c1_ref, c2_ref, pool_ref, norm_ref, hid_ref):
            g = g.reshape(ND * used, 128)

            def rows(k):
                return jnp.concatenate([g[pl.ds(k * own + b, ND, stride=used), :] for b in range(own)], axis=0)

            pooled = 0.0
            for r in range(2):
                c1 = jnp.concatenate([rows(r * nb + i) for i in range(nb)], axis=1)
                c2 = jnp.concatenate([rows((2 + r) * nb + i) for i in range(nb)], axis=1)
                c1_ref[r] = c1
                c2_ref[r] = c2
                pooled = pooled + vec[r, 0:1] * c2 + vec[r, 1:2] * c1
            pooled = pooled * (1.0 / area)
            pool_ref[...] = pooled
            norm, actf, _ = squeeze_norm(exact(pooled, wsq_of(wsq)), sfc, s, sgb)
            norm_ref[...] = norm
            hid_ref[...] = jnp.maximum(actf, 0.0)

        c1_all, c2_all, pool_all, normf_all, hid_all = call(
            all_body,
            image_counts,
            [c12_g.reshape(ND, BLOCK, 128), vec, pw_all, sfc, sgb],
            [
                ((2, ni, mid), F32),
                ((2, ni, mid), F32),
                ((ni, mid), F32),
                ((ni, inner), F32),
                ((ni, inner), F32),
            ],
            far={0: slice(0, used), 2: WSQ},
        )
        for k, g in enumerate(sum_groups):
            got = [swap(merged, both, m) for m in g]
            z = merged + got[0]
            merged = z + (got[1] + got[2]) if len(g) == 3 else z
            if k == 1:
                merged, c1_all = lax.optimization_barrier((merged, c1_all))

        def all_valid(s):
            row = lax.broadcasted_iota(jnp.int32, (ni, inner), 0)
            dev = row & (ND - 1)
            at, chan = dev >> (nc.bit_length() - 1), dev & (nc - 1)
            slot = (row >> (ND.bit_length() - 1)) + own * sum(
                ((chan >> i) & 1) * (nc >> (i + 1)) for i in range(len(cbits))
            )
            live = jnp.zeros((ni, inner), jnp.int32)
            for i in range(nd):
                live = jnp.where(at == i, s[i], live)
            return jnp.where(slot < live, 1.0, 0.0)

        def back_body(
            s, merged, c1a, c2a, normf, sfc, sgb, wsq, ga, spl, sums2, vec, wts, l0, l1, l2, l3,
            gs_ref, b0, b1, b2, b3, gq_ref, sg2, gfc, wab, blk, arrive,
        ):
            dzf = merged[0:ni]
            norm_all = normf[...]
            s_f = colsum(dzf)
            g_f = colsum(dzf * norm_all)
            gfc[0:1] = g_f
            gfc[1:2] = s_f
            for r in range(2):
                for i in range(nb):
                    k = ni + (4 + r) * nb + i
                    wab[r : r + 1, i * 128 : (i + 1) * 128] = merged[k : k + 1]
            nf, n = recip(s, 1), recip(s, area)
            _, _, inv = squeeze_norm(0.0, sfc, s, sgb)
            gq = sgb[0:1] * inv * (dzf - all_valid(s) * (s_f + norm_all * g_f) * nf)
            gq_ref[...] = gq
            arrive(6)
            gp = exact(gq, wsq_of(wsq), ((1,), (1,))) * (1.0 / area)
            mask = mask_of(valid(s, 0), R, mid, edge)
            imgs = lax.broadcasted_iota(jnp.int32, (R, mid), 0)
            grow = lax.broadcasted_iota(jnp.int32, (ni, mid), 0)
            c, _ = me()
            mine = lax.axis_index("dp") * nc + c
            gpo = [colsum(jnp.where(grow == mine + b * ND, gp, 0.0)) for b in range(own)]
            gprow = gpo[0]
            for b in range(1, own):
                gprow = jnp.where(imgs >= b * span, gpo[b], gprow)
            lane = lax.broadcasted_iota(jnp.int32, (R, 2 * lw), 1)
            gss = []
            acts = []
            for r in range(2):
                def piece(j):
                    k = (r * 2 + j) * nb
                    return jnp.concatenate([merged[ni + k + i : ni + k + i + 1] for i in range(nb)], axis=1)

                s2v = piece(0) + colsum(gp * c1a[r])
                g2v = piece(1) + colsum(gp * c2a[r])
                sg2[0, r : r + 1] = s2v
                sg2[1, r : r + 1] = g2v
                norm, act, on, inv2 = second(spl, sums2, n, vec, r, mask)
                w = wts[r]
                wrow = w[0:1]
                for b in range(1, own):
                    wrow = jnp.where(imgs >= b * span, w[b : b + 1], wrow)
                if r == 0:
                    arrive(7)
                dz = jnp.where(on, wrow * ga[...] + gprow, 0.0)
                gs = vec[r, 0:1] * inv2 * (dz - (s2v + norm * g2v) * n)
                gs = jnp.where(mask, gs, 0.0)
                gss.append(gs)
            for pair in range(nc // 2):
                cols = slice(pair * 2 * lw, (pair + 1) * 2 * lw)
                a, b = gss[0][:, cols], gss[1][:, cols]
                blk[2 * pair] = jnp.where(lane < lw, a, pltpu.roll(b, lw, 1))
                blk[2 * pair + 1] = jnp.where(lane < lw, pltpu.roll(a, lw, 1), b)
            for k, (o, z) in enumerate(((b0, l0), (b1, l1), (b2, l2), (b3, l3))):
                o[0:R] = blk[c ^ k]
                o[R : R + 8] = z[...]
            for r in range(2):
                gs_ref[:, r * mid : (r + 1) * mid] = gss[r]

        def conv_back_body(s, gs, red, sums1, vec, w1, dz1, sg1, zh, arrive):
            mask = mask_of(valid(s, 0), R, mid, edge)
            avg1, inv1, _ = stats(sums1, s)
            norm1 = (red[...] - avg1) * inv1
            on1 = (norm1 * vec[0, 3:4] + vec[1, 3:4] > 0) & mask
            for r in range(2):
                taps_in(gs[:, r * mid : (r + 1) * mid], (zh,), own)
                if r == 0:
                    arrive(4)
                acc = 0.0
                for t, (u, v) in enumerate(TAPS):
                    z = zh[2 - v, :, 2 - u : 2 - u + edge].reshape(R, mid)
                    acc += mm(z, w1[r, :, t * half : (t + 1) * half])
                cols = slice(r * half, (r + 1) * half)
                acc = jnp.where(on1[:, cols], acc, 0.0)
                dz1[:, cols] = acc
                sg1[0:1, cols] = colsum(acc)
                sg1[1:2, cols] = colsum(acc * norm1[:, cols])

        gs, blk0, blk1, blk2, blk3, gq, sg2, gfc, wab = call(
            back_body,
            image_counts,
            [merged, c1_all, c2_all, normf_all, sfc, sgb, pw_all, ga, spl, s2, vec, wts, l0, l1, l2, l3],
            [((R, 2 * mid), F32)]
            + [((R + 8, 2 * lw), F32)] * 4
            + [((ni, inner), F32), ((2, 2, mid), F32), ((2, inner), F32), ((2, mid), F32)],
            [pltpu.VMEM((nc, R, 2 * lw), F32)],
            far={6: WSQ, 7: None},
            lazy=True,
        )
        dz1, sg1 = call(
            conv_back_body,
            image_counts,
            [gs, red, s1, vec, w1],
            [((R, mid), F32), ((2, mid), F32)],
            [pltpu.VMEM((3, own, PAD, PAD, mid), BF16)],
            flops=4 * R * nw * mid,
            far=(4,),
            lazy=True,
        )
        blks = [blk0, swap(blk1, "chan", 1), swap(blk2, "chan", 2), swap(blk3, "chan", 3)]

        def prep_body(s, red_g, sums, vec, relu, norm):
            avg, inv, _ = stats(sums, s)
            for k in range(nc):
                mask = mask_of(valid(s, CHAN_REL[k]), R, mid, edge)
                v = (red_g[me()[0] ^ k] - avg) * inv
                rows = slice(k * R, (k + 1) * R)
                norm[rows, :] = v.astype(BF16)
                z = jnp.maximum(v * vec[0, 3:4] + vec[1, 3:4], 0.0)
                relu[rows, :] = jnp.where(mask, z, 0.0).astype(BF16)

        relu_all, norm_all = call(
            prep_body, image_counts, [after(red_g, gs), s1, vec], [((nc * R, mid), BF16)] * 2, far=(0,)
        )

        def masked_body(s, b0, b1, b2, b3, go, m0, m1, m2, m3, out_bo, scr):
            for r, (b, o) in enumerate(((b0, m0), (b1, m1), (b2, m2), (b3, m3))):
                bo = b[...]
                o[...] = load_quarter(go, scr, r, bo > 0)
                store_quarter(out_bo, scr, r, bo)

        *masked, block_out = call(
            masked_body,
            image_counts,
            [after(bos[0], gs)] + bos[1:] + [gouts],
            [((R, win), F32)] * 4 + [(feats.shape, F32)],
            [quarter_scratch],
            far=(0, 1, 2, 3, 4),
            far_out=(0, 1, 2, 3, 4),
        )

        dz1_y = swap(after(dz1, relu_all, masked[0]), "chan", 2)

        n_w = 9 * 2 * lw
        n_dws = padded_rows(n_w + lb * mid + 2 * lw)

        def dws_body(s, k0, k1, k2, k3, relu, hid, t1, t2, u1, sums3, sg, eg, *refs):
            outs, (sg_out, zg, out) = refs[:-3], refs[-3:]
            acc = 0.0
            base = lax.axis_index("dp") * nc
            for k, a in enumerate((k0, k1, k2, k3)):
                row = lax.broadcasted_iota(jnp.int32, (8, inner), 0)
                h = jnp.zeros((8, inner), F32)
                for b in range(own):
                    h = jnp.where(row == b, hid[pl.ds(base + (me()[0] ^ k) + b * ND, 1), :], h)
                acc += exact(a[R : R + 8, :], h, ((0,), (0,)))
            out[n_w + lb * mid : n_w + lb * mid + 2 * lw] = acc
            _, inv, n = stats(mine_of(sums3), s)
            sg = mine_of(sg)
            sg_out[...] = sg
            outer = exact(u1[...], sg[0:1], ((0,), (0,)))
            z = (eg[0:1] * inv) * (t1[...] - (outer + t2[...] * sg[1:2]) * n)
            for i in range(lb):
                out[n_w + i * mid : n_w + (i + 1) * mid] = z[:, i * 128 : (i + 1) * 128]
            for k, bk in enumerate((k0, k1, k2, k3)):
                taps_in(bk[0:R, :], (zg.at[:, k * own : (k + 1) * own],), own)
            taps = [zg[2 - v, :, 2 - u : 2 - u + edge].reshape(nc * R, 2 * lw) for u, v in TAPS]
            y = mm(relu[...], jnp.concatenate(taps, axis=1), ((0,), (0,)))
            lane = lax.broadcasted_iota(jnp.int32, (half, 2 * lw), 1)
            for t in range(9):
                cols = slice(t * 2 * lw, (t + 1) * 2 * lw)
                out[t * 2 * lw : (t + 1) * 2 * lw, :] = jnp.where(lane < lw, y[:half, cols], y[half:, cols]).T
            cut_chunks(out, groups[0], outs)

        *dws, sg3l = call(
            dws_body,
            image_counts,
            blks + [relu_all, after(hid_all, masked[0]), t1, t2, u1, s3, sg3, eg],
            chunk_outs(n_dws, groups[0]) + [((2, win), F32)],
            [pltpu.VMEM((3, slots, PAD, PAD, 2 * lw), BF16), pltpu.VMEM((n_dws, 128), F32)],
            flops=2 * nc * R * mid * 9 * 2 * lw,
            far=(0, 6, 7),
        )
        sg1_steps = sum_steps(after(sg1, dws[1]))
        sg1 = sg1_steps[-1]
        dz1_r = [dz1, dz1_y, swap(dz1, "chan", 1), swap(dz1_y, "chan", 1)]

        mb = mid // 128
        n_dwr = padded_rows(mb * win)

        def dwr_body(s, d0, d1, d2, d3, norms, x0, x1, x2, x3, sums, sg, vec, *refs):
            outs, (go0, go1, go2, go3, sent) = refs[:-5], refs[-5:]
            _, inv, n = stats(sums, s)
            acc = 0.0
            for r, (dz, go, x) in enumerate(((d0, go0, x0), (d1, go1, x1), (d2, go2, x2), (d3, go3, x3))):
                mask = mask_of(valid(s, r), R, win, edge)
                k = CHAN_REL[r]
                norm = norms[k * R : (k + 1) * R, :].astype(F32)
                g = vec[0, 3:4] * inv * (dz[...] - (sg[0:1] + norm * sg[1:2]) * n)
                g = jnp.where(mask, g, 0.0).astype(BF16)
                go[...] = g
                acc += mm(x[...], g, ((0,), (0,)))
            for i in range(mb):
                sent[i * win : (i + 1) * win] = acc[:, i * 128 : (i + 1) * 128]
            cut_chunks(sent, groups[0], outs)

        *sent, gr0, gr1, gr2, gr3 = call(
            dwr_body,
            image_counts,
            dz1_r + [norm_all, x0, x1, x2, x3, s1, sg1, vec],
            chunk_outs(n_dwr, groups[0]) + [((R, mid), BF16)] * 4,
            [pltpu.VMEM((n_dwr, 128), F32)],
            flops=8 * R * win * mid,
            far=(5, 6, 7, 8),
        )
        def gin_body(s, g0, g1, g2, g3, m0, m1, m2, m3, w_ref, out_gi, scr):
            w = w_ref[...].astype(BF16)
            for r, (g, m) in enumerate(((g0, m0), (g1, m1), (g2, m2), (g3, m3))):
                store_quarter(out_gi, scr, r, mm(g[...], w, ((1,), (1,))) + m[...])

        (grad_input,) = call(
            gin_body,
            image_counts,
            [gr0, gr1, gr2, gr3] + masked + [reduce_weight],
            [(feats.shape, F32)],
            [quarter_scratch],
            flops=8 * R * win * mid,
            far=(4, 5, 6, 7, 8),
            far_out=(0,),
        )

        def write_dwr(whole, out):
            for i in range(mb):
                out[:, i * 128 : (i + 1) * 128] = whole[i * win : (i + 1) * win, :]

        (grad_reduce_weight,) = sum_dp(image_counts, sent, write_dwr, [((win, mid), F32)])
        def write_dws(whole, o_ws, o_we, o_at):
            o_ws[...] = whole[:n_w, :]
            for i in range(lb):
                o_we[:, i * 128 : (i + 1) * 128] = whole[n_w + i * mid : n_w + (i + 1) * mid, :]
            o_at[...] = whole[n_w + lb * mid : n_w + lb * mid + 2 * lw, :]

        dws, grad_expand_weight, watt = sum_dp(
            image_counts,
            dws,
            write_dws,
            [((n_w, 128), F32), ((mid, win), F32), ((2 * lw, 128), F32)],
            [(), (grad_input,)],
        )
        grad_split_weight = dws.reshape(3, 3, 2, lw, half).transpose(0, 1, 4, 2, 3)
        block_out, grad_input = from_native(block_out), from_native(grad_input)

        def sq_body(s, pool, gq, out):
            out[...] = exact(pool[...], gq[...], ((0,), (0,)))

        (wsw,) = call(sq_body, image_counts, [pool_all, gq], [((mid, inner), F32)])

        def own_lanes(z, axis):
            return lax.dynamic_slice_in_dim(z, c * lw, lw, axis)

        return (
            block_out,
            grad_input,
            grad_reduce_weight,
            own_lanes(sg1[1], 0),
            own_lanes(sg1[0], 0),
            grad_split_weight,
            own_lanes(sg2[1], 1),
            own_lanes(sg2[0], 1),
            own_lanes(wsw, 0),
            gfc[0],
            gfc[1],
            watt.reshape(2, lw, inner).transpose(2, 0, 1),
            own_lanes(wab, 1),
            grad_expand_weight,
            sg3l[1],
            sg3l[0],
        )

    return per_device


def solution(mesh):
    in_specs = (
        P("dp", None, None, "chan"),
        P(),
        P("chan", None),
        P("chan"),
        P("chan"),
        P(None, None, None, None, "chan"),
        P(None, "chan"),
        P(None, "chan"),
        P("chan", None),
        P(),
        P(),
        P(None, None, "chan"),
        P(None, "chan"),
        P(None, "chan"),
        P("chan"),
        P("chan"),
        P("dp", None, None, "chan"),
    )
    out_specs = (
        P("dp", None, None, "chan"),
        P("dp", None, None, "chan"),
        P("chan", None),
        P("chan"),
        P("chan"),
        P(None, None, None, None, "chan"),
        P(None, "chan"),
        P(None, "chan"),
        P("chan", None),
        P(),
        P(),
        P(None, None, "chan"),
        P(None, "chan"),
        P(None, "chan"),
        P("chan"),
        P("chan"),
    )
    return jax.shard_map(
        build(mesh), mesh=mesh, in_specs=in_specs, out_specs=out_specs, check_vma=False
    )
```

```python
import functools

import jax
import jax.numpy as jnp
from jax import lax
from jax.experimental import pallas as pl
from jax.experimental.pallas import tpu as pltpu
from jax.sharding import PartitionSpec as P

EPSILON = 1e-05
F32, BF16 = jnp.float32, jnp.bfloat16
PAD = 16
VMEM_LIMIT = 32 * 1024 * 1024


def bits_of(n):
    out, k = [], 1
    while k < n:
        out.append(k)
        k *= 2
    return out


def split2(x):
    hi = x.astype(BF16)
    return hi, (x - hi.astype(F32)).astype(BF16)


def mm(a, b, dims=((1,), (0,))):
    return lax.dot_general(a, b, (dims, ((), ())), preferred_element_type=F32)


def split3(x):
    hi = x.astype(BF16)
    x = x - hi.astype(F32)
    mid = x.astype(BF16)
    return hi, mid, (x - mid.astype(F32)).astype(BF16)


def mm3(a, b, dims=((1,), (0,))):
    return mm(a[0], b[0], dims) + (mm(a[0], b[1], dims) + mm(a[1], b[0], dims))


def mm6(a, b, dims=((1,), (0,))):
    small = mm(a[0], b[2], dims) + mm(a[2], b[0], dims) + mm(a[1], b[1], dims)
    return mm(a[0], b[0], dims) + (mm(a[0], b[1], dims) + mm(a[1], b[0], dims) + small)


def exact(a, b, dims=((1,), (0,))):
    return lax.dot_general(
        a, b, (dims, ((), ())), precision=lax.Precision.HIGHEST, preferred_element_type=F32
    )


def call(body, counts, ins, outs, scratch=(), flops=0, far=(), far_out=(), lazy=False):
    cuts = far if isinstance(far, dict) else {k: None for k in far}
    far, far_out = sorted(cuts), sorted(far_out)
    moved = sum(a.size * a.dtype.itemsize for a in ins) + sum(
        int(jnp.dtype(d).itemsize) * functools.reduce(lambda x, y: x * y, s, 1) for s, d in outs
    )
    vmem, hbm = pl.BlockSpec(memory_space=pltpu.VMEM), pl.BlockSpec(memory_space=pltpu.HBM)
    own_scratch = len(scratch)
    def shape_of(k):
        shape, part = ins[k].shape, cuts[k]
        return shape if part is None else shape[:1] + (part.stop - part.start,) + shape[2:]

    held = [pltpu.VMEM(shape_of(k), ins[k].dtype) for k in far] + [pltpu.VMEM(*outs[k]) for k in far_out]
    sems = [pltpu.SemaphoreType.DMA] * len(held)

    def kernel(s, *refs):
        n, m = len(ins), len(outs)
        refs_in, refs_out = list(refs[:n]), list(refs[n : n + m])
        rest = refs[n + m :]
        scr, bufs, sem = rest[:own_scratch], rest[own_scratch : own_scratch + len(held)], rest[own_scratch + len(held) :]
        copies = []
        for i, k in enumerate(far):
            part = cuts[k]
            src = refs_in[k] if part is None else refs_in[k].at[:, part.start : part.stop, :]
            copies.append(pltpu.make_async_copy(src, bufs[i], sem[i]))
            copies[-1].start()
            refs_in[k] = bufs[i]
        homes = []
        for i, k in enumerate(far_out):
            i += len(far)
            homes.append(pltpu.make_async_copy(bufs[i], refs_out[k], sem[i]))
            refs_out[k] = bufs[i]
        if lazy:
            body(s, *refs_in, *refs_out, *scr, arrive=lambda k: copies[far.index(k)].wait())
        else:
            for copy in copies:
                copy.wait()
            body(s, *refs_in, *refs_out, *scr)
        for copy in homes:
            copy.start()
        for copy in homes:
            copy.wait()

    ins = [pltpu.with_memory_space_constraint(a, pltpu.HBM) if k in far else a for k, a in enumerate(ins)]
    return pl.pallas_call(
        kernel,
        out_shape=[pltpu.HBM(s, d) if k in far_out else jax.ShapeDtypeStruct(s, d) for k, (s, d) in enumerate(outs)],
        in_specs=[pl.BlockSpec(memory_space=pltpu.SMEM)] + [hbm if k in far else vmem for k in range(len(ins))],
        out_specs=[hbm if k in far_out else vmem for k in range(len(outs))],
        scratch_shapes=list(scratch) + held + sems,
        compiler_params=pltpu.CompilerParams(vmem_limit_bytes=VMEM_LIMIT),
        cost_estimate=pl.CostEstimate(flops=flops, bytes_accessed=moved, transcendentals=0),
    )(counts, *ins)


def mask_of(nv, rows, cols, edge):
    r = lax.broadcasted_iota(jnp.int32, (rows, cols), 0)
    return ((r & (PAD - 1)) < edge) & (r < nv * (edge * PAD))


def colsum(x):
    return jnp.sum(x, axis=0, keepdims=True)


def build(mesh):
    nd, nc = mesh.shape["dp"], mesh.shape["chan"]
    both = ("dp", "chan")
    cbits, dbits = bits_of(nc), bits_of(nd)
    flat_bits = bits_of(nd * nc)
    pairs = [flat_bits[i : i + 2] for i in range(1, len(flat_bits), 2)]
    sum_groups = [[1]] + [[k | 1 for k in ([p[0], p[1], p[0] ^ p[1]] if len(p) == 2 else p)] for p in pairs[::-1]]

    def swap(x, axis, k):
        n = {"dp": nd, "chan": nc}[axis] if isinstance(axis, str) else nd * nc
        return lax.ppermute(x, axis, [(i, i ^ k) for i in range(n)])

    def after(x, *deps):
        return lax.optimization_barrier((x,) + deps)[0]

    def sum_steps(x, before_last=()):
        out = [x]
        for i, g in enumerate(sum_groups):
            x = out[-1]
            if before_last and i == len(sum_groups) - 1:
                x = after(x, *before_last)
            got = [swap(x, both, k) for k in g]
            x = x + got[0]
            out.append(x + (got[1] + got[2]) if len(g) == 3 else x)
        return out

    def sum_all(x):
        return sum_steps(x)[-1]

    def pick(x, i):
        return lax.dynamic_index_in_dim(x, i, 0, False)

    groups = [dbits[:1]] + [dbits[i : i + 2] for i in range(1, len(dbits), 2)]

    def masks(g):
        out = [0]
        for k in g:
            out = out + [m ^ k for m in out]
        return out

    def place_in(g):
        n = 2 ** len(g)
        return (lax.axis_index("dp") // g[0]) % n, n

    def cut_chunks(scr, g, outs):
        at, n = place_in(g)
        rows = scr.shape[0] // n
        for m, o in enumerate(outs):
            o[...] = scr[pl.ds(pl.multiple_of((at ^ m) * rows, 8), rows), :]

    def chunk_outs(rows, g):
        n = 2 ** len(g)
        return [((rows // n, 128), F32)] * n

    def padded_rows(rows):
        return -(-rows // (8 * nd)) * 8 * nd

    def sum_dp(counts, chunks, write, outs, before=()):
        stages = []

        def exchanged(first, rest, g):
            got = [first] + [swap(z, "dp", m) for z, m in zip(rest, masks(g)[1:])]
            k = len(stages)
            if k < len(before) and before[k]:
                got[0] = after(got[0], *before[k])
            return got

        for i, g in enumerate(groups):
            got = exchanged(chunks[0], chunks[1:], g)
            rows = got[0].shape[0]
            last = i == len(groups) - 1

            def add_body(s, *refs, n=len(got), last=last, i=i):
                v = refs[0][...]
                for z in refs[1:n]:
                    v = v + z[...]
                if last:
                    refs[n][...] = v
                else:
                    refs[-1][...] = v
                    cut_chunks(refs[-1], groups[i + 1], refs[n:-1])

            chunks = call(
                add_body,
                counts,
                got,
                [((rows, 128), F32)] if last else chunk_outs(rows, groups[i + 1]),
                [] if last else [pltpu.VMEM((rows, 128), F32)],
            )
            stages.append(chunks[0])
        (x,) = chunks
        for g in groups[::-1]:
            got = exchanged(x, [x] * (2 ** len(g) - 1), g)
            rows = x.shape[0]
            last = g is groups[0]

            def join_body(s, *refs, n=len(got), g=g, rows=rows, last=last):
                at, _ = place_in(g)
                for m, z in enumerate(refs[:n]):
                    refs[-1][pl.ds(pl.multiple_of((at ^ m) * rows, 8), rows), :] = z[...]
                if last:
                    write(refs[-1], *refs[n:-1])

            whole = ((rows * len(got), 128), F32)
            if last:
                return call(join_body, counts, got, outs, [pltpu.VMEM(*whole)])
            (x,) = call(join_body, counts, got, [whole])
            stages.append(x)

    def quarter_of(chan):
        q = chan * 0
        for k in cbits:
            q = q * 2 + (chan // k) % 2
        return q

    def per_device(
        features_in,
        image_counts,
        reduce_weight,
        reduce_gain,
        reduce_shift,
        split_weight,
        split_gain,
        split_shift,
        squeeze_weight,
        squeeze_gain,
        squeeze_shift,
        attend_weight,
        attend_bias,
        expand_weight,
        expand_gain,
        expand_shift,
        grad_out,
    ):
        slots, edge = features_in.shape[0], features_in.shape[1]
        area = edge * edge
        win = features_in.shape[3]
        mid = reduce_weight.shape[1]
        half = mid // 2
        lw = split_weight.shape[4]
        inner = squeeze_gain.shape[0]
        own = slots // nc
        span = edge * PAD
        R = own * span
        ni = nd * slots
        c = lax.axis_index("chan")

        def me():
            c = lax.axis_index("chan")
            return c, quarter_of(c)

        def valid(s, r):
            return jnp.clip(s[lax.axis_index("dp")] - (me()[1] ^ r) * own, 0, own)

        def recip(s, each):
            total = s[0]
            for i in range(1, nd):
                total = total + s[i]
            return (1.0 / (jnp.full((1, 128), total, jnp.int32).astype(F32) * each))[:, 0:1]

        TAPS = [(u, v) for u in range(3) for v in range(3)]

        def stats(sum_ref, s):
            n = recip(s, area)
            avg = sum_ref[0:1] * n
            inv = lax.rsqrt(sum_ref[1:2] * n - avg * avg + EPSILON)
            return avg, inv, n

        lb = win // 128

        def native(x):
            x = x.transpose(1, 2, 0, 3).reshape(area, slots, lb, 128)
            return x.transpose(0, 2, 1, 3).reshape(area * lb * slots, 128)

        def from_native(z):
            z = z.reshape(area, lb, slots, 128).transpose(0, 2, 1, 3)
            return z.reshape(edge, edge, slots, win).transpose(2, 0, 1, 3)

        def place_of(h, i, b, r):
            at = (h * edge * lb + i) * slots + (me()[1] ^ r) * own + b
            return pl.ds(at, edge, stride=lb * slots)

        def load_quarter(ref, scr, r, mask):
            for b in range(own):
                for h in range(edge):
                    for i in range(lb):
                        scr[b * edge + h, :edge, i * 128 : (i + 1) * 128] = ref[place_of(h, i, b, r), :]
            return jnp.where(mask, scr[...].reshape(R, win), 0.0)

        def store_quarter(ref, scr, r, z):
            scr[...] = z.reshape(own * edge, PAD, win)
            for b in range(own):
                for h in range(edge):
                    for i in range(lb):
                        ref[place_of(h, i, b, r), :] = scr[b * edge + h, :edge, i * 128 : (i + 1) * 128]

        def mine_of(ref):
            c, out = me()[0], ref[0:2]
            for k in range(1, nc):
                out = jnp.where(c == k, ref[2 * k : 2 * k + 2], out)
            return out

        feats, gouts = native(features_in), native(grad_out)
        quarter_scratch = pltpu.VMEM((own * edge, PAD, win), F32)

        wt = split_weight.transpose(0, 1, 3, 4, 2).reshape(-1, half)


        def pack(rg, rs, sg, ss, ab, eg):
            return jnp.concatenate(
                [
                    sg.reshape(1, -1),
                    ss.reshape(1, -1),
                    ab.reshape(1, -1),
                    jnp.concatenate([rg, rs])[None],
                    eg.reshape(-1, 2 * lw),
                    jnp.zeros((8 - 4 - win // (2 * lw), 2 * lw), F32),
                ]
            )

        nw = 9 * half

        def reduce_body(rels, s, x_ref, w_ref, *refs):
            n, scr = len(rels), refs[-1]
            w = split3(w_ref[...])
            for k, r in enumerate(rels):
                x = split3(load_quarter(x_ref, scr, r, mask_of(valid(s, r), R, win, edge)))
                refs[n + k][...] = x[0]
                refs[k][...] = mm6(x, w)

        def reduce_call(rels, feats=feats):
            return call(
                functools.partial(reduce_body, rels),
                image_counts,
                [feats, reduce_weight],
                [((R, mid), F32)] * len(rels) + [((R, win), BF16)] * len(rels),
                [quarter_scratch],
                flops=12 * R * win * mid * len(rels),
                far=(0, 1),
                far_out=(len(rels), len(rels) + 1),
            )

        p3, p1, x3, x1 = reduce_call((3, 1))
        p2, p0, x2, x0 = reduce_call((2, 0))
        y1 = p1 + swap(p3, "chan", 1)
        ys = swap(y1, "chan", 2)
        rc = swap(p2, "chan", 1)

        def gather3(x, gate=None):
            y = swap(x, "chan", 2)
            return [x, y, swap(x, "chan", 1), swap(y if gate is None else after(y, gate), "chan", 1)]

        small = lax.optimization_barrier(
            (y1, reduce_gain, reduce_shift, split_gain, split_shift, attend_bias, expand_gain)
        )
        ps = pack(*small[1:])

        wt_y = swap(after(wt, ys), "chan", 2)
        wt_r = [wt, wt_y, swap(wt, "chan", 1), swap(wt_y, "chan", 1)]

        small = lax.optimization_barrier((y1, expand_weight, attend_weight, squeeze_weight))
        pw = jnp.concatenate(
            [small[1][:, i * 128 : (i + 1) * 128] for i in range(lb)]
            + [small[2].transpose(1, 2, 0).reshape(2 * lw, inner), small[3]]
        )
        CHAN_REL = (0, 2, 1, 3)

        nl = mid // 128

        def red_body(s, a, b, y, ps, red, sums):
            v = a[...] + b[...] + y[...]
            red[...] = v
            sums[...] = jnp.zeros((8 + 8 * nc, 128), F32)
            for k, z in enumerate((colsum(v), colsum(v * v))):
                for i in range(nl):
                    sums[k * nl + i : k * nl + i + 1, :] = z[:, i * 128 : (i + 1) * 128]
            sums[pl.ds(pl.multiple_of(8 + 8 * me()[0], 8), 8), :] = ps[...]

        red, s1 = call(red_body, image_counts, [p0, rc, ys, ps], [((R, mid), F32), ((8 + 8 * nc, 128), F32)])
        s1_steps = sum_steps(s1, (wt_y,))

        def vec_body(s, sums, s1, vec, g3):
            for k in range(2):
                for i in range(nl):
                    s1[k : k + 1, i * 128 : (i + 1) * 128] = sums[k * nl + i : k * nl + i + 1, :]
            own_of = [sums[8 + 8 * k : 16 + 8 * k, :] * (1.0 / nd) for k in range(nc)]
            lane = lax.broadcasted_iota(jnp.int32, (8, 2 * lw), 1)
            for pair in range(nc // 2):
                a, b = own_of[2 * pair], own_of[2 * pair + 1]
                cols = slice(pair * 2 * lw, (pair + 1) * 2 * lw)
                vec[0, :, cols] = jnp.where(lane < lw, a, pltpu.roll(b, lw, 1))
                vec[1, :, cols] = jnp.where(lane < lw, pltpu.roll(a, lw, 1), b)
            g3[...] = jnp.zeros((8, win), F32)
            for k in range(nc):
                for i in range(win // (2 * lw)):
                    g3[k : k + 1, i * 2 * lw : (i + 1) * 2 * lw] = own_of[k][4 + i : 5 + i, :]

        s1, vec, g3 = call(
            vec_body, image_counts, [s1_steps[-1]], [((2, mid), F32), ((2, 8, mid), F32), ((8, win), F32)]
        )

        pw_all = lax.all_gather(after(pw, s1_steps[-2], wt_y), "chan")
        WE = slice(0, lb * mid)
        WAT = slice(lb * mid, lb * mid + 2 * lw)
        WSQ = slice(lb * mid + 2 * lw, lb * mid + 3 * lw)

        def we_of(ref, k):
            return jnp.concatenate([ref[k, i * mid : (i + 1) * mid, :] for i in range(lb)], axis=1)

        def wat_of(ref, r):
            return jnp.concatenate([ref[k, r * lw : (r + 1) * lw, :] for k in range(nc)], axis=0)

        def wsq_of(ref):
            return ref[...].reshape(mid, inner)

        def taps_in(z, scrs, n):
            w = z.shape[1]
            rows = n * span
            for v in range(3):
                zz = z if v == 1 else pltpu.roll(z, 1 if v == 0 else rows - 1, 0)
                parts = split2(zz) if len(scrs) == 2 else [zz.astype(BF16)]
                for scr, part in zip(scrs, parts):
                    scr[v, :, 0] = jnp.zeros((n, PAD, w), BF16)
                    scr[v, :, edge + 1] = jnp.zeros((n, PAD, w), BF16)
                    scr[v, :, 1 : edge + 1] = part.reshape(n, edge, PAD, w)

        def conv_body(s, red, sums, vec, v0, v1, v2, v3, out, sums2, w1, za, zb, w2, arrive):
            avg, inv, _ = stats(sums, s)
            mask = mask_of(valid(s, 0), R, mid, edge)
            z = jnp.maximum((red[...] - avg) * inv * vec[0, 3:4] + vec[1, 3:4], 0.0)
            z = jnp.where(mask, z, 0.0)
            taps_in(z, (za, zb), own)
            for rel, ref in enumerate((v0, v1, v2, v3)):
                arrive(3 + rel)
                rows = pl.ds(pl.multiple_of((me()[0] ^ CHAN_REL[rel]) * lw, lw), lw)
                for t in range(9):
                    for r in range(2):
                        at = t * 2 * lw + r * lw
                        for o, z in zip((w1, w2), split2(ref[at : at + lw, :])):
                            o[r, rows, t * half : (t + 1) * half] = z
            for r in range(2):
                cols = slice(r * half, (r + 1) * half)
                lhs = [
                    jnp.concatenate([z[v, :, u : u + edge, :, cols].reshape(R, half) for u, v in TAPS], axis=1)
                    for z in (za, zb)
                ]
                y = mm3(lhs, (w1[r], w2[r]), ((1,), (1,)))
                out[:, r * mid : (r + 1) * mid] = y
                y = jnp.where(mask, y, 0.0)
                sums2[0:1, r * mid : (r + 1) * mid] = colsum(y)
                sums2[1:2, r * mid : (r + 1) * mid] = colsum(y * y)

        spl, s2, w1 = call(
            conv_body,
            image_counts,
            [red, s1, vec] + wt_r,
            [((R, 2 * mid), F32), ((2, 2 * mid), F32), ((2, mid, nw), BF16)],
            [pltpu.VMEM((3, own, PAD, PAD, mid), BF16)] * 2 + [pltpu.VMEM((2, mid, nw), BF16)],
            flops=12 * R * nw * mid,
            far=(3, 4, 5, 6),
            far_out=(2,),
            lazy=True,
        )

        s2_steps = sum_steps(s2)
        s2 = s2_steps[-1]

        def second(spl, sums, n, vec, r, mask):
            cols = slice(r * mid, (r + 1) * mid)
            avg = sums[0:1, cols] * n
            inv = lax.rsqrt(sums[1:2, cols] * n - avg * avg + EPSILON)
            norm = (spl[:, cols] - avg) * inv
            act = norm * vec[r, 0:1] + vec[r, 1:2]
            return norm, act, (act > 0) & mask, inv

        def per_image(z):
            return [colsum(z[b * span : (b + 1) * span]) for b in range(own)]

        nb = mid // 128
        BLOCK = max(64, 4 * nb * own)
        ND = nd * nc

        def pool_body(s, spl, sums, vec, wsq, c12, sq, sfc, arrive):
            mask = mask_of(valid(s, 0), R, mid, edge)
            n = recip(s, area)
            pooled = [0.0] * own
            c12[...] = jnp.zeros((BLOCK, 128), F32)
            for r in range(2):
                norm, act, on, _ = second(spl, sums, n, vec, r, mask)
                c1 = per_image(jnp.where(on, 1.0, 0.0))
                c2 = per_image(jnp.where(on, norm, 0.0))
                for b in range(own):
                    for i in range(nb):
                        sl = slice(i * 128, (i + 1) * 128)
                        for k, z in ((r * nb + i, c1), ((2 + r) * nb + i, c2)):
                            c12[k * own + b : k * own + b + 1, :] = z[b][:, sl]
                    pooled[b] = pooled[b] + vec[r, 0:1] * c2[b] + vec[r, 1:2] * c1[b]
            p = jnp.concatenate(pooled + [jnp.zeros((8 - own, mid), F32)], axis=0) * (1.0 / area)
            arrive(3)
            v = exact(p, wsq_of(wsq))
            sq[...] = v
            live = lax.broadcasted_iota(jnp.int32, (8, inner), 0) < valid(s, 0)
            v = jnp.where(live, v, 0.0)
            sfc[0:1] = colsum(v)
            sfc[1:2] = colsum(v * v)

        c12, sq, sfc = call(
            pool_body,
            image_counts,
            [spl, s2, vec, pw_all],
            [((BLOCK, 128), F32), ((8, inner), F32), ((2, inner), F32)],
            far={3: WSQ},
            lazy=True,
        )
        c12_g = lax.all_gather(c12, both, axis=0, tiled=True)
        sfc = sum_all(sfc)
        red_g = lax.all_gather(after(red, sfc), "chan")
        sgb = jnp.stack([squeeze_gain, squeeze_shift])

        def squeeze_norm(sq, sums, s, sgb):
            n = recip(s, 1)
            avg = sums[0:1] * n
            inv = lax.rsqrt(sums[1:2] * n - avg * avg + EPSILON)
            norm = (sq - avg) * inv
            return norm, norm * sgb[0:1] + sgb[1:2], inv

        def attend_body(s, spl, sums, vec, sfc, sq, sgb, wat, att, wts, arrive):
            mask = mask_of(valid(s, 0), R, mid, edge)
            n = recip(s, area)
            _, actf, _ = squeeze_norm(sq[...], sfc, s, sgb)
            hidden = jnp.maximum(actf, 0.0)
            halves = [second(spl, sums, n, vec, r, mask) for r in range(2)]
            arrive(6)
            lg = [exact(hidden, wat_of(wat, r), ((1,), (1,))) + vec[r, 2:3] for r in range(2)]
            top = jnp.maximum(lg[0], lg[1])
            e = [jnp.exp(z - top) for z in lg]
            total = e[0] + e[1]
            acc = 0.0
            imgs = lax.broadcasted_iota(jnp.int32, (R, mid), 0)
            for r in range(2):
                w = e[r] / total
                wts[r] = w
                _, act, on, _ = halves[r]
                wrow = w[0:1]
                for b in range(1, own):
                    wrow = jnp.where(imgs >= b * span, w[b : b + 1], wrow)
                acc = acc + jnp.where(on, act * wrow, 0.0)
            att[...] = acc

        att, wts = call(
            attend_body,
            image_counts,
            [spl, s2, vec, sfc, sq, sgb, pw_all],
            [((R, mid), F32), ((2, 8, mid), F32)],
            far={6: WAT},
            lazy=True,
        )

        def own_expand_body(s, att, we, sums):
            a = split2(att[...])
            for k in range(nc):
                y = mm3(a, split2(we_of(we, k)))
                sums[2 * k : 2 * k + 1] = colsum(y)
                sums[2 * k + 1 : 2 * k + 2] = colsum(y * y)

        (s3,) = call(
            own_expand_body, image_counts, [att, pw_all], [((2 * nc, win), F32)], flops=6 * R * mid * win * nc, far={1: WE}
        )
        att_y = swap(att, "chan", 2)
        s3_steps = sum_steps(s3, (att_y,))
        s3 = s3_steps[-1]
        att_r = [att, att_y, swap(att, "chan", 1), swap(after(att_y, s3_steps[-2]), "chan", 1)]
        eg = jnp.stack([expand_gain, expand_shift])

        def expand_body(rels, extra, s, *refs, arrive):
            n = len(rels)
            atts, (x_ref, g_ref, w_ref, sums, eg) = refs[:n], refs[n : n + 5]
            prev, refs = refs[n + 5 : n + 5 + extra], refs[n + 5 + extra :]
            bos, gas, dzs = refs[:n], refs[n : 2 * n], refs[2 * n : 3 * n]
            sg, t1, t2, u1, scr = refs[3 * n :]
            avg, inv, _ = stats(mine_of(sums), s)
            arrive(n + 2)
            w = split2(w_ref[...])
            sg_acc, t1_acc, t2_acc, u_acc = [0.0, 0.0], 0.0, 0.0, 0.0
            for k, r in enumerate(rels):
                mask = mask_of(valid(s, r), R, win, edge)
                a = atts[k][...]
                ap = split2(a)
                norm = (mm3(ap, w) - avg) * inv
                if k == 0:
                    arrive(n)
                x = load_quarter(x_ref, scr, r, mask)
                pre = norm * eg[0:1] + eg[1:2] + x
                on = (pre > 0) & mask
                bos[k][...] = jnp.where(on, pre, 0.0)
                if k == 0:
                    arrive(n + 1)
                g = load_quarter(g_ref, scr, r, on)
                dzs[k][...] = g
                sg_acc[0] += colsum(g)
                sg_acc[1] += colsum(g * norm)
                gb = g.astype(BF16)
                nb = jnp.where(mask, norm, 0.0).astype(BF16)
                gas[k][...] = mm((g * (eg[0:1] * inv)).astype(BF16), w[0], ((1,), (1,)))
                t = mm(ap[0], jnp.concatenate([gb, nb], axis=1), ((0,), (0,)))
                t1_acc += t[:, :win]
                t2_acc += t[:, win:]
                u_acc += colsum(a)
            row = lax.broadcasted_iota(jnp.int32, (2 * nc, win), 0)
            c, _ = me()
            z = jnp.where(row == 2 * c, sg_acc[0], 0.0)
            sg[...] = jnp.where(row == 2 * c + 1, sg_acc[1], z)
            for o, z, p in zip((t1, t2, u1), (t1_acc, t2_acc, u_acc), prev[1:] or (None,) * 3):
                o[...] = z if p is None else z + p[...]
            if prev:
                sg[...] = sg[...] + prev[0][...]

        def expand_call(rels, prev):
            n = len(rels)
            return call(
                functools.partial(expand_body, rels, len(prev)),
                image_counts,
                [att_r[r] for r in rels] + [feats, gouts, expand_weight, s3, eg] + prev,
                [((R, win), F32)] * n
                + [((R, mid), F32)] * n
                + [((R, win), F32)] * n
                + [((2 * nc, win), F32), ((mid, win), F32), ((mid, win), F32), ((1, mid), F32)],
                [quarter_scratch],
                flops=12 * R * mid * win * n,
                far=(n, n + 1, n + 2),
                far_out=tuple(range(n)) + tuple(range(2 * n, 3 * n)) + ((3 * n + 1, 3 * n + 2) if prev else ()),
                lazy=True,
            )

        bo3, bo1, ga3, ga1, dz3, dz1_, *prev = expand_call((3, 1), [])
        gy1 = ga1 + swap(ga3, "chan", 1)
        bo2, bo0, ga2, ga0, dz2, dz0, sg3, t1, t2, u1 = expand_call((2, 0), [after(prev[0], gy1)] + list(prev[1:]))
        gys = swap(gy1, "chan", 2)
        grc = swap(ga2, "chan", 1)
        sg3 = sum_steps(sg3, (gys,))[-1]
        bos = [bo0, bo1, bo2, bo3]
        masked = [dz0, dz1_, dz2, dz3]

        def gatt_body(s, p, rc, ys, att, we, g3, sums, sg, spl, sums2, vec, wts, sfc, sq, sgb, wat, ga, l0, l1, l2, l3, merged, scr):
            m_acc, v_acc = 0.0, 0.0
            n = recip(s, area)
            for k in range(nc):
                avg = sums[2 * k : 2 * k + 1] * n
                inv = lax.rsqrt(sums[2 * k + 1 : 2 * k + 2] * n - avg * avg + EPSILON)
                sc = g3[k : k + 1] * inv * n
                kap = sg[2 * k + 1 : 2 * k + 2] * inv * sc
                w = we_of(we, k)
                wb = w.astype(BF16)
                m_acc += mm((w * kap).astype(BF16), wb, ((1,), (1,)))
                vv = sg[2 * k : 2 * k + 1] * sc - avg * kap
                row = lax.broadcasted_iota(jnp.int32, (16, win), 0)
                high = jnp.where(row == 0, vv, 0.0)
                low = jnp.where(row == 1, vv - vv.astype(BF16).astype(F32), 0.0)
                v_acc += colsum(mm((high + low).astype(BF16), wb, ((1,), (1,))))
            mask = mask_of(valid(s, 0), R, mid, edge)
            g = p[...] + rc[...] + ys[...] - mm(att[...].astype(BF16), m_acc.astype(BF16)) - v_acc
            g = jnp.where(mask, g, 0.0)
            ga[...] = g
            gw, a12 = [], []
            for r in range(2):
                norm, act, on, _ = second(spl, sums2, n, vec, r, mask)
                gon = jnp.where(on, g, 0.0)
                a1, a2 = per_image(gon), per_image(gon * norm)
                zero = [jnp.zeros((8 - own, mid), F32)]
                a1, a2 = jnp.concatenate(a1 + zero, axis=0), jnp.concatenate(a2 + zero, axis=0)
                a12.append((a1, a2))
                gw.append(vec[r, 0:1] * a2 + vec[r, 1:2] * a1)
            mean = wts[0] * gw[0] + wts[1] * gw[1]
            gh = 0.0
            parts, zs = [], []
            for r in range(2):
                z = wts[r] * (gw[r] - mean)
                zs.append(z)
                gh = gh + exact(z, wat_of(wat, r))
                for j in range(2):
                    parts.append(colsum(wts[r] * a12[r][j]))
            parts += [colsum(z) for z in zs]
            _, actf, _ = squeeze_norm(sq[...], sfc, s, sgb)
            dzf = jnp.where(actf > 0, gh, 0.0)
            c, _ = me()
            row = lax.broadcasted_iota(jnp.int32, (ni, inner), 0)
            z = jnp.zeros((ni, inner), F32)
            for b in range(own):
                z = jnp.where(row == lax.axis_index("dp") * nc + c + b * ND, dzf[b : b + 1], z)
            merged[0:ni] = z
            lane = lax.broadcasted_iota(jnp.int32, (8, 2 * lw), 1)
            for pair in range(nc // 2):
                cols = slice(pair * 2 * lw, (pair + 1) * 2 * lw)
                a, b = zs[0][:, cols], zs[1][:, cols]
                scr[2 * pair] = jnp.where(lane < lw, a, pltpu.roll(b, lw, 1))
                scr[2 * pair + 1] = jnp.where(lane < lw, pltpu.roll(a, lw, 1), b)
            for k, o in enumerate((l0, l1, l2, l3)):
                o[...] = scr[c ^ k]
            merged[ni:] = jnp.zeros((6 * nb + 4, inner), F32)
            for k, pz in enumerate(parts):
                for i in range(nb):
                    merged[ni + k * nb + i : ni + k * nb + i + 1] = pz[:, i * 128 : (i + 1) * 128]

        ga, l0, l1, l2, l3, merged = call(
            gatt_body,
            image_counts,
            [ga0, grc, gys, att, pw_all, g3, s3, sg3, spl, s2, vec, wts, sfc, sq, sgb, pw_all],
            [((R, mid), F32)] + [((8, 2 * lw), F32)] * 4 + [((ni + 6 * nb + 4, inner), F32)],
            [pltpu.VMEM((nc, 8, 2 * lw), F32)],
            flops=2 * R * mid * mid + 2 * nc * mid * mid * win,
            far={4: WE, 15: WAT},
            far_out=(0,),
        )

        used = 4 * nb * own

        def all_body(s, g, vec, wsq, sfc, sgb, c1_ref, c2_ref, pool_ref, norm_ref, hid_ref):
            g = g.reshape(ND * used, 128)

            def rows(k):
                return jnp.concatenate([g[pl.ds(k * own + b, ND, stride=used), :] for b in range(own)], axis=0)

            pooled = 0.0
            for r in range(2):
                c1 = jnp.concatenate([rows(r * nb + i) for i in range(nb)], axis=1)
                c2 = jnp.concatenate([rows((2 + r) * nb + i) for i in range(nb)], axis=1)
                c1_ref[r] = c1
                c2_ref[r] = c2
                pooled = pooled + vec[r, 0:1] * c2 + vec[r, 1:2] * c1
            pooled = pooled * (1.0 / area)
            pool_ref[...] = pooled
            norm, actf, _ = squeeze_norm(exact(pooled, wsq_of(wsq)), sfc, s, sgb)
            norm_ref[...] = norm
            hid_ref[...] = jnp.maximum(actf, 0.0)

        c1_all, c2_all, pool_all, normf_all, hid_all = call(
            all_body,
            image_counts,
            [c12_g.reshape(ND, BLOCK, 128), vec, pw_all, sfc, sgb],
            [
                ((2, ni, mid), F32),
                ((2, ni, mid), F32),
                ((ni, mid), F32),
                ((ni, inner), F32),
                ((ni, inner), F32),
            ],
            far={0: slice(0, used), 2: WSQ},
        )
        for k, g in enumerate(sum_groups):
            got = [swap(merged, both, m) for m in g]
            z = merged + got[0]
            merged = z + (got[1] + got[2]) if len(g) == 3 else z
            if k == 1:
                merged, c1_all = lax.optimization_barrier((merged, c1_all))

        def all_valid(s):
            row = lax.broadcasted_iota(jnp.int32, (ni, inner), 0)
            dev = row & (ND - 1)
            at, chan = dev >> (nc.bit_length() - 1), dev & (nc - 1)
            slot = (row >> (ND.bit_length() - 1)) + own * sum(
                ((chan >> i) & 1) * (nc >> (i + 1)) for i in range(len(cbits))
            )
            live = jnp.zeros((ni, inner), jnp.int32)
            for i in range(nd):
                live = jnp.where(at == i, s[i], live)
            return jnp.where(slot < live, 1.0, 0.0)

        def back_body(
            s, merged, c1a, c2a, normf, sfc, sgb, wsq, ga, spl, sums2, vec, wts, l0, l1, l2, l3,
            gs_ref, b0, b1, b2, b3, gq_ref, sg2, gfc, wab, blk, arrive,
        ):
            dzf = merged[0:ni]
            norm_all = normf[...]
            s_f = colsum(dzf)
            g_f = colsum(dzf * norm_all)
            gfc[0:1] = g_f
            gfc[1:2] = s_f
            for r in range(2):
                for i in range(nb):
                    k = ni + (4 + r) * nb + i
                    wab[r : r + 1, i * 128 : (i + 1) * 128] = merged[k : k + 1]
            nf, n = recip(s, 1), recip(s, area)
            _, _, inv = squeeze_norm(0.0, sfc, s, sgb)
            gq = sgb[0:1] * inv * (dzf - all_valid(s) * (s_f + norm_all * g_f) * nf)
            gq_ref[...] = gq
            arrive(6)
            gp = exact(gq, wsq_of(wsq), ((1,), (1,))) * (1.0 / area)
            mask = mask_of(valid(s, 0), R, mid, edge)
            imgs = lax.broadcasted_iota(jnp.int32, (R, mid), 0)
            grow = lax.broadcasted_iota(jnp.int32, (ni, mid), 0)
            c, _ = me()
            mine = lax.axis_index("dp") * nc + c
            gpo = [colsum(jnp.where(grow == mine + b * ND, gp, 0.0)) for b in range(own)]
            gprow = gpo[0]
            for b in range(1, own):
                gprow = jnp.where(imgs >= b * span, gpo[b], gprow)
            lane = lax.broadcasted_iota(jnp.int32, (R, 2 * lw), 1)
            gss = []
            acts = []
            for r in range(2):
                def piece(j):
                    k = (r * 2 + j) * nb
                    return jnp.concatenate([merged[ni + k + i : ni + k + i + 1] for i in range(nb)], axis=1)

                s2v = piece(0) + colsum(gp * c1a[r])
                g2v = piece(1) + colsum(gp * c2a[r])
                sg2[0, r : r + 1] = s2v
                sg2[1, r : r + 1] = g2v
                norm, act, on, inv2 = second(spl, sums2, n, vec, r, mask)
                w = wts[r]
                wrow = w[0:1]
                for b in range(1, own):
                    wrow = jnp.where(imgs >= b * span, w[b : b + 1], wrow)
                if r == 0:
                    arrive(7)
                dz = jnp.where(on, wrow * ga[...] + gprow, 0.0)
                gs = vec[r, 0:1] * inv2 * (dz - (s2v + norm * g2v) * n)
                gs = jnp.where(mask, gs, 0.0)
                gss.append(gs)
            for pair in range(nc // 2):
                cols = slice(pair * 2 * lw, (pair + 1) * 2 * lw)
                a, b = gss[0][:, cols], gss[1][:, cols]
                blk[2 * pair] = jnp.where(lane < lw, a, pltpu.roll(b, lw, 1))
                blk[2 * pair + 1] = jnp.where(lane < lw, pltpu.roll(a, lw, 1), b)
            for k, (o, z) in enumerate(((b0, l0), (b1, l1), (b2, l2), (b3, l3))):
                o[0:R] = blk[c ^ k]
                o[R : R + 8] = z[...]
            for r in range(2):
                gs_ref[:, r * mid : (r + 1) * mid] = gss[r]

        def conv_back_body(s, gs, red, sums1, vec, w1, dz1, sg1, zh, arrive):
            mask = mask_of(valid(s, 0), R, mid, edge)
            avg1, inv1, _ = stats(sums1, s)
            norm1 = (red[...] - avg1) * inv1
            on1 = (norm1 * vec[0, 3:4] + vec[1, 3:4] > 0) & mask
            for r in range(2):
                taps_in(gs[:, r * mid : (r + 1) * mid], (zh,), own)
                if r == 0:
                    arrive(4)
                acc = 0.0
                for t, (u, v) in enumerate(TAPS):
                    z = zh[2 - v, :, 2 - u : 2 - u + edge].reshape(R, mid)
                    acc += mm(z, w1[r, :, t * half : (t + 1) * half])
                cols = slice(r * half, (r + 1) * half)
                acc = jnp.where(on1[:, cols], acc, 0.0)
                dz1[:, cols] = acc
                sg1[0:1, cols] = colsum(acc)
                sg1[1:2, cols] = colsum(acc * norm1[:, cols])

        gs, blk0, blk1, blk2, blk3, gq, sg2, gfc, wab = call(
            back_body,
            image_counts,
            [merged, c1_all, c2_all, normf_all, sfc, sgb, pw_all, ga, spl, s2, vec, wts, l0, l1, l2, l3],
            [((R, 2 * mid), F32)]
            + [((R + 8, 2 * lw), F32)] * 4
            + [((ni, inner), F32), ((2, 2, mid), F32), ((2, inner), F32), ((2, mid), F32)],
            [pltpu.VMEM((nc, R, 2 * lw), F32)],
            far={6: WSQ, 7: None},
            lazy=True,
        )
        dz1, sg1 = call(
            conv_back_body,
            image_counts,
            [gs, red, s1, vec, w1],
            [((R, mid), F32), ((2, mid), F32)],
            [pltpu.VMEM((3, own, PAD, PAD, mid), BF16)],
            flops=4 * R * nw * mid,
            far=(4,),
            lazy=True,
        )
        blks = [blk0, swap(blk1, "chan", 1), swap(blk2, "chan", 2), swap(blk3, "chan", 3)]

        def prep_body(s, red_g, sums, vec, relu, norm):
            avg, inv, _ = stats(sums, s)
            for k in range(nc):
                mask = mask_of(valid(s, CHAN_REL[k]), R, mid, edge)
                v = (red_g[me()[0] ^ k] - avg) * inv
                rows = slice(k * R, (k + 1) * R)
                norm[rows, :] = v.astype(BF16)
                z = jnp.maximum(v * vec[0, 3:4] + vec[1, 3:4], 0.0)
                relu[rows, :] = jnp.where(mask, z, 0.0).astype(BF16)

        relu_all, norm_all = call(
            prep_body, image_counts, [after(red_g, gs), s1, vec], [((nc * R, mid), BF16)] * 2, far=(0,)
        )

        def store_body(s, b0, b1, b2, b3, out_bo, scr):
            for r, b in enumerate((b0, b1, b2, b3)):
                store_quarter(out_bo, scr, r, b[...])

        (block_out,) = call(
            store_body,
            image_counts,
            [after(bos[0], gs)] + bos[1:],
            [(feats.shape, F32)],
            [quarter_scratch],
            far=(0, 1, 2, 3),
            far_out=(0,),
        )

        dz1_y = swap(after(dz1, relu_all, block_out), "chan", 2)

        n_w = 9 * 2 * lw
        n_dws = padded_rows(n_w + lb * mid + 2 * lw)

        def dws_body(s, k0, k1, k2, k3, relu, hid, t1, t2, u1, sums3, sg, eg, *refs):
            outs, (sg_out, zg, out) = refs[:-3], refs[-3:]
            acc = 0.0
            base = lax.axis_index("dp") * nc
            for k, a in enumerate((k0, k1, k2, k3)):
                row = lax.broadcasted_iota(jnp.int32, (8, inner), 0)
                h = jnp.zeros((8, inner), F32)
                for b in range(own):
                    h = jnp.where(row == b, hid[pl.ds(base + (me()[0] ^ k) + b * ND, 1), :], h)
                acc += exact(a[R : R + 8, :], h, ((0,), (0,)))
            out[n_w + lb * mid : n_w + lb * mid + 2 * lw] = acc
            _, inv, n = stats(mine_of(sums3), s)
            sg = mine_of(sg)
            sg_out[...] = sg
            outer = exact(u1[...], sg[0:1], ((0,), (0,)))
            z = (eg[0:1] * inv) * (t1[...] - (outer + t2[...] * sg[1:2]) * n)
            for i in range(lb):
                out[n_w + i * mid : n_w + (i + 1) * mid] = z[:, i * 128 : (i + 1) * 128]
            for k, bk in enumerate((k0, k1, k2, k3)):
                taps_in(bk[0:R, :], (zg.at[:, k * own : (k + 1) * own],), own)
            taps = [zg[2 - v, :, 2 - u : 2 - u + edge].reshape(nc * R, 2 * lw) for u, v in TAPS]
            y = mm(relu[...], jnp.concatenate(taps, axis=1), ((0,), (0,)))
            lane = lax.broadcasted_iota(jnp.int32, (half, 2 * lw), 1)
            for t in range(9):
                cols = slice(t * 2 * lw, (t + 1) * 2 * lw)
                out[t * 2 * lw : (t + 1) * 2 * lw, :] = jnp.where(lane < lw, y[:half, cols], y[half:, cols]).T
            cut_chunks(out, groups[0], outs)

        *dws, sg3l = call(
            dws_body,
            image_counts,
            blks + [relu_all, after(hid_all, block_out), t1, t2, u1, s3, sg3, eg],
            chunk_outs(n_dws, groups[0]) + [((2, win), F32)],
            [pltpu.VMEM((3, slots, PAD, PAD, 2 * lw), BF16), pltpu.VMEM((n_dws, 128), F32)],
            flops=2 * nc * R * mid * 9 * 2 * lw,
            far=(0, 6, 7),
        )
        sg1_steps = sum_steps(after(sg1, dws[1]))
        sg1 = sg1_steps[-1]
        dz1_r = [dz1, dz1_y, swap(dz1, "chan", 1), swap(dz1_y, "chan", 1)]

        mb = mid // 128
        n_dwr = padded_rows(mb * win)

        def dwr_body(s, d0, d1, d2, d3, norms, x0, x1, x2, x3, sums, sg, vec, *refs):
            outs, (go0, go1, go2, go3, sent) = refs[:-5], refs[-5:]
            _, inv, n = stats(sums, s)
            acc = 0.0
            for r, (dz, go, x) in enumerate(((d0, go0, x0), (d1, go1, x1), (d2, go2, x2), (d3, go3, x3))):
                mask = mask_of(valid(s, r), R, win, edge)
                k = CHAN_REL[r]
                norm = norms[k * R : (k + 1) * R, :].astype(F32)
                g = vec[0, 3:4] * inv * (dz[...] - (sg[0:1] + norm * sg[1:2]) * n)
                g = jnp.where(mask, g, 0.0).astype(BF16)
                go[...] = g
                acc += mm(x[...], g, ((0,), (0,)))
            for i in range(mb):
                sent[i * win : (i + 1) * win] = acc[:, i * 128 : (i + 1) * 128]
            cut_chunks(sent, groups[0], outs)

        *sent, gr0, gr1, gr2, gr3 = call(
            dwr_body,
            image_counts,
            dz1_r + [norm_all, x0, x1, x2, x3, s1, sg1, vec],
            chunk_outs(n_dwr, groups[0]) + [((R, mid), BF16)] * 4,
            [pltpu.VMEM((n_dwr, 128), F32)],
            flops=8 * R * win * mid,
            far=(5, 6, 7, 8),
        )
        def gin_body(s, g0, g1, g2, g3, m0, m1, m2, m3, w_ref, out_gi, scr):
            w = w_ref[...].astype(BF16)
            for r, (g, m) in enumerate(((g0, m0), (g1, m1), (g2, m2), (g3, m3))):
                store_quarter(out_gi, scr, r, mm(g[...], w, ((1,), (1,))) + m[...])

        (grad_input,) = call(
            gin_body,
            image_counts,
            [gr0, gr1, gr2, gr3] + masked + [reduce_weight],
            [(feats.shape, F32)],
            [quarter_scratch],
            flops=8 * R * win * mid,
            far=(4, 5, 6, 7, 8),
            far_out=(0,),
        )

        def write_dwr(whole, out):
            for i in range(mb):
                out[:, i * 128 : (i + 1) * 128] = whole[i * win : (i + 1) * win, :]

        (grad_reduce_weight,) = sum_dp(image_counts, sent, write_dwr, [((win, mid), F32)])
        def write_dws(whole, o_ws, o_we, o_at):
            o_ws[...] = whole[:n_w, :]
            for i in range(lb):
                o_we[:, i * 128 : (i + 1) * 128] = whole[n_w + i * mid : n_w + (i + 1) * mid, :]
            o_at[...] = whole[n_w + lb * mid : n_w + lb * mid + 2 * lw, :]

        dws, grad_expand_weight, watt = sum_dp(
            image_counts,
            dws,
            write_dws,
            [((n_w, 128), F32), ((mid, win), F32), ((2 * lw, 128), F32)],
            [(), (grad_input,)],
        )
        grad_split_weight = dws.reshape(3, 3, 2, lw, half).transpose(0, 1, 4, 2, 3)
        block_out, grad_input = from_native(block_out), from_native(grad_input)

        def sq_body(s, pool, gq, out):
            out[...] = exact(pool[...], gq[...], ((0,), (0,)))

        (wsw,) = call(sq_body, image_counts, [pool_all, gq], [((mid, inner), F32)])

        def own_lanes(z, axis):
            return lax.dynamic_slice_in_dim(z, c * lw, lw, axis)

        return (
            block_out,
            grad_input,
            grad_reduce_weight,
            own_lanes(sg1[1], 0),
            own_lanes(sg1[0], 0),
            grad_split_weight,
            own_lanes(sg2[1], 1),
            own_lanes(sg2[0], 1),
            own_lanes(wsw, 0),
            gfc[0],
            gfc[1],
            watt.reshape(2, lw, inner).transpose(2, 0, 1),
            own_lanes(wab, 1),
            grad_expand_weight,
            sg3l[1],
            sg3l[0],
        )

    return per_device


def solution(mesh):
    in_specs = (
        P("dp", None, None, "chan"),
        P(),
        P("chan", None),
        P("chan"),
        P("chan"),
        P(None, None, None, None, "chan"),
        P(None, "chan"),
        P(None, "chan"),
        P("chan", None),
        P(),
        P(),
        P(None, None, "chan"),
        P(None, "chan"),
        P(None, "chan"),
        P("chan"),
        P("chan"),
        P("dp", None, None, "chan"),
    )
    out_specs = (
        P("dp", None, None, "chan"),
        P("dp", None, None, "chan"),
        P("chan", None),
        P("chan"),
        P("chan"),
        P(None, None, None, None, "chan"),
        P(None, "chan"),
        P(None, "chan"),
        P("chan", None),
        P(),
        P(),
        P(None, None, "chan"),
        P(None, "chan"),
        P(None, "chan"),
        P("chan"),
        P("chan"),
    )
    return jax.shard_map(
        build(mesh), mesh=mesh, in_specs=in_specs, out_specs=out_specs, check_vma=False
    )
```
